256 devices in a mesh: gx: 32 (over x, z), gy: 8 (over y, core).
Axes of the slice: x: 4, y: 4, z: 8, core: 2. Of those that a mesh axis runs over, the one named last changes fastest.
Arguments:
- pressure_source: float32 [1024, 256, 256], P('gx', 'gy'), may hold values from -6 to 6
- phase: int32 [1024, 256, 256], P('gx', 'gy'), may hold values 0 or 1
Outputs:
- scaled_pressure: float32 [1024, 256, 256], P('gx', 'gy')
- residual: float32 [1024, 256, 256], P('gx', 'gy')
The draws below stay inside these ranges and needn't reach their ends.
All inputs are finite; a program needn't handle non-finite values. No bound on the sum of `phase` on one device may be relied on, other than what follows from the above.
Results may differ from the reference program's by a relative error of at most 0.0003.
Values sent between devices are 32-bit elements; how exact they have to be, the bound alone decides.
No kernel may reach another device: no remote copies, remote signals or barrier semaphores. Data moves between devices by JAX's collectives and lax.ppermute only.
A program may use at most 192 MiB of HBM per device.

```python
import jax
import jax.numpy as jnp
from jax import lax

CZ = 256
LEVELS = 4
SWEEPS = 2
NX = 1024
NY = 256


def set_ends(drawn, key, smallest, top_value):
    dims = drawn.shape
    place = [jax.random.randint(jax.random.fold_in(key, axis), (), 0, dims[axis]) for axis in range(len(dims))]
    drawn = drawn.at[tuple(place)].set(smallest)
    longest = dims.index(max(dims))
    place[longest] = (place[longest] + 1) % dims[longest]
    return drawn.at[tuple(place)].set(top_value)


def shard_levels(key, shape, split, smallest, top_value):
    factor_of, own = 1.0, jax.random.fold_in(key, 6)
    for dim, blocks in split:
        heights = jnp.exp(jax.random.uniform(jax.random.fold_in(own, dim), (blocks,), jnp.float32, smallest / len(split), top_value / len(split)))
        factor_of = factor_of * jnp.repeat(heights, shape[dim] // blocks).reshape([-1 if axis == dim else 1 for axis in range(len(shape))])
    return factor_of


def scatter_about(stream_key, shape, scale, most, shards=(), kind=jnp.bfloat16):
    entries = scale * jax.random.normal(stream_key, shape, jnp.float32)
    if shards:
        entries = entries * shard_levels(stream_key, shape, shards, -0.22, 0.18)
    return jnp.clip(entries, -most, most).astype(kind)


def setup_inputs(seed: int = 0) -> dict:
    key_list = jax.random.split(jax.random.key(seed), 3)
    return {
        "pressure_source": scatter_about(key_list[0], (NX, NY, CZ), 1.0, 6.0, ((0, 32), (1, 8)), jnp.float32),
        "phase": set_ends((jax.random.randint(key_list[1], (NX, NY, CZ), 0, 2) < 1).astype(jnp.int32), jax.random.fold_in(key_list[1], 1), 0, 1),
    }


OMEGA = 0.8
WATER_MOBILITY = 0.001


def neighbours(padded):
    return [padded[2:, 1:-1, 1:-1], padded[:-2, 1:-1, 1:-1], padded[1:-1, 2:, 1:-1],
            padded[1:-1, :-2, 1:-1], padded[1:-1, 1:-1, 2:], padded[1:-1, 1:-1, :-2]]


def centre_of(padded):
    return padded[1:-1, 1:-1, 1:-1]


def harmonic(centre, beside):
    other = jnp.where(beside > 0.0, beside, centre)
    summed = centre + other
    return 2.0 * centre * other / jnp.where(summed > 0.0, summed, 1.0)


def face_weights(padded_mobility):
    centre = centre_of(padded_mobility)
    return [harmonic(centre, beside) for beside in neighbours(padded_mobility)]


def diagonal_of(weights, level_scale):
    summed = weights[0]
    for weight in weights[1:]:
        summed = summed + weight
    return level_scale * summed


def apply_operator(padded_field, weights, level_scale):
    centre = centre_of(padded_field)
    besides = neighbours(padded_field)
    summed = weights[0] * (centre - besides[0])
    for weight, beside in zip(weights[1:], besides[1:]):
        summed = summed + weight * (centre - beside)
    return level_scale * summed


def relax_step(field, padded_field, source, weights, diagonal, level_scale):
    return field + OMEGA * (source - apply_operator(padded_field, weights, level_scale)) / diagonal


def restrict_along(padded, along):
    count = padded.shape[along] - 2
    first = lax.slice_in_dim(padded, 0, count, 2, along)
    second = lax.slice_in_dim(padded, 1, count + 1, 2, along)
    third = lax.slice_in_dim(padded, 2, count + 2, 2, along)
    fourth = lax.slice_in_dim(padded, 3, count + 2, 2, along)
    return (first + 3.0 * second + 3.0 * third + fourth) * 0.125


def restrict(padded):
    for along in range(3):
        padded = restrict_along(padded, along)
    return padded


def coarsen(mobility):
    sx, sy, sz = mobility.shape
    return mobility.reshape(sx // 2, 2, sy // 2, 2, sz // 2, 2).mean(axis=(1, 3, 5))


def prolong(field):
    return jnp.repeat(jnp.repeat(jnp.repeat(field, 2, 0), 2, 1), 2, 2)


def reference(pressure_source, phase):
    mobility = jnp.where(phase == 1, WATER_MOBILITY, 1.0).astype(jnp.float32)
    source = pressure_source
    stored = []
    for depth in range(LEVELS - 1):
        level_scale = 0.25 ** depth
        weights = face_weights(jnp.pad(mobility, 1))
        diagonal = diagonal_of(weights, level_scale)
        field = OMEGA * source / diagonal
        for _ in range(SWEEPS - 1):
            field = relax_step(field, jnp.pad(field, 1), source, weights, diagonal, level_scale)
        remainder = source - apply_operator(jnp.pad(field, 1), weights, level_scale)
        stored.append((field, source, mobility, level_scale))
        source = restrict(jnp.pad(remainder, 1))
        mobility = coarsen(mobility)
    level_scale = 0.25 ** (LEVELS - 1)
    weights = face_weights(jnp.pad(mobility, 1))
    diagonal = diagonal_of(weights, level_scale)
    field = OMEGA * source / diagonal
    for _ in range(SWEEPS - 1):
        field = relax_step(field, jnp.pad(field, 1), source, weights, diagonal, level_scale)
    for depth in reversed(range(LEVELS - 1)):
        fine_field, source, mobility, level_scale = stored[depth]
        weights = face_weights(jnp.pad(mobility, 1))
        diagonal = diagonal_of(weights, level_scale)
        field = fine_field + prolong(field)
        for _ in range(SWEEPS):
            field = relax_step(field, jnp.pad(field, 1), source, weights, diagonal, level_scale)
    residual = source - apply_operator(jnp.pad(field, 1), weights, level_scale)
    return diagonal * field, residual
```

```python
import jax
import jax.numpy as jnp
from jax import lax
from jax.experimental import pallas as pl
from jax.experimental.pallas import tpu as pltpu
from jax.sharding import PartitionSpec as P

OMEGA = 0.8
KEEP = 0.2
WATER = 0.001
MIXED = 2.0 * WATER / (1.0 + WATER)
OUT = 0.25
F32 = jnp.float32
MIB = 1024 * 1024


def up_y(a):
    return pltpu.roll(a, a.shape[0] - 1, 0)


def dn_y(a):
    return pltpu.roll(a, 1, 0)


def up_z(a):
    return pltpu.roll(a, a.shape[1] - 1, 1)


def dn_z(a):
    return pltpu.roll(a, 1, 1)


def iota(shape, dim):
    return lax.broadcasted_iota(jnp.int32, shape, dim)


def ring(row, cut, rows):
    return jnp.where(row < cut, row, row - rows)


def restrict_weight(offset):
    near = (offset == 0) | (offset == 1)
    far = (offset == -1) | (offset == 2)
    return jnp.where(near, 0.375, jnp.where(far, 0.125, 0.0)).astype(F32)


def pair_weight(offset):
    return jnp.where((offset == 0) | (offset == 1), 1.0, 0.0).astype(F32)


def dot(a, b):
    return jnp.dot(a, b, precision=lax.Precision.HIGHEST, preferred_element_type=F32)


def face_code(a, b):
    s = a + b
    return jnp.where(s < 0.75, 1.0, jnp.where(s < 1.1, MIXED, WATER)).astype(F32)


def face_mean(a, b):
    product = a * b
    return jnp.where(product > 0.0, 2.0 * product / (a + b), jnp.maximum(a, b))


def weights_at(m, m_next, wx_prev, face, outside, full):
    lane = iota(m.shape, 1)
    last = m.shape[1] - 1
    wx = face(m, m_next)
    wy = face(m, up_y(m))
    m_up = up_z(m)
    if full:
        m_up = jnp.where(lane == last, outside, m_up)
    wz = face(m, m_up)
    wz_low = dn_z(wz)
    if full:
        wz_low = jnp.where(lane == 0, face(m, jnp.full_like(m, outside)), wz_low)
    d = (wx + wx_prev) + (wy + dn_y(wy)) + (wz + wz_low)
    q = jnp.where(m != outside, OMEGA / d, 0.0)
    if full:
        wz = jnp.where(lane == last, 0.0, wz)
    return wx, wy, wz, d, q


def weights_pass(lo, hi, m_ref, w, face, outside, full, first):
    wx_ref, wy_ref, wz_ref, d_ref, q_ref = w
    start = face(m_ref[lo - 1], m_ref[lo])
    wx_ref[lo - 1] = start

    def body(j, wx_prev):
        wx, wy, wz, d, q = weights_at(m_ref[j], m_ref[j + 1], wx_prev, face, outside, full)
        wx_ref[j] = wx
        wy_ref[j] = wy
        wz_ref[j] = wz
        d_ref[j] = d
        q_ref[j] = q
        first(j, q)
        return wx

    lax.fori_loop(lo, hi, body, start)


def flow(j, p, p_ref, w):
    wx_ref, wy_ref, wz_ref = w[:3]
    wy, wz = wy_ref[j], wz_ref[j]
    along_x = wx_ref[j] * p_ref[j + 1] + wx_ref[j - 1] * p_ref[j - 1]
    along_y = wy * up_y(p) + dn_y(wy * p)
    along_z = wz * up_z(p) + dn_z(wz * p)
    return along_x + along_y + along_z


def sweep(lo, hi, p_ref, out_ref, s_ref, w):
    def body(j, carry):
        p = p_ref[j]
        out_ref[j] = KEEP * p + w[4][j] * (s_ref[j] + flow(j, p, p_ref, w))
        return carry

    lax.fori_loop(lo, hi, body, 0)


def remainder(lo, hi, p_ref, out_ref, s_ref, w):
    def body(j, carry):
        p = p_ref[j]
        r = s_ref[j] + flow(j, p, p_ref, w) - w[3][j] * p
        out_ref[j] = jnp.where(w[4][j] > 0.0, r, 0.0)
        return carry

    lax.fori_loop(lo, hi, body, 0)


def restrict_x(r_ref, j):
    return (r_ref[j] + r_ref[j + 3]) * 0.125 + (r_ref[j + 1] + r_ref[j + 2]) * 0.375


def edge(axis):
    i = lax.axis_index(axis)
    return i == 0, i == lax.axis_size(axis) - 1


def blank(flag, value, other):
    return jnp.where(flag, other, value)


X0 = 5
N0 = 32 + 2 * X0


def pack0_kernel(s_lo, s_hi, f_lo, f_hi, xl_lo, xl_hi, xh_lo, xh_hi, dn_ref, upw_ref, s_ref, c_ref):
    low_x, high_x = edge("gx")
    sub = iota((8, 256), 0)
    for own_s, own_f, xl, xh, out_ref, row in (
        (s_lo, f_lo, xl_lo, xh_lo, dn_ref, 3),
        (s_hi, f_hi, xl_hi, xh_hi, upw_ref, 4),
    ):
        s_ref[0] = jnp.zeros((8, 256), F32)
        s_ref[N0 - 1] = jnp.zeros((8, 256), F32)
        s_ref[1:X0] = blank(low_x, xl[:4], 0.0)
        c_ref[0:X0] = blank(low_x, xl[4:], OUT)
        s_ref[X0 + 32 : N0 - 1] = blank(high_x, xh[:4], 0.0)
        c_ref[X0 + 32 : N0] = blank(high_x, xh[4:], OUT)
        s_ref[X0 : X0 + 32] = own_s[...]
        c_ref[X0 : X0 + 32] = own_f[...].astype(F32)
        is_source = sub < 4 if row == 3 else sub >= 4

        def message(j, s, out_ref=out_ref, is_source=is_source):
            out_ref[j] = jnp.where(is_source, s, pltpu.roll(c_ref[j], 4, 0))

        message(0, s_ref[0])
        message(N0 - 1, s_ref[N0 - 1])

        def body(j, wx_prev, row=row, message=message):
            c = c_ref[j]
            wx, _, _, _, q = weights_at(c, c_ref[j + 1], wx_prev, face_code, OUT, True)
            s = s_ref[j]
            message(j, jnp.where(sub == row, q * s, s))
            return wx

        lax.fori_loop(1, N0 - 1, body, face_code(c_ref[0], c_ref[1]))


def pack0(source, phase, xlo, xhi):
    own = lambda k: pl.BlockSpec((32, 8, 256), lambda i, k=k: (0, k, 0))
    halo = lambda k: pl.BlockSpec((9, 8, 256), lambda i, k=k: (0, k, 0))
    whole = pl.BlockSpec((N0, 8, 256), lambda i: (0, 0, 0))
    shape = jax.ShapeDtypeStruct((N0, 8, 256), F32)
    return pl.pallas_call(
        pack0_kernel,
        grid=(1,),
        in_specs=[own(0), own(3), own(0), own(3), halo(0), halo(3), halo(0), halo(3)],
        out_specs=[whole, whole],
        out_shape=[shape, shape],
        scratch_shapes=[pltpu.VMEM((N0, 8, 256), F32)] * 2,
        compiler_params=pltpu.CompilerParams(vmem_limit_bytes=16 * MIB),
        name="pack0",
    )(source, source, phase, phase, xlo, xlo, xhi, xhi)


N1 = 28
N2 = 28
N3 = 12


def copies(pairs, sems):
    return [pltpu.make_async_copy(a, b, sems.at[k]) for k, (a, b) in enumerate(pairs)]


def down0_kernel(
    s_in, f_in, xlo, xhi, ylo, yhi,
    src1, mob1, dn1, upw1, wx_o, wy_o, wz_o, d_o, q_o, s_o, p_o,
    s_ref, c_ref, wx, wy, wz, d_ref, q_ref, p1, p2, r_ref, t_ref, sems,
):
    low_x, high_x = edge("gx")
    low_y, high_y = edge("gy")
    own = slice(X0, X0 + 32)
    s_ref[0, :32] = jnp.zeros((32, 256), F32)
    s_ref[N0 - 1, :32] = jnp.zeros((32, 256), F32)
    s_ref[1:X0, :32] = blank(low_x, xlo[:4], 0.0)
    c_ref[0:X0, :32] = blank(low_x, xlo[4:], OUT)
    s_ref[X0 + 32 : N0 - 1, :32] = blank(high_x, xhi[:4], 0.0)
    c_ref[X0 + 32 : N0, :32] = blank(high_x, xhi[4:], OUT)
    sub = iota((8, 256), 0)
    above = sub < 4
    outer = (above & high_y) | (~above & low_y)

    def tile4(j, carry):
        hi, lo = yhi[j], ylo[j]
        s_ref[j, 32:] = jnp.where(outer, 0.0, jnp.where(above, hi, lo))
        c_ref[j, 32:] = jnp.where(outer, OUT, pltpu.roll(jnp.where(above, lo, hi), 4, 0))
        return carry

    lax.fori_loop(0, N0, tile4, 0)

    def own_planes(j, carry):
        s_ref[j + X0, :32] = s_in[j]
        c_ref[j + X0, :32] = f_in[j].astype(F32)
        return carry

    lax.fori_loop(0, 32, own_planes, 0)

    w = (wx, wy, wz, d_ref, q_ref)
    row = iota((40, 256), 0)
    seam = (row == 35) | (row == 36)

    def first(j, q):
        s = s_ref[j]
        p1[j] = jnp.where(seam, s, q * s)

    weights_pass(1, N0 - 1, c_ref, w, face_code, OUT, True, first)
    state = copies(
        [(wx, wx_o), (wy, wy_o), (wz, wz_o), (d_ref, d_o), (q_ref, q_o), (s_ref, s_o), (p2, p_o)], sems
    )
    for copy in state[:-1]:
        copy.start()
    sweep(2, N0 - 2, p1, p2, s_ref, w)
    state[-1].start()
    remainder(4, N0 - 4, p2, r_ref, s_ref, w)

    fine_z, coarse_z = iota((256, 128), 0), iota((256, 128), 1)
    fine_y = ring(iota((16, 40), 1), 36, 40)
    coarse_y = iota((16, 40), 0)
    rz = restrict_weight(fine_z - 2 * coarse_z)
    mz = pair_weight(fine_z - 2 * coarse_z)
    ry = restrict_weight(fine_y - 2 * coarse_y)
    my = pair_weight(fine_y - 2 * coarse_y)

    def halve(k, carry):
        t_ref[pl.ds(pl.multiple_of(k * 40, 8), 40)] = restrict_x(r_ref, 2 * k + 4)
        return carry

    lax.fori_loop(0, 16, halve, 0)
    coarse = dot(t_ref[...], rz)
    for k in range(16):
        src1[k] = dot(ry, coarse[k * 40 : k * 40 + 40])

    def count(k, carry):
        t_ref[pl.ds(pl.multiple_of(k * 40, 8), 40)] = c_ref[2 * k + X0] + c_ref[2 * k + X0 + 1]
        return carry

    lax.fori_loop(0, 16, count, 0)
    water = dot(t_ref[...], mz)
    for k in range(16):
        n = dot(my, water[k * 40 : k * 40 + 40])
        mob1[k] = 0.25 * ((8.0 - n) * 0.125 + n * (0.125 * WATER))
    dn1[:5] = src1[:5]
    dn1[5:] = mob1[:6]
    upw1[:5] = src1[11:]
    upw1[5:] = mob1[10:]
    for copy in state:
        copy.wait()


def down0(source, phase, xlo, xhi, ylo, yhi):
    big = jax.ShapeDtypeStruct((N0, 40, 256), F32)
    own1 = jax.ShapeDtypeStruct((16, 16, 128), F32)
    msg1 = jax.ShapeDtypeStruct((11, 16, 128), F32)
    vmem = pl.BlockSpec(memory_space=pltpu.VMEM)
    anyw = pl.BlockSpec(memory_space=pl.ANY)
    return pl.pallas_call(
        down0_kernel,
        in_specs=[vmem] * 6,
        out_specs=[vmem] * 4 + [anyw] * 7,
        out_shape=[own1, own1, msg1, msg1] + [big] * 7,
        scratch_shapes=[pltpu.VMEM((N0, 40, 256), F32)] * 10
        + [pltpu.VMEM((640, 256), F32), pltpu.SemaphoreType.DMA((7,))],
        compiler_params=pltpu.CompilerParams(vmem_limit_bytes=40 * MIB),
        name="down0",
    )(source, phase, xlo, xhi, ylo, yhi)


def pack1_kernel(src, mob, xlo, xhi, dn_ref, upw_ref):
    low_x, high_x = edge("gx")
    for rows, out in ((slice(0, 8), dn_ref), (slice(8, 16), upw_ref)):
        out[0, :8] = jnp.zeros((8, 128), F32)
        out[N1 - 1, :8] = jnp.zeros((8, 128), F32)
        out[1:6, :8] = blank(low_x, xlo[:5, rows], 0.0)
        out[0:6, 8:] = blank(low_x, xlo[5:, rows], 0.0)
        out[6:22, :8] = src[:, rows]
        out[6:22, 8:] = mob[:, rows]
        out[22:27, :8] = blank(high_x, xhi[:5, rows], 0.0)
        out[22:28, 8:] = blank(high_x, xhi[5:, rows], 0.0)


def pack1(src, mob, xlo, xhi):
    shape = jax.ShapeDtypeStruct((N1, 16, 128), F32)
    vmem = pl.BlockSpec(memory_space=pltpu.VMEM)
    return pl.pallas_call(
        pack1_kernel,
        in_specs=[vmem] * 4,
        out_specs=[vmem] * 2,
        out_shape=[shape, shape],
        name="pack1",
    )(src, mob, xlo, xhi)


def down1_kernel(
    src, mob, xlo, xhi, ylo, yhi,
    own2, dn2, upw2, s_ref, wx, wy, wz, q_ref, p2,
    m_ref, d_ref, p1, r_ref, t_ref, pk_ref,
):
    low_x, high_x = edge("gx")
    low_y, high_y = edge("gy")
    zero = jnp.zeros((32, 128), F32)
    s_ref[0] = zero
    s_ref[N1 - 1] = zero
    s_ref[1:6, :16] = blank(low_x, xlo[:5], 0.0)
    m_ref[0:6, :16] = blank(low_x, xlo[5:], 0.0)
    s_ref[6:22, :16] = src[...]
    m_ref[6:22, :16] = mob[...]
    s_ref[22:27, :16] = blank(high_x, xhi[:5], 0.0)
    m_ref[22:28, :16] = blank(high_x, xhi[5:], 0.0)
    s_ref[:, 16:24] = blank(high_y, yhi[:, :8], 0.0)
    m_ref[:, 16:24] = blank(high_y, yhi[:, 8:], 0.0)
    s_ref[:, 24:] = blank(low_y, ylo[:, :8], 0.0)
    m_ref[:, 24:] = blank(low_y, ylo[:, 8:], 0.0)
    w = (wx, wy, wz, d_ref, q_ref)

    def first(j, q):
        p1[j] = q * s_ref[j]

    weights_pass(1, N1 - 1, m_ref, w, face_mean, 0.0, True, first)
    sweep(2, N1 - 2, p1, p2, s_ref, w)
    remainder(3, N1 - 3, p2, r_ref, s_ref, w)

    lane_in, lane_out = iota((128, 128), 0), iota((128, 128), 1)
    rz = jnp.where(lane_out < 64, restrict_weight(lane_in - 2 * lane_out), 0.0)
    mz = pair_weight(lane_in - 2 * (lane_out - 64))
    row_out = iota((16, 32), 0)
    coarse_y = ring(row_out, 12, 16)
    held = (coarse_y >= -2) & (coarse_y <= 9)
    fine_y = ring(iota((16, 32), 1), 24, 32)
    ry = jnp.where(held, restrict_weight(fine_y - 2 * coarse_y), 0.0)
    my = jnp.where(held, pair_weight(fine_y - 2 * coarse_y), 0.0)
    zero16 = jnp.zeros((16, 128), F32)
    for k in range(10):
        t_ref[k * 32 : k * 32 + 32] = restrict_x(r_ref, 2 * k + 3)
    coarse = dot(t_ref[:320], rz)
    for k in range(12):
        t_ref[k * 32 : k * 32 + 32] = (m_ref[2 * k + 2] + m_ref[2 * k + 3]) * (0.25 * 0.125)
    mean = dot(t_ref[...], mz)
    for k in range(12):
        value = dot(my, mean[k * 32 : k * 32 + 32])
        if 1 <= k <= 10:
            value = value + dot(ry, coarse[(k - 1) * 32 : k * 32])
        pk_ref[k] = value
    own2[...] = pk_ref[2:10]
    dn2[...] = pk_ref[2:12]
    upw2[...] = pk_ref[0:10]


def down1(src, mob, xlo, xhi, ylo, yhi):
    big = jax.ShapeDtypeStruct((N1, 32, 128), F32)
    vmem = pl.BlockSpec(memory_space=pltpu.VMEM)
    return pl.pallas_call(
        down1_kernel,
        in_specs=[vmem] * 6,
        out_specs=[vmem] * 9,
        out_shape=[jax.ShapeDtypeStruct((k, 16, 128), F32) for k in (8, 10, 10)] + [big] * 6,
        scratch_shapes=[pltpu.VMEM((N1, 32, 128), F32)] * 4
        + [pltpu.VMEM((384, 128), F32), pltpu.VMEM((12, 16, 128), F32)],
        compiler_params=pltpu.CompilerParams(vmem_limit_bytes=16 * MIB),
        name="down1",
    )(src, mob, xlo, xhi, ylo, yhi)


def pack2_kernel(own, xlo, xhi, out):
    low_x, high_x = edge("gx")
    out[:10] = blank(low_x, xlo[...], 0.0)
    out[10:18] = own[...]
    out[18:] = blank(high_x, xhi[...], 0.0)


def pack2(own, xlo, xhi):
    vmem = pl.BlockSpec(memory_space=pltpu.VMEM)
    return pl.pallas_call(
        pack2_kernel,
        in_specs=[vmem] * 3,
        out_specs=vmem,
        out_shape=jax.ShapeDtypeStruct((N2, 16, 128), F32),
        name="pack2",
    )(own, xlo, xhi)


def up_kernel(
    ext, ylo, yhi, s1, wx1, wy1, wz1, q1, down1_ref,
    wx0_h, wy0_h, wz0_h, d0_h, q0_h, s0_h, p0_h,
    scaled, residual,
    wx0, wy0, wz0, d0, q0, s0, pa0, pb0,
    pa1, pb1,
    s2, m2, wx2, wy2, wz2, d2, q2, pa2, pb2, r2,
    s3, m3, wx3, wy3, wz3, d3, q3, pa3, pb3,
    t_ref, u_ref, v_ref, sems,
):
    state = copies(
        [(wx0_h, wx0), (wy0_h, wy0), (wz0_h, wz0), (d0_h, d0), (q0_h, q0), (s0_h, s0), (p0_h, pa0)], sems
    )
    for copy in state:
        copy.start()
    low_y, high_y = edge("gy")

    lane8, sub8 = iota((8, 128), 1), iota((8, 128), 0)

    def unpack(j, carry):
        def put(rows, packed):
            s2[j, rows] = packed
            m2[j, rows] = jnp.where(lane8 < 64, pltpu.roll(packed, 64, 1), 0.0)

        hi = blank(high_y, yhi[j], 0.0)
        lo = blank(low_y, ylo[j], 0.0)
        put(slice(0, 8), ext[j, :8])
        put(slice(8, 16), hi[:8])
        put(slice(16, 24), jnp.where(sub8 < 4, hi[8:], lo[8:]))
        put(slice(24, 32), lo[:8])
        return carry

    lax.fori_loop(0, N2, unpack, 0)
    w2 = (wx2, wy2, wz2, d2, q2)

    def first2(j, q):
        pa2[j] = q * s2[j]

    weights_pass(1, N2 - 1, m2, w2, face_mean, 0.0, False, first2)
    sweep(2, N2 - 2, pa2, pb2, s2, w2)
    remainder(3, N2 - 3, pb2, r2, s2, w2)

    lane_in, lane_out = iota((128, 128), 0), iota((128, 128), 1)
    down_z = lane_in - 2 * lane_out
    inner = (lane_in < 64) & (lane_out < 32)
    rz = jnp.where(inner, restrict_weight(down_z), 0.0)
    mz = jnp.where(inner, pair_weight(down_z), 0.0)
    coarse_y = ring(iota((16, 32), 0), 8, 16)
    fine_y = ring(iota((16, 32), 1), 20, 32)
    ry = restrict_weight(fine_y - 2 * coarse_y)
    my = pair_weight(fine_y - 2 * coarse_y)
    for k in range(10):
        t_ref[k * 32 : k * 32 + 32] = restrict_x(r2, 2 * k + 3)
    coarse = dot(t_ref[:320], rz)
    for k in range(12):
        t_ref[k * 32 : k * 32 + 32] = (m2[2 * k + 2] + m2[2 * k + 3]) * (0.25 * 0.125)
    mean = dot(t_ref[:384], mz)
    for k in range(12):
        m3[k] = dot(my, mean[k * 32 : k * 32 + 32])
        if 1 <= k <= 10:
            s3[k] = dot(ry, coarse[(k - 1) * 32 : k * 32])
    w3 = (wx3, wy3, wz3, d3, q3)

    def first3(j, q):
        pa3[j] = q * s3[j]

    weights_pass(1, N3 - 1, m3, w3, face_mean, 0.0, False, first3)
    sweep(2, N3 - 2, pa3, pb3, s3, w3)

    pz = pair_weight(lane_out - 2 * lane_in)
    pz = jnp.where(lane_in < 32, pz, 0.0)
    py = pair_weight(ring(iota((32, 16), 0), 20, 32) - 2 * ring(iota((32, 16), 1), 8, 16))
    for k in range(8):
        t_ref[k * 32 : k * 32 + 32] = dot(py, pb3[k + 2])
    u_ref[:256] = dot(t_ref[:256], pz)
    for k in range(8):
        rise = u_ref[k * 32 : k * 32 + 32]
        pb2[2 * k + 6] = pb2[2 * k + 6] + rise
        pb2[2 * k + 7] = pb2[2 * k + 7] + rise
    sweep(7, 21, pb2, pa2, s2, w2)
    sweep(8, 20, pa2, pb2, s2, w2)

    pz = pair_weight(lane_out - 2 * lane_in)
    py = pair_weight(ring(iota((32, 32), 0), 24, 32) - 2 * ring(iota((32, 32), 1), 20, 32))
    for k in range(12):
        t_ref[k * 32 : k * 32 + 32] = dot(py, pb2[k + 8])
    u_ref[:384] = dot(t_ref[:384], pz)
    for k in range(12):
        rise = u_ref[k * 32 : k * 32 + 32]
        pa1[2 * k + 2] = down1_ref[2 * k + 2] + rise
        pa1[2 * k + 3] = down1_ref[2 * k + 3] + rise
    w1 = (wx1, wy1, wz1, None, q1)
    sweep(3, 25, pa1, pb1, s1, w1)
    sweep(4, 24, pb1, pa1, s1, w1)

    pz = pair_weight(iota((128, 256), 1) - 2 * iota((128, 256), 0))
    py = pair_weight(ring(iota((40, 32), 0), 36, 40) - 2 * ring(iota((40, 32), 1), 24, 32))
    for k in range(20):
        t_ref[k * 40 : k * 40 + 40] = dot(py, pa1[k + 4])
    v_ref[...] = dot(t_ref[...], pz)
    for copy in state:
        copy.wait()

    def rise0(j, carry):
        k = (j - 1) // 2
        pa0[j] = pa0[j] + v_ref[pl.ds(pl.multiple_of(k * 40, 8), 40)]
        return carry

    lax.fori_loop(2, N0 - 2, rise0, 0)
    w0 = (wx0, wy0, wz0, d0, q0)
    sweep(3, N0 - 3, pa0, pb0, s0, w0)
    sweep(4, N0 - 4, pb0, pa0, s0, w0)

    def last(j, carry):
        p = pa0[j]
        dp = d0[j] * p
        scaled[j - X0] = dp[:32]
        residual[j - X0] = (s0[j] + flow(j, p, pa0, w0) - dp)[:32]
        return carry

    lax.fori_loop(X0, X0 + 32, last, 0)


def way_up(ext, ylo, yhi, level1, level0):
    vmem = pl.BlockSpec(memory_space=pltpu.VMEM)
    anyw = pl.BlockSpec(memory_space=pl.ANY)
    shape = jax.ShapeDtypeStruct((32, 32, 256), F32)
    buf = lambda count, *shape: [pltpu.VMEM(shape, F32)] * count
    return pl.pallas_call(
        up_kernel,
        in_specs=[vmem] * 9 + [anyw] * 7,
        out_specs=[vmem] * 2,
        out_shape=[shape, shape],
        scratch_shapes=buf(8, N0, 40, 256)
        + buf(2, N1, 32, 128)
        + buf(10, N2, 32, 128)
        + buf(9, N3, 16, 128)
        + buf(1, 800, 128)
        + buf(1, 384, 128)
        + buf(1, 800, 256)
        + [pltpu.SemaphoreType.DMA((7,))],
        compiler_params=pltpu.CompilerParams(vmem_limit_bytes=40 * MIB),
        name="way_up",
    )(ext, ylo, yhi, *level1, *level0)


def shift(a, axis, step):
    count = lax.axis_size(axis)
    return lax.ppermute(a, axis, [(i, (i + step) % count) for i in range(count)])


def both(to_low, to_high, axis):
    return shift(to_high, axis, 1), shift(to_low, axis, -1)


def shards(source, phase):
    to_low = jnp.concatenate([source[:4], phase[:5].astype(F32)])
    to_high = jnp.concatenate([source[28:], phase[27:].astype(F32)])
    xlo, xhi = both(to_low, to_high, "gx")
    ylo, yhi = both(*pack0(source, phase, xlo, xhi), "gy")
    src1, mob1, dn1, up1, *level0 = down0(source, phase, xlo, xhi, ylo, yhi)
    xlo, xhi = both(dn1, up1, "gx")
    ylo, yhi = both(*pack1(src1, mob1, xlo, xhi), "gy")
    own2, dn2, up2, *level1 = down1(src1, mob1, xlo, xhi, ylo, yhi)
    xlo, xhi = both(dn2, up2, "gx")
    ext = pack2(own2, xlo, xhi)
    ylo, yhi = both(ext, ext, "gy")
    scaled, residual = way_up(ext, ylo, yhi, level1, level0)
    return scaled, residual


def solution(mesh):
    spec = P("gx", "gy", None)
    return jax.shard_map(shards, mesh=mesh, in_specs=(spec, spec), out_specs=(spec, spec), check_vma=False)
```

```python
import jax
import jax.numpy as jnp
from jax import lax
from jax.experimental import pallas as pl
from jax.experimental.pallas import tpu as pltpu
from jax.sharding import PartitionSpec as P

OMEGA = 0.8
KEEP = 0.2
WATER = 0.001
MIXED = 2.0 * WATER / (1.0 + WATER)
OUT = 0.25
F32 = jnp.float32
MIB = 1024 * 1024


def up_y(a):
    return pltpu.roll(a, a.shape[-2] - 1, a.ndim - 2)


def dn_y(a):
    return pltpu.roll(a, 1, a.ndim - 2)


def up_z(a):
    return pltpu.roll(a, a.shape[-1] - 1, a.ndim - 1)


def dn_z(a):
    return pltpu.roll(a, 1, a.ndim - 1)


def iota(shape, dim):
    return lax.broadcasted_iota(jnp.int32, shape, dim)


def ring(row, cut, rows):
    return jnp.where(row < cut, row, row - rows)


def restrict_weight(offset):
    near = (offset == 0) | (offset == 1)
    far = (offset == -1) | (offset == 2)
    return jnp.where(near, 0.375, jnp.where(far, 0.125, 0.0)).astype(F32)


def pair_weight(offset):
    return jnp.where((offset == 0) | (offset == 1), 1.0, 0.0).astype(F32)


def dot(a, b):
    return jnp.dot(a, b, precision=lax.Precision.HIGHEST, preferred_element_type=F32)


def face_code(a, b):
    s = a + b
    return jnp.where(s < 0.75, 1.0, jnp.where(s < 1.1, MIXED, WATER)).astype(F32)


def face_mean(a, b):
    product = a * b
    return jnp.where(product > 0.0, 2.0 * product / (a + b), jnp.maximum(a, b))


def blocks(lo, hi, size, work):
    count, rest = divmod(hi - lo, size)

    def body(i, carry):
        work(lo + i * size, size)
        return carry

    lax.fori_loop(0, count, body, 0)
    if rest:
        work(hi - rest, rest)


def weights_at(m_low, m, m_high, face, outside, full):
    lane = iota(m.shape, m.ndim - 1)
    last = m.shape[-1] - 1
    wx, wx_low = face(m, m_high), face(m_low, m)
    wy = face(m, up_y(m))
    m_up = up_z(m)
    if full:
        m_up = jnp.where(lane == last, outside, m_up)
    wz = face(m, m_up)
    wz_low = dn_z(wz)
    if full:
        wz_low = jnp.where(lane == 0, face(m, jnp.full_like(m, outside)), wz_low)
    d = (wx + wx_low) + (wy + dn_y(wy)) + (wz + wz_low)
    q = jnp.where(m != outside, OMEGA / d, 0.0)
    if full:
        wz = jnp.where(lane == last, 0.0, wz)
    return wx, wy, wz, d, q


def weights_pass(lo, hi, size, m_ref, w, face, outside, full, first):
    wx_ref, wy_ref, wz_ref, d_ref, q_ref = w
    wx_ref[lo - 1] = face(m_ref[lo - 1], m_ref[lo])

    def work(j, n):
        here = pl.ds(j, n)
        wx, wy, wz, d, q = weights_at(
            m_ref[pl.ds(j - 1, n)], m_ref[here], m_ref[pl.ds(j + 1, n)], face, outside, full
        )
        start = first(here, q)
        wx_ref[here] = wx
        wy_ref[here] = wy
        wz_ref[here] = wz
        d_ref[here] = d
        q_ref[here] = q
        start()

    blocks(lo, hi, size, work)


def flow(j, n, p, p_ref, w):
    wx_ref, wy_ref, wz_ref = w[:3]
    here, above, below = pl.ds(j, n), pl.ds(j + 1, n), pl.ds(j - 1, n)
    wy, wz = wy_ref[here], wz_ref[here]
    along_x = wx_ref[here] * p_ref[above] + wx_ref[below] * p_ref[below]
    along_y = wy * up_y(p) + dn_y(wy * p)
    along_z = wz * up_z(p) + dn_z(wz * p)
    return along_x + along_y + along_z


def sweep(lo, hi, size, p_ref, out_ref, s_ref, w):
    def work(j, n):
        here = pl.ds(j, n)
        p = p_ref[here]
        out_ref[here] = KEEP * p + w[4][here] * (s_ref[here] + flow(j, n, p, p_ref, w))

    blocks(lo, hi, size, work)


def remainder(lo, hi, size, p_ref, out_ref, s_ref, w):
    def work(j, n):
        here = pl.ds(j, n)
        p = p_ref[here]
        r = s_ref[here] + flow(j, n, p, p_ref, w) - w[3][here] * p
        out_ref[here] = jnp.where(w[4][here] > 0.0, r, 0.0)

    blocks(lo, hi, size, work)


def first_sweep(out_ref, s_ref):
    def first(here, q):
        p = q * s_ref[here]

        def start():
            out_ref[here] = p

        return start

    return first


def restrict_x(r_ref, j):
    return (r_ref[j] + r_ref[j + 3]) * 0.125 + (r_ref[j + 1] + r_ref[j + 2]) * 0.375


def edge(axis):
    i = lax.axis_index(axis)
    return i == 0, i == lax.axis_size(axis) - 1


def blank(flag, value, other):
    return jnp.where(flag, other, value)


X0 = 5
N0 = 32 + 2 * X0


def pack0_kernel(s_lo, s_hi, f_lo, f_hi, xl_lo, xl_hi, xh_lo, xh_hi, dn_ref, upw_ref, s_ref, c_ref):
    low_x, high_x = edge("gx")
    sub = iota((8, 256), 0)
    for own_s, own_f, xl, xh, out_ref, row in (
        (s_lo, f_lo, xl_lo, xh_lo, dn_ref, 3),
        (s_hi, f_hi, xl_hi, xh_hi, upw_ref, 4),
    ):
        s_ref[0] = jnp.zeros((8, 256), F32)
        s_ref[N0 - 1] = jnp.zeros((8, 256), F32)
        s_ref[1:X0] = blank(low_x, xl[:4], 0.0)
        c_ref[0:X0] = blank(low_x, xl[4:], OUT)
        s_ref[X0 + 32 : N0 - 1] = blank(high_x, xh[:4], 0.0)
        c_ref[X0 + 32 : N0] = blank(high_x, xh[4:], OUT)
        s_ref[X0 : X0 + 32] = own_s[...]
        c_ref[X0 : X0 + 32] = own_f[...].astype(F32)
        is_source = sub < 4 if row == 3 else sub >= 4

        def message(here, s, out_ref=out_ref, is_source=is_source):
            out_ref[here] = jnp.where(is_source, s, pltpu.roll(c_ref[here], 4, 1))

        message(pl.ds(0, 1), s_ref[0:1])
        message(pl.ds(N0 - 1, 1), s_ref[N0 - 1 :])

        def work(j, n, row=row, message=message):
            here = pl.ds(j, n)
            q = weights_at(c_ref[pl.ds(j - 1, n)], c_ref[here], c_ref[pl.ds(j + 1, n)], face_code, OUT, True)[-1]
            s = s_ref[here]
            message(here, jnp.where(sub == row, q * s, s))

        blocks(1, N0 - 1, 10, work)


def pack0(source, phase, xlo, xhi):
    own = lambda k: pl.BlockSpec((32, 8, 256), lambda i, k=k: (0, k, 0))
    halo = lambda k: pl.BlockSpec((9, 8, 256), lambda i, k=k: (0, k, 0))
    whole = pl.BlockSpec((N0, 8, 256), lambda i: (0, 0, 0))
    shape = jax.ShapeDtypeStruct((N0, 8, 256), F32)
    return pl.pallas_call(
        pack0_kernel,
        grid=(1,),
        in_specs=[own(0), own(3), own(0), own(3), halo(0), halo(3), halo(0), halo(3)],
        out_specs=[whole, whole],
        out_shape=[shape, shape],
        scratch_shapes=[pltpu.VMEM((N0, 8, 256), F32)] * 2,
        compiler_params=pltpu.CompilerParams(vmem_limit_bytes=6 * MIB),
        name="pack0",
    )(source, source, phase, phase, xlo, xlo, xhi, xhi)


N1 = 28
N2 = 28
N3 = 12


def down0_kernel(
    s_in, f_in, xlo, xhi, ylo, yhi,
    src1, mob1, dn1, upw1, wx, wy, wz, q_ref, s_ref, p2,
    c_ref, d_ref, p1, r_ref, t_ref,
):
    low_x, high_x = edge("gx")
    low_y, high_y = edge("gy")
    own = slice(X0, X0 + 32)
    s_ref[0, :32] = jnp.zeros((32, 256), F32)
    s_ref[N0 - 1, :32] = jnp.zeros((32, 256), F32)
    s_ref[1:X0, :32] = blank(low_x, xlo[:4], 0.0)
    c_ref[0:X0, :32] = blank(low_x, xlo[4:], OUT)
    s_ref[X0 + 32 : N0 - 1, :32] = blank(high_x, xhi[:4], 0.0)
    c_ref[X0 + 32 : N0, :32] = blank(high_x, xhi[4:], OUT)
    sub = iota((8, 256), 0)
    above = sub < 4
    outer = (above & high_y) | (~above & low_y)

    def tile4(j, n):
        here = pl.ds(j, n)
        hi, lo = yhi[here], ylo[here]
        s_ref[here, 32:] = jnp.where(outer, 0.0, jnp.where(above, hi, lo))
        c_ref[here, 32:] = jnp.where(outer, OUT, pltpu.roll(jnp.where(above, lo, hi), 4, 1))

    blocks(0, N0, 7, tile4)

    def own_planes(j, n):
        s_ref[pl.ds(j + X0, n), :32] = s_in[pl.ds(j, n)]
        c_ref[pl.ds(j + X0, n), :32] = f_in[pl.ds(j, n)].astype(F32)

    blocks(0, 32, 4, own_planes)

    w = (wx, wy, wz, d_ref, q_ref)
    row = iota((40, 256), 0)
    seam = (row == 35) | (row == 36)

    def first(here, q):
        s = s_ref[here]
        p = jnp.where(seam, s, q * s)

        def start():
            p1[here] = p

        return start

    weights_pass(1, N0 - 1, 4, c_ref, w, face_code, OUT, True, first)
    sweep(2, N0 - 2, 4, p1, p2, s_ref, w)
    remainder(4, N0 - 4, 4, p2, r_ref, s_ref, w)

    fine_z, coarse_z = iota((256, 128), 0), iota((256, 128), 1)
    fine_y = ring(iota((16, 40), 1), 36, 40)
    coarse_y = iota((16, 40), 0)
    rz = restrict_weight(fine_z - 2 * coarse_z)
    mz = pair_weight(fine_z - 2 * coarse_z)
    ry = restrict_weight(fine_y - 2 * coarse_y)
    my = pair_weight(fine_y - 2 * coarse_y)

    def halve(k, n):
        for i in range(n):
            t_ref[pl.ds(pl.multiple_of((k + i) * 40, 8), 40)] = restrict_x(r_ref, 2 * (k + i) + 4)

    blocks(0, 16, 4, halve)
    coarse = dot(t_ref[...], rz)
    for k in range(16):
        src1[k] = dot(ry, coarse[k * 40 : k * 40 + 40])

    def count(k, n):
        for i in range(n):
            j = 2 * (k + i) + X0
            t_ref[pl.ds(pl.multiple_of((k + i) * 40, 8), 40)] = c_ref[j] + c_ref[j + 1]

    blocks(0, 16, 4, count)
    water = dot(t_ref[...], mz)
    for k in range(16):
        n = dot(my, water[k * 40 : k * 40 + 40])
        mob1[k] = 0.25 * ((8.0 - n) * 0.125 + n * (0.125 * WATER))
    dn1[:5] = src1[:5]
    dn1[5:] = mob1[:6]
    upw1[:5] = src1[11:]
    upw1[5:] = mob1[10:]


def down0(source, phase, xlo, xhi, ylo, yhi):
    big = pltpu.VMEM((N0, 40, 256), F32)
    own1 = jax.ShapeDtypeStruct((16, 16, 128), F32)
    msg1 = jax.ShapeDtypeStruct((11, 16, 128), F32)
    vmem = pl.BlockSpec(memory_space=pltpu.VMEM)
    return pl.pallas_call(
        down0_kernel,
        in_specs=[vmem] * 6,
        out_specs=[vmem] * 10,
        out_shape=[own1, own1, msg1, msg1] + [big] * 6,
        scratch_shapes=[pltpu.VMEM((N0, 40, 256), F32)] * 4 + [pltpu.VMEM((640, 256), F32)],
        compiler_params=pltpu.CompilerParams(vmem_limit_bytes=16 * MIB),
        name="down0",
    )(source, phase, xlo, xhi, ylo, yhi)


def pack1_kernel(src, mob, xlo, xhi, dn_ref, upw_ref):
    low_x, high_x = edge("gx")
    for rows, out in ((slice(0, 8), dn_ref), (slice(8, 16), upw_ref)):
        out[0, :8] = jnp.zeros((8, 128), F32)
        out[N1 - 1, :8] = jnp.zeros((8, 128), F32)
        out[1:6, :8] = blank(low_x, xlo[:5, rows], 0.0)
        out[0:6, 8:] = blank(low_x, xlo[5:, rows], 0.0)
        out[6:22, :8] = src[:, rows]
        out[6:22, 8:] = mob[:, rows]
        out[22:27, :8] = blank(high_x, xhi[:5, rows], 0.0)
        out[22:28, 8:] = blank(high_x, xhi[5:, rows], 0.0)


def pack1(src, mob, xlo, xhi):
    shape = jax.ShapeDtypeStruct((N1, 16, 128), F32)
    vmem = pl.BlockSpec(memory_space=pltpu.VMEM)
    return pl.pallas_call(
        pack1_kernel,
        in_specs=[vmem] * 4,
        out_specs=[vmem] * 2,
        out_shape=[shape, shape],
        compiler_params=pltpu.CompilerParams(vmem_limit_bytes=4 * MIB),
        name="pack1",
    )(src, mob, xlo, xhi)


def down1_kernel(
    src, mob, xlo, xhi, ylo, yhi,
    own2, dn2, upw2, s_ref, wx, wy, wz, q_ref, p2,
    m_ref, d_ref, p1, r_ref, t_ref, pk_ref,
):
    low_x, high_x = edge("gx")
    low_y, high_y = edge("gy")
    zero = jnp.zeros((32, 128), F32)
    s_ref[0] = zero
    s_ref[N1 - 1] = zero
    s_ref[1:6, :16] = blank(low_x, xlo[:5], 0.0)
    m_ref[0:6, :16] = blank(low_x, xlo[5:], 0.0)
    s_ref[6:22, :16] = src[...]
    m_ref[6:22, :16] = mob[...]
    s_ref[22:27, :16] = blank(high_x, xhi[:5], 0.0)
    m_ref[22:28, :16] = blank(high_x, xhi[5:], 0.0)
    s_ref[:, 16:24] = blank(high_y, yhi[:, :8], 0.0)
    m_ref[:, 16:24] = blank(high_y, yhi[:, 8:], 0.0)
    s_ref[:, 24:] = blank(low_y, ylo[:, :8], 0.0)
    m_ref[:, 24:] = blank(low_y, ylo[:, 8:], 0.0)
    w = (wx, wy, wz, d_ref, q_ref)

    weights_pass(1, N1 - 1, 13, m_ref, w, face_mean, 0.0, True, first_sweep(p1, s_ref))
    sweep(2, N1 - 2, 12, p1, p2, s_ref, w)
    remainder(3, N1 - 3, 11, p2, r_ref, s_ref, w)

    lane_in, lane_out = iota((128, 128), 0), iota((128, 128), 1)
    rz = jnp.where(lane_out < 64, restrict_weight(lane_in - 2 * lane_out), 0.0)
    mz = pair_weight(lane_in - 2 * (lane_out - 64))
    row_out = iota((16, 32), 0)
    coarse_y = ring(row_out, 12, 16)
    held = (coarse_y >= -2) & (coarse_y <= 9)
    fine_y = ring(iota((16, 32), 1), 24, 32)
    ry = jnp.where(held, restrict_weight(fine_y - 2 * coarse_y), 0.0)
    my = jnp.where(held, pair_weight(fine_y - 2 * coarse_y), 0.0)
    zero16 = jnp.zeros((16, 128), F32)
    for k in range(10):
        t_ref[k * 32 : k * 32 + 32] = restrict_x(r_ref, 2 * k + 3)
    coarse = dot(t_ref[:320], rz)
    for k in range(12):
        t_ref[k * 32 : k * 32 + 32] = (m_ref[2 * k + 2] + m_ref[2 * k + 3]) * (0.25 * 0.125)
    mean = dot(t_ref[...], mz)
    for k in range(12):
        value = dot(my, mean[k * 32 : k * 32 + 32])
        if 1 <= k <= 10:
            value = value + dot(ry, coarse[(k - 1) * 32 : k * 32])
        pk_ref[k] = value
    own2[...] = pk_ref[2:10]
    dn2[...] = pk_ref[2:12]
    upw2[...] = pk_ref[0:10]


def down1(src, mob, xlo, xhi, ylo, yhi):
    vmem = pl.BlockSpec(memory_space=pltpu.VMEM)
    return pl.pallas_call(
        down1_kernel,
        in_specs=[vmem] * 6,
        out_specs=[vmem] * 9,
        out_shape=[jax.ShapeDtypeStruct((k, 16, 128), F32) for k in (8, 10, 10)] + [pltpu.VMEM((N1, 32, 128), F32)] * 6,
        scratch_shapes=[pltpu.VMEM((N1, 32, 128), F32)] * 4
        + [pltpu.VMEM((384, 128), F32), pltpu.VMEM((12, 16, 128), F32)],
        compiler_params=pltpu.CompilerParams(vmem_limit_bytes=8 * MIB),
        name="down1",
    )(src, mob, xlo, xhi, ylo, yhi)


def pack2_kernel(own, xlo, xhi, out):
    low_x, high_x = edge("gx")
    out[:10] = blank(low_x, xlo[...], 0.0)
    out[10:18] = own[...]
    out[18:] = blank(high_x, xhi[...], 0.0)


def pack2(own, xlo, xhi):
    vmem = pl.BlockSpec(memory_space=pltpu.VMEM)
    return pl.pallas_call(
        pack2_kernel,
        in_specs=[vmem] * 3,
        out_specs=vmem,
        out_shape=jax.ShapeDtypeStruct((N2, 16, 128), F32),
        compiler_params=pltpu.CompilerParams(vmem_limit_bytes=4 * MIB),
        name="pack2",
    )(own, xlo, xhi)


def up_kernel(
    ext, ylo, yhi, s1, wx1, wy1, wz1, q1, down1_ref,
    wx0, wy0, wz0, q0, s0, down0_ref,
    scaled, residual,
    pa0, pb0,
    pa1, pb1,
    s2, m2, wx2, wy2, wz2, d2, q2, pa2, pb2, r2,
    s3, m3, wx3, wy3, wz3, d3, q3, pa3, pb3,
    t_ref, u_ref, v_ref,
):
    low_y, high_y = edge("gy")

    lane8, sub8 = iota((8, 128), 1), iota((8, 128), 0)

    def unpack(j, carry):
        def put(rows, packed):
            s2[j, rows] = packed
            m2[j, rows] = jnp.where(lane8 < 64, pltpu.roll(packed, 64, 1), 0.0)

        hi = blank(high_y, yhi[j], 0.0)
        lo = blank(low_y, ylo[j], 0.0)
        put(slice(0, 8), ext[j, :8])
        put(slice(8, 16), hi[:8])
        put(slice(16, 24), jnp.where(sub8 < 4, hi[8:], lo[8:]))
        put(slice(24, 32), lo[:8])
        return carry

    lax.fori_loop(0, N2, unpack, 0)
    w2 = (wx2, wy2, wz2, d2, q2)

    weights_pass(1, N2 - 1, 13, m2, w2, face_mean, 0.0, False, first_sweep(pa2, s2))
    sweep(2, N2 - 2, 12, pa2, pb2, s2, w2)
    remainder(3, N2 - 3, 11, pb2, r2, s2, w2)

    lane_in, lane_out = iota((128, 128), 0), iota((128, 128), 1)
    down_z = lane_in - 2 * lane_out
    inner = (lane_in < 64) & (lane_out < 32)
    rz = jnp.where(inner, restrict_weight(down_z), 0.0)
    mz = jnp.where(inner, pair_weight(down_z), 0.0)
    coarse_y = ring(iota((16, 32), 0), 8, 16)
    fine_y = ring(iota((16, 32), 1), 20, 32)
    ry = restrict_weight(fine_y - 2 * coarse_y)
    my = pair_weight(fine_y - 2 * coarse_y)
    for k in range(10):
        t_ref[k * 32 : k * 32 + 32] = restrict_x(r2, 2 * k + 3)
    coarse = dot(t_ref[:320], rz)
    for k in range(12):
        t_ref[k * 32 : k * 32 + 32] = (m2[2 * k + 2] + m2[2 * k + 3]) * (0.25 * 0.125)
    mean = dot(t_ref[:384], mz)
    for k in range(12):
        m3[k] = dot(my, mean[k * 32 : k * 32 + 32])
        if 1 <= k <= 10:
            s3[k] = dot(ry, coarse[(k - 1) * 32 : k * 32])
    w3 = (wx3, wy3, wz3, d3, q3)

    weights_pass(1, N3 - 1, 10, m3, w3, face_mean, 0.0, False, first_sweep(pa3, s3))
    sweep(2, N3 - 2, 8, pa3, pb3, s3, w3)

    pz = pair_weight(lane_out - 2 * lane_in)
    pz = jnp.where(lane_in < 32, pz, 0.0)
    py = pair_weight(ring(iota((32, 16), 0), 20, 32) - 2 * ring(iota((32, 16), 1), 8, 16))
    for k in range(8):
        t_ref[k * 32 : k * 32 + 32] = dot(py, pb3[k + 2])
    u_ref[:256] = dot(t_ref[:256], pz)
    for k in range(8):
        rise = u_ref[k * 32 : k * 32 + 32]
        pb2[2 * k + 6] = pb2[2 * k + 6] + rise
        pb2[2 * k + 7] = pb2[2 * k + 7] + rise
    sweep(7, 21, 7, pb2, pa2, s2, w2)
    sweep(8, 20, 12, pa2, pb2, s2, w2)

    pz = pair_weight(lane_out - 2 * lane_in)
    py = pair_weight(ring(iota((32, 32), 0), 24, 32) - 2 * ring(iota((32, 32), 1), 20, 32))
    for k in range(12):
        t_ref[k * 32 : k * 32 + 32] = dot(py, pb2[k + 8])
    u_ref[:384] = dot(t_ref[:384], pz)
    for k in range(12):
        rise = u_ref[k * 32 : k * 32 + 32]
        pa1[2 * k + 2] = down1_ref[2 * k + 2] + rise
        pa1[2 * k + 3] = down1_ref[2 * k + 3] + rise
    w1 = (wx1, wy1, wz1, None, q1)
    sweep(3, 25, 11, pa1, pb1, s1, w1)
    sweep(4, 24, 10, pb1, pa1, s1, w1)

    pz = pair_weight(iota((128, 256), 1) - 2 * iota((128, 256), 0))
    py = pair_weight(ring(iota((40, 32), 0), 36, 40) - 2 * ring(iota((40, 32), 1), 24, 32))
    for k in range(20):
        t_ref[k * 40 : k * 40 + 40] = dot(py, pa1[k + 4])
    v_ref[...] = dot(t_ref[...], pz)

    def rise0(k, n):
        for i in range(n):
            rise = v_ref[pl.ds(pl.multiple_of((k + i) * 40, 8), 40)]
            for j in (2 * (k + i) + 1, 2 * (k + i) + 2):
                pa0[j] = down0_ref[j] + rise

    pa0[2] = down0_ref[2] + v_ref[:40]
    blocks(1, 19, 3, rise0)
    pa0[N0 - 3] = down0_ref[N0 - 3] + v_ref[760:]
    w0 = (wx0, wy0, wz0, None, q0)
    sweep(3, N0 - 3, 4, pa0, pb0, s0, w0)
    sweep(4, N0 - 4, 4, pb0, pa0, s0, w0)

    def last(j, n):
        here, out = pl.ds(j, n), pl.ds(j - X0, n)
        p = pa0[here]
        dp = (OMEGA / q0[here]) * p
        scaled[out] = dp[:, :32]
        residual[out] = (s0[here] + flow(j, n, p, pa0, w0) - dp)[:, :32]

    blocks(X0, X0 + 32, 4, last)


def way_up(ext, ylo, yhi, level1, level0):
    vmem = pl.BlockSpec(memory_space=pltpu.VMEM)
    shape = jax.ShapeDtypeStruct((32, 32, 256), F32)
    buf = lambda count, *shape: [pltpu.VMEM(shape, F32)] * count
    return pl.pallas_call(
        up_kernel,
        in_specs=[vmem] * 15,
        out_specs=[vmem] * 2,
        out_shape=[shape, shape],
        scratch_shapes=buf(2, N0, 40, 256)
        + buf(2, N1, 32, 128)
        + buf(10, N2, 32, 128)
        + buf(9, N3, 16, 128)
        + buf(1, 800, 128)
        + buf(1, 384, 128)
        + buf(1, 800, 256),
        compiler_params=pltpu.CompilerParams(vmem_limit_bytes=20 * MIB),
        name="way_up",
    )(ext, ylo, yhi, *level1, *level0)


def shift(a, axis, step):
    count = lax.axis_size(axis)
    return lax.ppermute(a, axis, [(i, (i + step) % count) for i in range(count)])


def both(to_low, to_high, axis):
    return shift(to_high, axis, 1), shift(to_low, axis, -1)


def shards(source, phase):
    to_low = jnp.concatenate([source[:4], phase[:5].astype(F32)])
    to_high = jnp.concatenate([source[28:], phase[27:].astype(F32)])
    xlo, xhi = both(to_low, to_high, "gx")
    ylo, yhi = both(*pack0(source, phase, xlo, xhi), "gy")
    src1, mob1, dn1, up1, *level0 = down0(source, phase, xlo, xhi, ylo, yhi)
    xlo, xhi = both(dn1, up1, "gx")
    ylo, yhi = both(*pack1(src1, mob1, xlo, xhi), "gy")
    own2, dn2, up2, *level1 = down1(src1, mob1, xlo, xhi, ylo, yhi)
    xlo, xhi = both(dn2, up2, "gx")
    ext = pack2(own2, xlo, xhi)
    ylo, yhi = both(ext, ext, "gy")
    scaled, residual = way_up(ext, ylo, yhi, level1, level0)
    return scaled, residual


def solution(mesh):
    spec = P("gx", "gy", None)
    return jax.shard_map(shards, mesh=mesh, in_specs=(spec, spec), out_specs=(spec, spec), check_vma=False)
```

```python
import jax
import jax.numpy as jnp
from jax import lax
from jax.experimental import pallas as pl
from jax.experimental.pallas import tpu as pltpu
from jax.sharding import PartitionSpec as P

OMEGA = 0.8
KEEP = 0.2
WATER = 0.001
MIXED = 2.0 * WATER / (1.0 + WATER)
OUT = 0.25
F32 = jnp.float32
MIB = 1024 * 1024


def up_y(a):
    return pltpu.roll(a, a.shape[-2] - 1, a.ndim - 2)


def dn_y(a):
    return pltpu.roll(a, 1, a.ndim - 2)


def up_z(a):
    return pltpu.roll(a, a.shape[-1] - 1, a.ndim - 1)


def dn_z(a):
    return pltpu.roll(a, 1, a.ndim - 1)


def iota(shape, dim):
    return lax.broadcasted_iota(jnp.int32, shape, dim)


def ring(row, cut, rows):
    return jnp.where(row < cut, row, row - rows)


def restrict_weight(offset):
    near = (offset == 0) | (offset == 1)
    far = (offset == -1) | (offset == 2)
    return jnp.where(near, 0.375, jnp.where(far, 0.125, 0.0)).astype(F32)


def pair_weight(offset):
    return jnp.where((offset == 0) | (offset == 1), 1.0, 0.0).astype(F32)


def dot(a, b):
    return jnp.dot(a, b, precision=lax.Precision.HIGHEST, preferred_element_type=F32)


def face_code(a, b):
    s = a + b
    return jnp.where(s < 0.75, 1.0, jnp.where(s < 1.1, MIXED, WATER)).astype(F32)


def face_mean(a, b):
    product = a * b
    return jnp.where(product > 0.0, 2.0 * product / (a + b), jnp.maximum(a, b))


def blocks(lo, hi, size, work):
    count, rest = divmod(hi - lo, size)
    if count == 1:
        work(lo, size)
    elif count:

        def body(i, carry):
            work(lo + i * size, size)
            return carry

        lax.fori_loop(0, count, body, 0)
    if rest:
        work(hi - rest, rest)


def planes(lo, hi, size, plane, refs):
    def work(j, n):
        results = [plane(j + i) for i in range(n)]
        for i, values in enumerate(results):
            for ref, value in zip(refs, values):
                ref[j + i] = value

    blocks(lo, hi, size, work)


def weights_at(m_low, m, m_high, face, outside, full):
    lane = iota(m.shape, m.ndim - 1)
    last = m.shape[-1] - 1
    wx, wx_low = face(m, m_high), face(m_low, m)
    wy = face(m, up_y(m))
    m_up = up_z(m)
    if full:
        m_up = jnp.where(lane == last, outside, m_up)
    wz = face(m, m_up)
    wz_low = dn_z(wz)
    if full:
        wz_low = jnp.where(lane == 0, face(m, jnp.full_like(m, outside)), wz_low)
    d = (wx + wx_low) + (wy + dn_y(wy)) + (wz + wz_low)
    q = jnp.where(m != outside, OMEGA / d, 0.0)
    if full:
        wz = jnp.where(lane == last, 0.0, wz)
    return wx, wy, wz, q


def weights_pass(lo, hi, size, m_ref, w, s_ref, p_ref, face, outside, full):
    w[0][lo - 1] = face(m_ref[lo - 1], m_ref[lo])

    def plane(j):
        wx, wy, wz, q = weights_at(m_ref[j - 1], m_ref[j], m_ref[j + 1], face, outside, full)
        return wx, wy, wz, q, q * s_ref[j]

    planes(lo, hi, size, plane, (*w, p_ref))


def flow(j, p, p_ref, w):
    wx_ref, wy_ref, wz_ref = w[:3]
    wy, wz = wy_ref[j], wz_ref[j]
    along_x = wx_ref[j] * p_ref[j + 1] + wx_ref[j - 1] * p_ref[j - 1]
    along_y = wy * up_y(p) + dn_y(wy * p)
    along_z = wz * up_z(p) + dn_z(wz * p)
    return along_x + along_y + along_z


def sweep(lo, hi, size, p_ref, out_ref, s_ref, w):
    def plane(j):
        p = p_ref[j]
        return (KEEP * p + w[3][j] * (s_ref[j] + flow(j, p, p_ref, w)),)

    planes(lo, hi, size, plane, (out_ref,))


def remainder(lo, hi, size, p_ref, out_ref, s_ref, w):
    def plane(j):
        p, q = p_ref[j], w[3][j]
        r = s_ref[j] + flow(j, p, p_ref, w) - (OMEGA / q) * p
        return (jnp.where(q > 0.0, r, 0.0),)

    planes(lo, hi, size, plane, (out_ref,))


def restrict_x(r_ref, j):
    return (r_ref[j] + r_ref[j + 3]) * 0.125 + (r_ref[j + 1] + r_ref[j + 2]) * 0.375


def edge(axis):
    i = lax.axis_index(axis)
    return i == 0, i == lax.axis_size(axis) - 1


def blank(flag, value, other):
    return jnp.where(flag, other, value)


X0 = 5
N0 = 32 + 2 * X0
N1 = 28
N2 = 28
N3 = 12
BIG = (N0, 40, 256)
VM = pl.BlockSpec(memory_space=pltpu.VMEM)


def call(kernel, name, out_shape, scratch, limit, *operands, aliases=None, out_specs=None):
    return pl.pallas_call(
        kernel,
        in_specs=[VM] * len(operands),
        out_specs=[VM] * len(out_shape) if out_specs is None else out_specs,
        out_shape=out_shape,
        scratch_shapes=scratch,
        input_output_aliases=aliases or {},
        compiler_params=pltpu.CompilerParams(vmem_limit_bytes=limit * MIB),
        name=name,
    )(*operands)


def kept(*shape):
    return pltpu.VMEM(shape, F32)


def send_rows_kernel(s_in, f_in, dn_ref, upw_ref):
    above = iota((8, 256), 0) < 4

    def work(j, n):
        here = pl.ds(j, n)
        dn_ref[here] = jnp.where(above, s_in[here, :8], pltpu.roll(f_in[here, :8].astype(F32), 4, 1))
        upw_ref[here] = jnp.where(above, pltpu.roll(f_in[here, 24:].astype(F32), 4, 1), s_in[here, 24:])

    blocks(0, 32, 8, work)


def halo_rows(lo, hi):
    low_y, high_y = edge("gy")
    above = iota((8, 256), 0) < 4
    outer = (above & high_y) | (~above & low_y)
    source = jnp.where(outer, 0.0, jnp.where(above, hi, lo))
    code = jnp.where(outer, OUT, pltpu.roll(jnp.where(above, lo, hi), 4, lo.ndim - 2))
    return source, code


def send_planes_kernel(s_in, f_in, ylo, yhi, dn_ref, upw_ref):
    for first, out_ref, skip in ((0, dn_ref, 0), (28, upw_ref, 1)):
        block = slice(first, first + 4)
        source, code = halo_rows(ylo[block], yhi[block])
        out_ref[:3, :32] = s_in[first + skip : first + skip + 3]
        out_ref[:3, 32:] = source[skip : skip + 3]
        out_ref[3:, :32] = f_in[block].astype(F32)
        out_ref[3:, 32:] = code


def water_to_mobility(n):
    return 0.25 * ((8.0 - n) * 0.125 + n * (0.125 * WATER))


def rows_to_16():
    fine_y = ring(iota((16, 40), 1), 36, 40)
    return fine_y - 2 * iota((16, 40), 0)


def lanes_to_128():
    return iota((256, 128), 0) - 2 * iota((256, 128), 1)


def inner0_kernel(
    s_in, f_in, ylo, yhi,
    s_ref, c_ref, wx, wy, wz, q_ref, p1, p2, r_ref, src1, mob1,
    t_ref,
):
    def own_planes(j, n):
        here, there = pl.ds(j, n), pl.ds(j + X0, n)
        source, code = halo_rows(ylo[here], yhi[here])
        s_ref[there, :32] = s_in[here]
        s_ref[there, 32:] = source
        c_ref[there, :32] = f_in[here].astype(F32)
        c_ref[there, 32:] = code

    blocks(0, 32, 4, own_planes)
    w = (wx, wy, wz, q_ref)
    weights_pass(6, 36, 6, c_ref, w, s_ref, p1, face_code, OUT, True)
    sweep(7, 35, 7, p1, p2, s_ref, w)
    remainder(8, 34, 6, p2, r_ref, s_ref, w)

    ry, rz = restrict_weight(rows_to_16()), restrict_weight(lanes_to_128())
    my, mz = pair_weight(rows_to_16()), pair_weight(lanes_to_128())
    for k in range(2, 14):
        t_ref[k * 16 : k * 16 + 16] = dot(ry, restrict_x(r_ref, 2 * k + 4))
    coarse = dot(t_ref[32:224], rz)
    for k in range(2, 14):
        src1[k] = coarse[k * 16 - 32 : k * 16 - 16]
    for k in range(16):
        t_ref[k * 16 : k * 16 + 16] = dot(my, c_ref[2 * k + X0] + c_ref[2 * k + X0 + 1])
    mobility = water_to_mobility(dot(t_ref[...], mz))
    for k in range(16):
        mob1[k] = mobility[k * 16 : k * 16 + 16]


def inner0(source, phase, ylo, yhi):
    return call(
        inner0_kernel, "inner0", [kept(*BIG)] * 9 + [kept(16, 16, 128)] * 2,
        [kept(256, 256)], 4, source, phase, ylo, yhi,
    )


def lay_rows(out, first, rows):
    for k in range(4):
        out[first + k] = rows[k // 2 * 16 : k // 2 * 16 + 16, k % 2 * 128 : k % 2 * 128 + 128]


def outer0_kernel(
    xlo, xhi, mob1, s_0, c_0, wx_0, wy_0, wz_0, q_0, p1_0, p2_0, r_0, src1_0,
    s_ref, c_ref, wx, wy, wz, q_ref, p1, p2, r_ref, src1, dn1, upw1, rows_dn, rows_up,
    t_ref,
):
    low_x, high_x = edge("gx")
    s_ref[2:5] = blank(low_x, xlo[:3], 0.0)
    c_ref[1:5] = blank(low_x, xlo[3:], OUT)
    s_ref[37:40] = blank(high_x, xhi[:3], 0.0)
    c_ref[37:41] = blank(high_x, xhi[3:], OUT)
    w = (wx, wy, wz, q_ref)
    for lo in (2, 36):
        weights_pass(lo, lo + 4, 4, c_ref, w, s_ref, p1, face_code, OUT, True)
    for lo in (3, 35):
        sweep(lo, lo + 4, 4, p1, p2, s_ref, w)
    for lo in (4, 34):
        remainder(lo, lo + 4, 4, p2, r_ref, s_ref, w)
    ry, rz = restrict_weight(rows_to_16()), restrict_weight(lanes_to_128())
    edges = (0, 1, 14, 15)
    for i, k in enumerate(edges):
        t_ref[i * 16 : i * 16 + 16] = dot(ry, restrict_x(r_ref, 2 * k + 4))
    coarse = dot(t_ref[...], rz)
    for i, k in enumerate(edges):
        src1[k] = coarse[i * 16 : i * 16 + 16]
    dn1[:5] = src1[:5]
    dn1[5:11] = mob1[:6]
    lay_rows(dn1, 11, p2[X0 + 2, :32])
    upw1[:5] = src1[11:]
    upw1[5:11] = mob1[10:]
    lay_rows(upw1, 11, p2[X0 + 29, :32])
    for k in range(32):
        rows_dn[k : k + 1] = p2[X0 + k, 2:3]
        rows_up[k : k + 1] = p2[X0 + k, 29:30]


def outer0(xlo, xhi, mob1, state):
    return call(
        outer0_kernel, "outer0",
        [kept(*BIG)] * 9 + [kept(16, 16, 128)] + [kept(15, 16, 128)] * 2 + [kept(32, 256)] * 2,
        [kept(64, 256)], 4, xlo, xhi, mob1, *state, aliases={3 + k: k for k in range(10)},
    )


def pack1_kernel(src, mob, xlo, xhi, rows_dn, rows_up, dn_ref, upw_ref):
    low_x, high_x = edge("gx")
    for rows, out, p_rows in ((slice(0, 8), dn_ref, rows_dn), (slice(8, 16), upw_ref, rows_up)):
        out[0, :8] = jnp.zeros((8, 128), F32)
        out[N1 - 1, :8] = jnp.zeros((8, 128), F32)
        out[1:6, :8] = blank(low_x, xlo[:5, rows], 0.0)
        out[0:6, 8:] = blank(low_x, xlo[5:11, rows], 0.0)
        out[6:22, :8] = src[:, rows]
        out[6:22, 8:] = mob[:, rows]
        out[22:27, :8] = blank(high_x, xhi[:5, rows], 0.0)
        out[22:28, 8:] = blank(high_x, xhi[5:11, rows], 0.0)
        lay_rows(out, N1, p_rows[...])


def pack1(*operands):
    return call(pack1_kernel, "pack1", [kept(N1 + 4, 16, 128)] * 2, [], 4, *operands)


def down1_kernel(
    src, mob, xlo, xhi, ylo, yhi,
    own2, dn2, upw2, s_ref, wx, wy, wz, q_ref, p2,
    m_ref, p1, r_ref, t_ref, pk_ref,
):
    low_x, high_x = edge("gx")
    low_y, high_y = edge("gy")
    zero = jnp.zeros((32, 128), F32)
    s_ref[0] = zero
    s_ref[N1 - 1] = zero
    s_ref[1:6, :16] = blank(low_x, xlo[:5], 0.0)
    m_ref[0:6, :16] = blank(low_x, xlo[5:11], 0.0)
    s_ref[6:22, :16] = src[...]
    m_ref[6:22, :16] = mob[...]
    s_ref[22:27, :16] = blank(high_x, xhi[:5], 0.0)
    m_ref[22:28, :16] = blank(high_x, xhi[5:11], 0.0)
    s_ref[:, 16:24] = blank(high_y, yhi[:N1, :8], 0.0)
    m_ref[:, 16:24] = blank(high_y, yhi[:N1, 8:], 0.0)
    s_ref[:, 24:] = blank(low_y, ylo[:N1, :8], 0.0)
    m_ref[:, 24:] = blank(low_y, ylo[:N1, 8:], 0.0)
    w = (wx, wy, wz, q_ref)

    weights_pass(1, N1 - 1, 13, m_ref, w, s_ref, p1, face_mean, 0.0, True)
    sweep(2, N1 - 2, 12, p1, p2, s_ref, w)
    remainder(3, N1 - 3, 11, p2, r_ref, s_ref, w)

    lane_in, lane_out = iota((128, 128), 0), iota((128, 128), 1)
    rz = jnp.where(lane_out < 64, restrict_weight(lane_in - 2 * lane_out), 0.0)
    mz = pair_weight(lane_in - 2 * (lane_out - 64))
    row_out = iota((16, 32), 0)
    coarse_y = ring(row_out, 12, 16)
    held = (coarse_y >= -2) & (coarse_y <= 9)
    fine_y = ring(iota((16, 32), 1), 24, 32)
    ry = jnp.where(held, restrict_weight(fine_y - 2 * coarse_y), 0.0)
    my = jnp.where(held, pair_weight(fine_y - 2 * coarse_y), 0.0)
    zero16 = jnp.zeros((16, 128), F32)
    for k in range(10):
        t_ref[k * 32 : k * 32 + 32] = restrict_x(r_ref, 2 * k + 3)
    coarse = dot(t_ref[:320], rz)
    for k in range(12):
        t_ref[k * 32 : k * 32 + 32] = (m_ref[2 * k + 2] + m_ref[2 * k + 3]) * (0.25 * 0.125)
    mean = dot(t_ref[...], mz)
    for k in range(12):
        value = dot(my, mean[k * 32 : k * 32 + 32])
        if 1 <= k <= 10:
            value = value + dot(ry, coarse[(k - 1) * 32 : k * 32])
        pk_ref[k] = value
    own2[...] = pk_ref[2:10]
    dn2[...] = pk_ref[2:12]
    upw2[...] = pk_ref[0:10]


def down1(*operands):
    return call(
        down1_kernel, "down1", [kept(k, 16, 128) for k in (8, 10, 10)] + [kept(N1, 32, 128)] * 6,
        [kept(N1, 32, 128)] * 3 + [kept(384, 128), kept(12, 16, 128)], 6, *operands,
    )


def pack2_kernel(own, xlo, xhi, out):
    low_x, high_x = edge("gx")
    out[:10] = blank(low_x, xlo[...], 0.0)
    out[10:18] = own[...]
    out[18:] = blank(high_x, xhi[...], 0.0)


def pack2(*operands):
    return call(pack2_kernel, "pack2", [kept(N2, 16, 128)], [], 4, *operands)[0]


def up_kernel(
    ext, ylo, yhi, s1, wx1, wy1, wz1, q1, down1_ref,
    wx0, wy0, wz0, q0, s0, down0_ref, plane_lo, plane_hi, rows_lo, rows_hi,
    scaled, residual,
    pa0, pb0,
    pa1, pb1,
    s2, m2, wx2, wy2, wz2, q2, pa2, pb2, r2,
    s3, m3, wx3, wy3, wz3, q3, pa3, pb3,
    t_ref, u_ref, v_ref, out_a, out_b, row_ref, sems,
):
    low_y, high_y = edge("gy")

    lane8, sub8 = iota((8, 128), 1), iota((8, 128), 0)

    def unpack(j, carry):
        def put(rows, packed):
            s2[j, rows] = packed
            m2[j, rows] = jnp.where(lane8 < 64, pltpu.roll(packed, 64, 1), 0.0)

        hi = blank(high_y, yhi[j], 0.0)
        lo = blank(low_y, ylo[j], 0.0)
        put(slice(0, 8), ext[j, :8])
        put(slice(8, 16), hi[:8])
        put(slice(16, 24), jnp.where(sub8 < 4, hi[8:], lo[8:]))
        put(slice(24, 32), lo[:8])
        return carry

    lax.fori_loop(0, N2, unpack, 0)
    w2 = (wx2, wy2, wz2, q2)

    weights_pass(1, N2 - 1, 13, m2, w2, s2, pa2, face_mean, 0.0, False)
    sweep(2, N2 - 2, 12, pa2, pb2, s2, w2)
    remainder(3, N2 - 3, 11, pb2, r2, s2, w2)

    lane_in, lane_out = iota((128, 128), 0), iota((128, 128), 1)
    down_z = lane_in - 2 * lane_out
    inner = (lane_in < 64) & (lane_out < 32)
    rz = jnp.where(inner, restrict_weight(down_z), 0.0)
    mz = jnp.where(inner, pair_weight(down_z), 0.0)
    coarse_y = ring(iota((16, 32), 0), 8, 16)
    fine_y = ring(iota((16, 32), 1), 20, 32)
    ry = restrict_weight(fine_y - 2 * coarse_y)
    my = pair_weight(fine_y - 2 * coarse_y)
    for k in range(10):
        t_ref[k * 32 : k * 32 + 32] = restrict_x(r2, 2 * k + 3)
    coarse = dot(t_ref[:320], rz)
    for k in range(12):
        t_ref[k * 32 : k * 32 + 32] = (m2[2 * k + 2] + m2[2 * k + 3]) * (0.25 * 0.125)
    mean = dot(t_ref[:384], mz)
    for k in range(12):
        m3[k] = dot(my, mean[k * 32 : k * 32 + 32])
        if 1 <= k <= 10:
            s3[k] = dot(ry, coarse[(k - 1) * 32 : k * 32])
    w3 = (wx3, wy3, wz3, q3)

    weights_pass(1, N3 - 1, 10, m3, w3, s3, pa3, face_mean, 0.0, False)
    sweep(2, N3 - 2, 8, pa3, pb3, s3, w3)

    pz = pair_weight(lane_out - 2 * lane_in)
    pz = jnp.where(lane_in < 32, pz, 0.0)
    py = pair_weight(ring(iota((32, 16), 0), 20, 32) - 2 * ring(iota((32, 16), 1), 8, 16))
    for k in range(8):
        t_ref[k * 32 : k * 32 + 32] = dot(py, pb3[k + 2])
    u_ref[:256] = dot(t_ref[:256], pz)
    for k in range(8):
        rise = u_ref[k * 32 : k * 32 + 32]
        pb2[2 * k + 6] = pb2[2 * k + 6] + rise
        pb2[2 * k + 7] = pb2[2 * k + 7] + rise
    sweep(7, 21, 7, pb2, pa2, s2, w2)
    sweep(8, 20, 12, pa2, pb2, s2, w2)

    pz = pair_weight(lane_out - 2 * lane_in)
    py = pair_weight(ring(iota((32, 32), 0), 24, 32) - 2 * ring(iota((32, 32), 1), 20, 32))
    for k in range(12):
        t_ref[k * 32 : k * 32 + 32] = dot(py, pb2[k + 8])
    u_ref[:384] = dot(t_ref[:384], pz)
    for k in range(12):
        rise = u_ref[k * 32 : k * 32 + 32]
        pa1[2 * k + 2] = down1_ref[2 * k + 2] + rise
        pa1[2 * k + 3] = down1_ref[2 * k + 3] + rise
    w1 = (wx1, wy1, wz1, q1)
    sweep(3, 25, 11, pa1, pb1, s1, w1)
    sweep(4, 24, 10, pb1, pa1, s1, w1)

    pz = pair_weight(iota((128, 256), 1) - 2 * iota((128, 256), 0))
    py = pair_weight(ring(iota((40, 32), 0), 36, 40) - 2 * ring(iota((40, 32), 1), 24, 32))
    for k in range(20):
        t_ref[k * 40 : k * 40 + 40] = dot(py, pa1[k + 4])
    v_ref[...] = dot(t_ref[...], pz)

    def rise0(k, n):
        for i in range(n):
            rise = v_ref[pl.ds(pl.multiple_of((k + i) * 40, 8), 40)]
            for j in (2 * (k + i) + 1, 2 * (k + i) + 2):
                pa0[j] = down0_ref[j] + rise

    low_x, high_x = edge("gx")
    row8 = iota((8, 256), 0)

    def plane_of(message, first):
        tiles = [message[first + k] for k in range(4)]
        return jnp.concatenate(
            [jnp.concatenate(tiles[:2], 1), jnp.concatenate(tiles[2:], 1), jnp.zeros((8, 256), F32)], 0
        )

    pa0[2] = v_ref[:40] + blank(low_x, plane_of(plane_lo, 11), 0.0)
    pa0[N0 - 3] = v_ref[760:] + blank(high_x, plane_of(plane_hi, 11), 0.0)
    for k in range(4):
        h, z = k // 2 * 16, k % 2 * 128
        row_ref[0, h : h + 16, z : z + 128] = blank(high_y, rows_hi[N1 + k], 0.0)
        row_ref[1, h : h + 16, z : z + 128] = blank(low_y, rows_lo[N1 + k], 0.0)
    for j in (3, 4, 37, 38):
        k = (j - 1) // 2
        pa0[j] = down0_ref[j] + v_ref[k * 40 : k * 40 + 40]

    def rise0(k, n):
        for i in range(n):
            rise = v_ref[pl.ds(pl.multiple_of((k + i) * 40, 8), 40)]
            for j in (2 * (k + i) + 1, 2 * (k + i) + 2):
                pa0[j, :32] = down0_ref[j, :32] + rise[:32]
                above = row_ref[0, pl.ds(j - X0, 1)]
                below = row_ref[1, pl.ds(j - X0, 1)]
                halo = jnp.where(row8 == 2, above, jnp.where(row8 == 5, below, down0_ref[j, 32:]))
                pa0[j, 32:] = halo + rise[32:]

    blocks(2, 18, 2, rise0)
    w0 = (wx0, wy0, wz0, q0)
    sweep(3, N0 - 3, 6, pa0, pb0, s0, w0)
    sweep(4, N0 - 4, 8, pb0, pa0, s0, w0)

    def out_copies(k, j):
        here = pl.ds(j, 8)
        return (
            pltpu.make_async_copy(out_a.at[here], scaled.at[here], sems.at[0, k]),
            pltpu.make_async_copy(out_b.at[here], residual.at[here], sems.at[1, k]),
        )

    def last(k, carry):
        j = k * 8
        results = []
        for i in range(8):
            p = pa0[j + i + X0]
            dp = (OMEGA / q0[j + i + X0]) * p
            results.append((dp[:32], (s0[j + i + X0] + flow(j + i + X0, p, pa0, w0) - dp)[:32]))
        for i, (a, b) in enumerate(results):
            out_a[j + i] = a
            out_b[j + i] = b
        for copy in out_copies(k, j):
            copy.start()
        return carry

    lax.fori_loop(0, 4, last, 0)
    for k in range(4):
        for copy in out_copies(k, k * 8):
            copy.wait()


def way_up(*operands):
    shape = jax.ShapeDtypeStruct((32, 32, 256), F32)
    buf = lambda count, *shape: [kept(*shape)] * count
    scratch = (
        buf(2, *BIG)
        + buf(2, N1, 32, 128)
        + buf(9, N2, 32, 128)
        + buf(8, N3, 16, 128)
        + buf(1, 800, 128)
        + buf(1, 384, 128)
        + buf(1, 800, 256)
        + buf(2, 32, 32, 256)
        + buf(1, 2, 32, 256)
        + [pltpu.SemaphoreType.DMA((2, 4))]
    )
    hbm = pl.BlockSpec(memory_space=pl.ANY)
    return call(up_kernel, "way_up", [shape] * 2, scratch, 20, *operands, out_specs=[hbm] * 2)


def shift(a, axis, step):
    count = lax.axis_size(axis)
    return lax.ppermute(a, axis, [(i, (i + step) % count) for i in range(count)])


def both(to_low, to_high, axis):
    return shift(to_high, axis, 1), shift(to_low, axis, -1)


def shards(source, phase):
    msg = [kept(32, 8, 256)] * 2
    ylo, yhi = both(*call(send_rows_kernel, "send_rows", msg, [], 4, source, phase), "gy")
    msg = [kept(7, 40, 256)] * 2
    dn0, up0 = call(send_planes_kernel, "send_planes", msg, [], 4, source, phase, ylo, yhi)
    xlo, xhi = both(dn0, up0, "gx")
    *state, mob1 = inner0(source, phase, ylo, yhi)
    s0, _, wx0, wy0, wz0, q0, _, p0, _, src1, dn1, up1, rows_dn, rows_up = outer0(xlo, xhi, mob1, state)
    xlo1, xhi1 = both(dn1, up1, "gx")
    ylo1, yhi1 = both(*pack1(src1, mob1, xlo1, xhi1, rows_dn, rows_up), "gy")
    own2, dn2, up2, *level1 = down1(src1, mob1, xlo1, xhi1, ylo1, yhi1)
    xlo, xhi = both(dn2, up2, "gx")
    ext = pack2(own2, xlo, xhi)
    ylo, yhi = both(ext, ext, "gy")
    level0 = (wx0, wy0, wz0, q0, s0, p0, xlo1, xhi1, ylo1, yhi1)
    return tuple(way_up(ext, ylo, yhi, *level1, *level0))


def solution(mesh):
    spec = P("gx", "gy", None)
    return jax.shard_map(shards, mesh=mesh, in_specs=(spec, spec), out_specs=(spec, spec), check_vma=False)
```

```python
import jax
import jax.numpy as jnp
from jax import lax
from jax.experimental import pallas as pl
from jax.experimental.pallas import tpu as pltpu
from jax.sharding import PartitionSpec as P

OMEGA = 0.8
KEEP = 0.2
WATER = 0.001
MIXED = 2.0 * WATER / (1.0 + WATER)
OUT = 0.25
F32 = jnp.float32
MIB = 1024 * 1024


def up_y(a):
    return pltpu.roll(a, a.shape[-2] - 1, a.ndim - 2)


def dn_y(a):
    return pltpu.roll(a, 1, a.ndim - 2)


def up_z(a):
    return pltpu.roll(a, a.shape[-1] - 1, a.ndim - 1)


def dn_z(a):
    return pltpu.roll(a, 1, a.ndim - 1)


def iota(shape, dim):
    return lax.broadcasted_iota(jnp.int32, shape, dim)


def ring(row, cut, rows):
    return jnp.where(row < cut, row, row - rows)


def restrict_weight(offset):
    near = (offset == 0) | (offset == 1)
    far = (offset == -1) | (offset == 2)
    return jnp.where(near, 0.375, jnp.where(far, 0.125, 0.0)).astype(F32)


def pair_weight(offset):
    return jnp.where((offset == 0) | (offset == 1), 1.0, 0.0).astype(F32)


def dot(a, b):
    return jnp.dot(a, b, precision=lax.Precision.HIGHEST, preferred_element_type=F32)


def face_code(a, b):
    s = a + b
    return jnp.where(s < 0.75, 1.0, jnp.where(s < 1.1, MIXED, WATER)).astype(F32)


def face_mean(a, b):
    product = a * b
    return jnp.where(product > 0.0, 2.0 * product / (a + b), jnp.maximum(a, b))


def blocks(lo, hi, size, work):
    count, rest = divmod(hi - lo, size)
    if count == 1:
        work(lo, size)
    elif count:

        def body(i, carry):
            work(lo + i * size, size)
            return carry

        lax.fori_loop(0, count, body, 0)
    if rest:
        work(hi - rest, rest)


def planes(lo, hi, size, plane, refs):
    def work(j, n):
        results = [plane(j + i) for i in range(n)]
        for i, values in enumerate(results):
            for ref, value in zip(refs, values):
                ref[j + i] = value

    blocks(lo, hi, size, work)


def weights_at(m_low, m, m_high, face, outside, full):
    lane = iota(m.shape, m.ndim - 1)
    last = m.shape[-1] - 1
    wx, wx_low = face(m, m_high), face(m_low, m)
    wy = face(m, up_y(m))
    m_up = up_z(m)
    if full:
        m_up = jnp.where(lane == last, outside, m_up)
    wz = face(m, m_up)
    wz_low = dn_z(wz)
    if full:
        wz_low = jnp.where(lane == 0, face(m, jnp.full_like(m, outside)), wz_low)
    d = (wx + wx_low) + (wy + dn_y(wy)) + (wz + wz_low)
    q = jnp.where(m != outside, OMEGA / d, 0.0)
    if full:
        wz = jnp.where(lane == last, 0.0, wz)
    return wx, wy, wz, q


def weights_pass(lo, hi, size, m_ref, w, s_ref, p_ref, face, outside, full):
    w[0][lo - 1] = face(m_ref[lo - 1], m_ref[lo])

    def plane(j):
        wx, wy, wz, q = weights_at(m_ref[j - 1], m_ref[j], m_ref[j + 1], face, outside, full)
        return wx, wy, wz, q, q * s_ref[j]

    planes(lo, hi, size, plane, (*w, p_ref))


def flow(j, p, p_ref, w):
    wx_ref, wy_ref, wz_ref = w[:3]
    wy, wz = wy_ref[j], wz_ref[j]
    along_x = wx_ref[j] * p_ref[j + 1] + wx_ref[j - 1] * p_ref[j - 1]
    along_y = wy * up_y(p) + dn_y(wy * p)
    along_z = wz * up_z(p) + dn_z(wz * p)
    return along_x + along_y + along_z


def sweep(lo, hi, size, p_ref, out_ref, s_ref, w):
    def plane(j):
        p = p_ref[j]
        return (KEEP * p + w[3][j] * (s_ref[j] + flow(j, p, p_ref, w)),)

    planes(lo, hi, size, plane, (out_ref,))


def remainder(lo, hi, size, p_ref, out_ref, s_ref, w):
    def plane(j):
        p, q = p_ref[j], w[3][j]
        r = s_ref[j] + flow(j, p, p_ref, w) - (OMEGA / q) * p
        return (jnp.where(q > 0.0, r, 0.0),)

    planes(lo, hi, size, plane, (out_ref,))


def halving(valid):
    lane_in, lane_out = iota((256, 128), 0), iota((256, 128), 1)
    down = jnp.where((lane_in < 128) & (lane_out < valid), restrict_weight(lane_in - 2 * lane_out), 0.0)
    return down + jnp.where(lane_in >= 128, pair_weight(lane_in - 2 * lane_out), 0.0)


def halve_rows(t):
    above = up_y(t)
    near, far = t + above, dn_y(t) + up_y(above)
    return jnp.where(iota(t.shape, 1) < 64, near * 0.375 + far * 0.125, near)


def every_other(ref, first, count):
    return ref[pl.ds(first, count, stride=2)]


def twice(ref, first, value):
    count = value.shape[0]
    ref[pl.ds(first, count, stride=2)] = value
    ref[pl.ds(first + 1, count, stride=2)] = value


def halve(count, r_ref, m_ref, t_ref, u_ref, valid):
    for k in range(count):
        rows = slice(k * 32, k * 32 + 32)
        t_ref[rows, :128] = restrict_x(r_ref, 2 * k + 1) if 1 <= k < count - 1 else jnp.zeros((32, 128), F32)
        t_ref[rows, 128:] = (m_ref[2 * k + 2] + m_ref[2 * k + 3]) * (0.25 * 0.125)
    packed = dot(t_ref[...], halving(valid))
    for k in range(count):
        u_ref[k * 32 : k * 32 + 32] = halve_rows(packed[k * 32 : k * 32 + 32])
    return [every_other(u_ref, k * 32, 16) for k in range(count)]


def restrict_x(r_ref, j):
    return (r_ref[j] + r_ref[j + 3]) * 0.125 + (r_ref[j + 1] + r_ref[j + 2]) * 0.375


def edge(axis):
    i = lax.axis_index(axis)
    return i == 0, i == lax.axis_size(axis) - 1


def blank(flag, value, other):
    return jnp.where(flag, other, value)


X0 = 5
N0 = 32 + 2 * X0
N1 = 28
N2 = 28
N3 = 12
BIG = (N0, 40, 256)
VM = pl.BlockSpec(memory_space=pltpu.VMEM)


def call(kernel, name, out_shape, scratch, limit, *operands, aliases=None, in_specs=None, out_specs=None):
    return pl.pallas_call(
        kernel,
        in_specs=[VM] * len(operands) if in_specs is None else in_specs,
        out_specs=[VM] * len(out_shape) if out_specs is None else out_specs,
        out_shape=out_shape,
        scratch_shapes=scratch,
        input_output_aliases=aliases or {},
        compiler_params=pltpu.CompilerParams(vmem_limit_bytes=limit * MIB),
        name=name,
    )(*operands)


def kept(*shape):
    return pltpu.VMEM(shape, F32)


def send_rows_kernel(s_hbm, f_hbm, dn_ref, upw_ref, s_lo, s_hi, f_lo, f_hi, sems):
    parts = ((s_hbm, 0, s_lo), (f_hbm, 0, f_lo), (s_hbm, 24, s_hi), (f_hbm, 24, f_hi))
    copies = [
        pltpu.make_async_copy(ref.at[:, pl.ds(first, 8)], part, sems.at[k])
        for k, (ref, first, part) in enumerate(parts)
    ]
    for copy in copies:
        copy.start()
    for copy in copies:
        copy.wait()
    above = iota((8, 256), 0) < 4

    def work(j, n):
        here = pl.ds(j, n)
        dn_ref[here] = jnp.where(above, s_lo[here], pltpu.roll(f_lo[here].astype(F32), 4, 1))
        upw_ref[here] = jnp.where(above, pltpu.roll(f_hi[here].astype(F32), 4, 1), s_hi[here])

    blocks(0, 32, 8, work)


def send_rows(source, phase):
    part = (32, 8, 256)
    scratch = [kept(*part)] * 2 + [pltpu.VMEM(part, jnp.int32)] * 2 + [pltpu.SemaphoreType.DMA((4,))]
    hbm = [pl.BlockSpec(memory_space=pltpu.HBM)] * 2
    operands = [pltpu.with_memory_space_constraint(x, pltpu.HBM) for x in (source, phase)]
    return call(send_rows_kernel, "send_rows", [kept(*part)] * 2, scratch, 4, *operands, in_specs=hbm)


def halo_rows(lo, hi):
    low_y, high_y = edge("gy")
    above = iota((8, 256), 0) < 4
    outer = (above & high_y) | (~above & low_y)
    source = jnp.where(outer, 0.0, jnp.where(above, hi, lo))
    code = jnp.where(outer, OUT, pltpu.roll(jnp.where(above, lo, hi), 4, lo.ndim - 2))
    return source, code


def send_planes_kernel(s_in, f_in, ylo, yhi, dn_ref, upw_ref):
    for first, out_ref, skip in ((0, dn_ref, 0), (28, upw_ref, 1)):
        block = slice(first, first + 4)
        source, code = halo_rows(ylo[block], yhi[block])
        out_ref[:3, :32] = s_in[first + skip : first + skip + 3]
        out_ref[:3, 32:] = source[skip : skip + 3]
        out_ref[3:, :32] = f_in[block].astype(F32)
        out_ref[3:, 32:] = code


def water_to_mobility(n):
    return 0.25 * ((8.0 - n) * 0.125 + n * (0.125 * WATER))


def rows_to_16():
    fine_y = ring(iota((16, 40), 1), 36, 40)
    return fine_y - 2 * iota((16, 40), 0)


def lanes_to_128():
    return iota((256, 128), 0) - 2 * iota((256, 128), 1)


def inner0_kernel(
    s_in, f_in, ylo, yhi,
    s_ref, c_ref, wx, wy, wz, q_ref, p1, p2, r_ref, src1, mob1,
    t_ref,
):
    def own_planes(j, n):
        here, there = pl.ds(j, n), pl.ds(j + X0, n)
        source, code = halo_rows(ylo[here], yhi[here])
        s_ref[there, :32] = s_in[here]
        s_ref[there, 32:] = source
        c_ref[there, :32] = f_in[here].astype(F32)
        c_ref[there, 32:] = code

    blocks(0, 32, 4, own_planes)
    w = (wx, wy, wz, q_ref)
    weights_pass(6, 36, 6, c_ref, w, s_ref, p1, face_code, OUT, True)
    sweep(7, 35, 7, p1, p2, s_ref, w)
    remainder(8, 34, 6, p2, r_ref, s_ref, w)

    ry, rz = restrict_weight(rows_to_16()), restrict_weight(lanes_to_128())
    my, mz = pair_weight(rows_to_16()), pair_weight(lanes_to_128())
    for k in range(2, 14):
        t_ref[k * 16 : k * 16 + 16] = dot(ry, restrict_x(r_ref, 2 * k + 4))
    coarse = dot(t_ref[32:224], rz)
    for k in range(2, 14):
        src1[k] = coarse[k * 16 - 32 : k * 16 - 16]
    for k in range(16):
        t_ref[k * 16 : k * 16 + 16] = dot(my, c_ref[2 * k + X0] + c_ref[2 * k + X0 + 1])
    mobility = water_to_mobility(dot(t_ref[...], mz))
    for k in range(16):
        mob1[k] = mobility[k * 16 : k * 16 + 16]


def inner0(source, phase, ylo, yhi):
    return call(
        inner0_kernel, "inner0", [kept(*BIG)] * 9 + [kept(16, 16, 128)] * 2,
        [kept(256, 256)], 4, source, phase, ylo, yhi,
    )


def lay_rows(out, first, rows):
    for k in range(4):
        out[first + k] = rows[k // 2 * 16 : k // 2 * 16 + 16, k % 2 * 128 : k % 2 * 128 + 128]


def outer0_kernel(
    xlo, xhi, mob1, s_0, c_0, wx_0, wy_0, wz_0, q_0, p1_0, p2_0, r_0, src1_0,
    s_ref, c_ref, wx, wy, wz, q_ref, p1, p2, r_ref, src1, dn1, upw1, rows_dn, rows_up,
    t_ref,
):
    low_x, high_x = edge("gx")
    s_ref[2:5] = blank(low_x, xlo[:3], 0.0)
    c_ref[1:5] = blank(low_x, xlo[3:], OUT)
    s_ref[37:40] = blank(high_x, xhi[:3], 0.0)
    c_ref[37:41] = blank(high_x, xhi[3:], OUT)
    w = (wx, wy, wz, q_ref)
    for lo in (2, 36):
        weights_pass(lo, lo + 4, 4, c_ref, w, s_ref, p1, face_code, OUT, True)
    for lo in (3, 35):
        sweep(lo, lo + 4, 4, p1, p2, s_ref, w)
    for lo in (4, 34):
        remainder(lo, lo + 4, 4, p2, r_ref, s_ref, w)
    ry, rz = restrict_weight(rows_to_16()), restrict_weight(lanes_to_128())
    edges = (0, 1, 14, 15)
    for i, k in enumerate(edges):
        t_ref[i * 16 : i * 16 + 16] = dot(ry, restrict_x(r_ref, 2 * k + 4))
    coarse = dot(t_ref[...], rz)
    for i, k in enumerate(edges):
        src1[k] = coarse[i * 16 : i * 16 + 16]
    dn1[:5] = src1[:5]
    dn1[5:11] = mob1[:6]
    lay_rows(dn1, 11, p2[X0 + 2, :32])
    upw1[:5] = src1[11:]
    upw1[5:11] = mob1[10:]
    lay_rows(upw1, 11, p2[X0 + 29, :32])
    for k in range(32):
        rows_dn[k : k + 1] = p2[X0 + k, 2:3]
        rows_up[k : k + 1] = p2[X0 + k, 29:30]


def outer0(xlo, xhi, mob1, state):
    return call(
        outer0_kernel, "outer0",
        [kept(*BIG)] * 9 + [kept(16, 16, 128)] + [kept(15, 16, 128)] * 2 + [kept(32, 256)] * 2,
        [kept(64, 256)], 4, xlo, xhi, mob1, *state, aliases={3 + k: k for k in range(10)},
    )


def pack1_kernel(src, mob, xlo, xhi, rows_dn, rows_up, dn_ref, upw_ref):
    low_x, high_x = edge("gx")
    for rows, out, p_rows in ((slice(0, 8), dn_ref, rows_dn), (slice(8, 16), upw_ref, rows_up)):
        out[0, :8] = jnp.zeros((8, 128), F32)
        out[N1 - 1, :8] = jnp.zeros((8, 128), F32)
        out[1:6, :8] = blank(low_x, xlo[:5, rows], 0.0)
        out[0:6, 8:] = blank(low_x, xlo[5:11, rows], 0.0)
        out[6:22, :8] = src[:, rows]
        out[6:22, 8:] = mob[:, rows]
        out[22:27, :8] = blank(high_x, xhi[:5, rows], 0.0)
        out[22:28, 8:] = blank(high_x, xhi[5:11, rows], 0.0)
        lay_rows(out, N1, p_rows[...])


def pack1(*operands):
    return call(pack1_kernel, "pack1", [kept(N1 + 4, 16, 128)] * 2, [], 4, *operands)


def down1_kernel(
    src, mob, xlo, xhi, ylo, yhi,
    own2, dn2, upw2, s_ref, wx, wy, wz, q_ref, p2,
    m_ref, p1, r_ref, t_ref, u_ref, pk_ref,
):
    low_x, high_x = edge("gx")
    low_y, high_y = edge("gy")
    zero = jnp.zeros((32, 128), F32)
    s_ref[0] = zero
    s_ref[N1 - 1] = zero
    s_ref[1:6, :16] = blank(low_x, xlo[:5], 0.0)
    m_ref[0:6, :16] = blank(low_x, xlo[5:11], 0.0)
    s_ref[6:22, :16] = src[...]
    m_ref[6:22, :16] = mob[...]
    s_ref[22:27, :16] = blank(high_x, xhi[:5], 0.0)
    m_ref[22:28, :16] = blank(high_x, xhi[5:11], 0.0)
    s_ref[:, 16:24] = blank(high_y, yhi[:N1, :8], 0.0)
    m_ref[:, 16:24] = blank(high_y, yhi[:N1, 8:], 0.0)
    s_ref[:, 24:] = blank(low_y, ylo[:N1, :8], 0.0)
    m_ref[:, 24:] = blank(low_y, ylo[:N1, 8:], 0.0)
    w = (wx, wy, wz, q_ref)

    weights_pass(1, N1 - 1, 13, m_ref, w, s_ref, p1, face_mean, 0.0, True)
    sweep(2, N1 - 2, 12, p1, p2, s_ref, w)
    remainder(3, N1 - 3, 11, p2, r_ref, s_ref, w)

    for k, packed in enumerate(halve(12, r_ref, m_ref, t_ref, u_ref, 64)):
        pk_ref[k] = packed
    own2[...] = pk_ref[2:10]
    dn2[...] = pk_ref[2:12]
    upw2[...] = pk_ref[0:10]


def down1(*operands):
    return call(
        down1_kernel, "down1", [kept(k, 16, 128) for k in (8, 10, 10)] + [kept(N1, 32, 128)] * 6,
        [kept(N1, 32, 128)] * 3 + [kept(384, 256), kept(384, 128), kept(12, 16, 128)], 6, *operands,
    )


def pack2_kernel(own, xlo, xhi, dn_ref, upw_ref):
    low_x, high_x = edge("gx")
    row = iota((8, 128), 0)
    for a in range(N2 // 4):
        two_dn = two_up = jnp.zeros((8, 128), F32)
        for b in range(4):
            j = 4 * a + b
            if j < 10:
                plane = blank(low_x, xlo[j], 0.0)
            elif j < 18:
                plane = own[j - 10]
            else:
                plane = blank(high_x, xhi[j - 18], 0.0)
            dn_ref[j] = plane[:8]
            upw_ref[j] = plane[:8]
            here = (row == 2 * b) | (row == 2 * b + 1)
            two_dn = jnp.where(here, pltpu.roll(plane[8:], 2 * b, 0) if b else plane[8:], two_dn)
            two_up = jnp.where(here, pltpu.roll(plane[8:], 2 * b + 2, 0) if b < 3 else plane[8:], two_up)
        dn_ref[N2 + a] = two_dn
        upw_ref[N2 + a] = two_up


def pack2(*operands):
    return call(pack2_kernel, "pack2", [kept(N2 + N2 // 4, 8, 128)] * 2, [], 4, *operands)


def up_kernel(
    ext, ylo, yhi, s1, wx1, wy1, wz1, q1, down1_ref,
    wx0, wy0, wz0, q0, s0, down0_ref, plane_lo, plane_hi, rows_lo, rows_hi,
    scaled, residual,
    pa0, pb0,
    pa1, pb1,
    s2, m2, wx2, wy2, wz2, q2, pa2, pb2, r2,
    s3, m3, wx3, wy3, wz3, q3, pa3, pb3,
    t_ref, u_ref, v_ref, rise_lo, rise_hi, out_a, out_b, row_ref, sems,
):
    low_y, high_y = edge("gy")

    lane8, sub8 = iota((8, 128), 1), iota((8, 128), 0)

    def put(j, rows, packed):
        s2[j, rows] = packed
        m2[j, rows] = jnp.where(lane8 < 64, pltpu.roll(packed, 64, 1), 0.0)

    for j in range(N2):
        a, b = divmod(j, 4)
        hi, lo = yhi[N2 + a], ylo[N2 + a]
        hi = pltpu.roll(hi, 8 - 2 * b, 0) if b else hi
        lo = pltpu.roll(lo, 6 - 2 * b, 0) if b < 3 else lo
        put(j, slice(0, 8), ext[j])
        put(j, slice(8, 16), blank(high_y, yhi[j], 0.0))
        put(j, slice(16, 24), jnp.where((sub8 < 4) & ~high_y, hi, jnp.where((sub8 >= 4) & ~low_y, lo, 0.0)))
        put(j, slice(24, 32), blank(low_y, ylo[j], 0.0))

    w2 = (wx2, wy2, wz2, q2)

    weights_pass(1, N2 - 1, 13, m2, w2, s2, pa2, face_mean, 0.0, False)
    sweep(2, N2 - 2, 12, pa2, pb2, s2, w2)
    remainder(3, N2 - 3, 11, pb2, r2, s2, w2)

    lane16 = iota((16, 128), 1)
    for k, packed in enumerate(halve(12, r2, m2, t_ref, u_ref, 32)):
        s3[k] = packed
        m3[k] = jnp.where(lane16 < 64, pltpu.roll(packed, 64, 1), 0.0)
    w3 = (wx3, wy3, wz3, q3)

    weights_pass(1, N3 - 1, 10, m3, w3, s3, pa3, face_mean, 0.0, False)
    sweep(2, N3 - 2, 8, pa3, pb3, s3, w3)

    lane_in, lane_out = iota((128, 128), 0), iota((128, 128), 1)
    double = pair_weight(lane_out - 2 * lane_in)
    for k in range(8):
        v_ref[k * 16 : k * 16 + 16] = pb3[k + 2]
    rise = dot(v_ref[:128], jnp.where(lane_in < 32, double, 0.0))
    for k in range(8):
        twice(u_ref, k * 32, rise[k * 16 : k * 16 + 16])
    for k in range(8):
        for j in (2 * k + 6, 2 * k + 7):
            pb2[j] = pb2[j] + u_ref[k * 32 : k * 32 + 32]
    sweep(7, 21, 7, pb2, pa2, s2, w2)
    sweep(8, 20, 12, pa2, pb2, s2, w2)

    for k in range(12):
        v_ref[k * 16 : k * 16 + 8] = pb2[k + 8, :8]
        v_ref[k * 16 + 8 : k * 16 + 16] = jnp.where(sub8 < 4, pb2[k + 8, 8:16], pb2[k + 8, 24:])
    rise = dot(v_ref[:192], double)
    for k in range(12):
        twice(u_ref, k * 32, rise[k * 16 : k * 16 + 16])
    for k in range(12):
        for j in (2 * k + 2, 2 * k + 3):
            pa1[j] = down1_ref[j] + u_ref[k * 32 : k * 32 + 32]
    w1 = (wx1, wy1, wz1, q1)
    sweep(3, 25, 11, pa1, pb1, s1, w1)
    sweep(4, 24, 10, pb1, pa1, s1, w1)

    for k in range(20):
        v_ref[k * 24 : k * 24 + 16] = pa1[k + 4, :16]
        v_ref[k * 24 + 16 : k * 24 + 24] = jnp.where(
            sub8 < 2, pa1[k + 4, 16:24], pltpu.roll(pa1[k + 4, 24:], 4, 0)
        )
    for z, out in ((0, rise_lo), (128, rise_hi)):
        double = pair_weight(lane_out + z - 2 * lane_in)
        rise = dot(v_ref[...], double)
        for k in range(20):
            twice(out, k * 48, rise[k * 24 : k * 24 + 24])

    def rise_at(k):
        here = pl.ds(k * 48 if isinstance(k, int) else pl.multiple_of(k * 48, 8), 40)
        return jnp.concatenate([rise_lo[here], rise_hi[here]], 1)

    low_x, high_x = edge("gx")
    row8 = iota((8, 256), 0)

    def plane_of(message, first):
        tiles = [message[first + k] for k in range(4)]
        return jnp.concatenate(
            [jnp.concatenate(tiles[:2], 1), jnp.concatenate(tiles[2:], 1), jnp.zeros((8, 256), F32)], 0
        )

    pa0[2] = rise_at(0) + blank(low_x, plane_of(plane_lo, 11), 0.0)
    pa0[N0 - 3] = rise_at(19) + blank(high_x, plane_of(plane_hi, 11), 0.0)
    for k in range(4):
        h, z = k // 2 * 16, k % 2 * 128
        row_ref[0, h : h + 16, z : z + 128] = blank(high_y, rows_hi[N1 + k], 0.0)
        row_ref[1, h : h + 16, z : z + 128] = blank(low_y, rows_lo[N1 + k], 0.0)
    for j in (3, 4, 37, 38):
        pa0[j] = down0_ref[j] + rise_at((j - 1) // 2)

    def rise0(k, n):
        for i in range(n):
            rise = rise_at(k + i)
            for j in (2 * (k + i) + 1, 2 * (k + i) + 2):
                pa0[j, :32] = down0_ref[j, :32] + rise[:32]
                above = row_ref[0, pl.ds(j - X0, 1)]
                below = row_ref[1, pl.ds(j - X0, 1)]
                halo = jnp.where(row8 == 2, above, jnp.where(row8 == 5, below, down0_ref[j, 32:]))
                pa0[j, 32:] = halo + rise[32:]

    blocks(2, 18, 2, rise0)
    w0 = (wx0, wy0, wz0, q0)
    sweep(3, N0 - 3, 6, pa0, pb0, s0, w0)
    sweep(4, N0 - 4, 8, pb0, pa0, s0, w0)

    def out_copies(k, j):
        here = pl.ds(j, 8)
        return (
            pltpu.make_async_copy(out_a.at[here], scaled.at[here], sems.at[0, k]),
            pltpu.make_async_copy(out_b.at[here], residual.at[here], sems.at[1, k]),
        )

    def last(k, carry):
        j = k * 8
        results = []
        for i in range(8):
            p = pa0[j + i + X0]
            dp = (OMEGA / q0[j + i + X0]) * p
            results.append((dp[:32], (s0[j + i + X0] + flow(j + i + X0, p, pa0, w0) - dp)[:32]))
        for i, (a, b) in enumerate(results):
            out_a[j + i] = a
            out_b[j + i] = b
        for copy in out_copies(k, j):
            copy.start()
        return carry

    lax.fori_loop(0, 4, last, 0)
    for k in range(4):
        for copy in out_copies(k, k * 8):
            copy.wait()


def way_up(*operands):
    shape = jax.ShapeDtypeStruct((32, 32, 256), F32)
    buf = lambda count, *shape: [kept(*shape)] * count
    scratch = (
        buf(2, *BIG)
        + buf(2, N1, 32, 128)
        + buf(9, N2, 32, 128)
        + buf(8, N3, 16, 128)
        + buf(1, 384, 256)
        + buf(1, 384, 128)
        + buf(1, 480, 128)
        + buf(2, 960, 128)
        + buf(2, 32, 32, 256)
        + buf(1, 2, 32, 256)
        + [pltpu.SemaphoreType.DMA((2, 4))]
    )
    hbm = pl.BlockSpec(memory_space=pl.ANY)
    return call(up_kernel, "way_up", [shape] * 2, scratch, 20, *operands, out_specs=[hbm] * 2)


def shift(a, axis, step):
    count = lax.axis_size(axis)
    return lax.ppermute(a, axis, [(i, (i + step) % count) for i in range(count)])


def both(to_low, to_high, axis):
    return shift(to_high, axis, 1), shift(to_low, axis, -1)


def shards(source, phase):
    ylo, yhi = both(*send_rows(source, phase), "gy")
    msg = [kept(7, 40, 256)] * 2
    dn0, up0 = call(send_planes_kernel, "send_planes", msg, [], 4, source, phase, ylo, yhi)
    xlo, xhi = both(dn0, up0, "gx")
    *state, mob1 = inner0(source, phase, ylo, yhi)
    s0, _, wx0, wy0, wz0, q0, _, p0, _, src1, dn1, up1, rows_dn, rows_up = outer0(xlo, xhi, mob1, state)
    xlo1, xhi1 = both(dn1, up1, "gx")
    ylo1, yhi1 = both(*pack1(src1, mob1, xlo1, xhi1, rows_dn, rows_up), "gy")
    own2, dn2, up2, *level1 = down1(src1, mob1, xlo1, xhi1, ylo1, yhi1)
    xlo, xhi = both(dn2, up2, "gx")
    ext, ext_up = pack2(own2, xlo, xhi)
    ylo, yhi = both(ext, ext_up, "gy")
    level0 = (wx0, wy0, wz0, q0, s0, p0, xlo1, xhi1, ylo1, yhi1)
    return tuple(way_up(ext, ylo, yhi, *level1, *level0))


def solution(mesh):
    spec = P("gx", "gy", None)
    return jax.shard_map(shards, mesh=mesh, in_specs=(spec, spec), out_specs=(spec, spec), check_vma=False)
```

```python
import jax
import jax.numpy as jnp
from jax import lax
from jax.experimental import pallas as pl
from jax.experimental.pallas import tpu as pltpu
from jax.sharding import PartitionSpec as P

OMEGA = 0.8
KEEP = 0.2
WATER = 0.001
MIXED = 2.0 * WATER / (1.0 + WATER)
OUT = 0.25
F32 = jnp.float32
MIB = 1024 * 1024


def up_y(a):
    return pltpu.roll(a, a.shape[-2] - 1, a.ndim - 2)


def dn_y(a):
    return pltpu.roll(a, 1, a.ndim - 2)


def up_z(a):
    return pltpu.roll(a, a.shape[-1] - 1, a.ndim - 1)


def dn_z(a):
    return pltpu.roll(a, 1, a.ndim - 1)


def iota(shape, dim):
    return lax.broadcasted_iota(jnp.int32, shape, dim)


def ring(row, cut, rows):
    return jnp.where(row < cut, row, row - rows)


def restrict_weight(offset):
    near = (offset == 0) | (offset == 1)
    far = (offset == -1) | (offset == 2)
    return jnp.where(near, 0.375, jnp.where(far, 0.125, 0.0)).astype(F32)


def pair_weight(offset):
    return jnp.where((offset == 0) | (offset == 1), 1.0, 0.0).astype(F32)


def dot(a, b, exact=False):
    high, b = a.astype(jnp.bfloat16), b.astype(jnp.bfloat16)
    if exact:
        return jnp.dot(high, b, preferred_element_type=F32)
    low = (a - high.astype(F32)).astype(jnp.bfloat16)
    if a.shape[1] == 128:
        both = jnp.concatenate([high, low], 1)
        return jnp.dot(both, jnp.concatenate([b, b], 0), preferred_element_type=F32)
    return jnp.dot(high, b, preferred_element_type=F32) + jnp.dot(low, b, preferred_element_type=F32)


def full_dot(a, b):
    return jnp.dot(a, b, precision=lax.Precision.HIGHEST, preferred_element_type=F32)


def face_code(a, b):
    s = a + b
    return jnp.where(s < 0.75, 1.0, jnp.where(s < 1.1, MIXED, WATER)).astype(F32)


def face_mean(a, b):
    product = a * b
    return jnp.where(product > 0.0, 2.0 * product / (a + b), jnp.maximum(a, b))


def blocks(lo, hi, size, work):
    count, rest = divmod(hi - lo, size)
    if count == 1:
        work(lo, size)
    elif count:

        def body(i, carry):
            work(lo + i * size, size)
            return carry

        lax.fori_loop(0, count, body, 0)
    if rest:
        work(hi - rest, rest)


def planes(lo, hi, size, plane, refs):
    def work(j, n):
        results = [plane(j + i) for i in range(n)]
        for i, values in enumerate(results):
            for ref, value in zip(refs, values):
                ref[j + i] = value

    blocks(lo, hi, size, work)


def planes_at(js, plane, refs):
    results = [plane(j) for j in js]
    for j, values in zip(js, results):
        for ref, value in zip(refs, values):
            ref[j] = value


def weights_at(m_low, m, m_high, face, outside, full):
    lane = iota(m.shape, m.ndim - 1)
    last = m.shape[-1] - 1
    wx, wx_low = face(m, m_high), face(m_low, m)
    wy = face(m, up_y(m))
    m_up = up_z(m)
    if full:
        m_up = jnp.where(lane == last, outside, m_up)
    wz = face(m, m_up)
    wz_low = dn_z(wz)
    if full:
        wz_low = jnp.where(lane == 0, face(m, jnp.full_like(m, outside)), wz_low)
    d = (wx + wx_low) + (wy + dn_y(wy)) + (wz + wz_low)
    q = jnp.where(m != outside, OMEGA / d, 0.0)
    if full:
        wz = jnp.where(lane == last, 0.0, wz)
    return wx, wy, wz, q


def weights_plane(m_ref, s_ref, face, outside, full):
    def plane(j):
        wx, wy, wz, q = weights_at(m_ref[j - 1], m_ref[j], m_ref[j + 1], face, outside, full)
        return wx, wy, wz, q, q * s_ref[j]

    return plane


def weights_pass(lo, hi, size, m_ref, w, s_ref, p_ref, face, outside, full):
    w[0][lo - 1] = face(m_ref[lo - 1], m_ref[lo])
    planes(lo, hi, size, weights_plane(m_ref, s_ref, face, outside, full), (*w, p_ref))


def flow(j, p, p_ref, w):
    wx_ref, wy_ref, wz_ref = w[:3]
    wy, wz = wy_ref[j], wz_ref[j]
    along_x = wx_ref[j] * p_ref[j + 1] + wx_ref[j - 1] * p_ref[j - 1]
    along_y = wy * up_y(p) + dn_y(wy * p)
    along_z = wz * up_z(p) + dn_z(wz * p)
    return along_x + along_y + along_z


def sweep_plane(p_ref, s_ref, w):
    def plane(j):
        p = p_ref[j]
        return (KEEP * p + w[3][j] * (s_ref[j] + flow(j, p, p_ref, w)),)

    return plane


def sweep(lo, hi, size, p_ref, out_ref, s_ref, w):
    planes(lo, hi, size, sweep_plane(p_ref, s_ref, w), (out_ref,))


def remainder_plane(p_ref, s_ref, w):
    def plane(j):
        p, q = p_ref[j], w[3][j]
        r = s_ref[j] + flow(j, p, p_ref, w) - (OMEGA / q) * p
        return (jnp.where(q > 0.0, r, 0.0),)

    return plane


def remainder(lo, hi, size, p_ref, out_ref, s_ref, w):
    planes(lo, hi, size, remainder_plane(p_ref, s_ref, w), (out_ref,))


def halving(valid):
    lane_in, lane_out = iota((256, 128), 0), iota((256, 128), 1)
    down = jnp.where((lane_in < 128) & (lane_out < valid), restrict_weight(lane_in - 2 * lane_out), 0.0)
    return down + jnp.where(lane_in >= 128, pair_weight(lane_in - 2 * lane_out), 0.0)


def halve_rows(t):
    above = up_y(t)
    near, far = t + above, dn_y(t) + up_y(above)
    return jnp.where(iota(t.shape, 1) < 64, near * 0.375 + far * 0.125, near)


def every_other(ref, first, count):
    return ref[pl.ds(first, count, stride=2)]


def twice(ref, first, value):
    count = value.shape[0]
    ref[pl.ds(first, count, stride=2)] = value
    ref[pl.ds(first + 1, count, stride=2)] = value


def halve(count, r_ref, m_ref, t_ref, u_ref, valid, product):
    for k in range(count):
        rows = slice(k * 32, k * 32 + 32)
        t_ref[rows, :128] = restrict_x(r_ref, 2 * k + 1) if 1 <= k < count - 1 else jnp.zeros((32, 128), F32)
        t_ref[rows, 128:] = (m_ref[2 * k + 2] + m_ref[2 * k + 3]) * (0.25 * 0.125)
    packed = product(t_ref[...], halving(valid))
    for k in range(count):
        u_ref[k * 32 : k * 32 + 32] = halve_rows(packed[k * 32 : k * 32 + 32])
    return [every_other(u_ref, k * 32, 16) for k in range(count)]


def restrict_x(r_ref, j):
    return (r_ref[j] + r_ref[j + 3]) * 0.125 + (r_ref[j + 1] + r_ref[j + 2]) * 0.375


def edge(axis):
    i = lax.axis_index(axis)
    return i == 0, i == lax.axis_size(axis) - 1


def blank(flag, value, other):
    return jnp.where(flag, other, value)


X0 = 5
N0 = 32 + 2 * X0
N1 = 28
N2 = 28
N3 = 12
BIG = (N0, 40, 256)
VM = pl.BlockSpec(memory_space=pltpu.VMEM)


def call(kernel, name, out_shape, scratch, limit, *operands, aliases=None, in_specs=None, out_specs=None):
    return pl.pallas_call(
        kernel,
        in_specs=[VM] * len(operands) if in_specs is None else in_specs,
        out_specs=[VM] * len(out_shape) if out_specs is None else out_specs,
        out_shape=out_shape,
        scratch_shapes=scratch,
        input_output_aliases=aliases or {},
        compiler_params=pltpu.CompilerParams(vmem_limit_bytes=limit * MIB),
        name=name,
    )(*operands)


def kept(*shape):
    return pltpu.VMEM(shape, F32)


def send_rows_kernel(s_hbm, f_hbm, dn_ref, upw_ref, s_lo, s_hi, f_lo, f_hi, sems):
    parts = ((s_hbm, 0, s_lo), (f_hbm, 0, f_lo), (s_hbm, 24, s_hi), (f_hbm, 24, f_hi))
    copies = [
        pltpu.make_async_copy(ref.at[:, pl.ds(first, 8)], part, sems.at[k])
        for k, (ref, first, part) in enumerate(parts)
    ]
    for copy in copies:
        copy.start()
    for copy in copies:
        copy.wait()
    above = iota((8, 256), 0) < 4

    def work(j, n):
        here = pl.ds(j, n)
        dn_ref[here] = jnp.where(above, s_lo[here], pltpu.roll(f_lo[here].astype(F32), 4, 1))
        upw_ref[here] = jnp.where(above, pltpu.roll(f_hi[here].astype(F32), 4, 1), s_hi[here])

    blocks(0, 32, 8, work)


def send_rows(source, phase):
    part = (32, 8, 256)
    scratch = [kept(*part)] * 2 + [pltpu.VMEM(part, jnp.int32)] * 2 + [pltpu.SemaphoreType.DMA((4,))]
    hbm = [pl.BlockSpec(memory_space=pltpu.HBM)] * 2
    operands = [pltpu.with_memory_space_constraint(x, pltpu.HBM) for x in (source, phase)]
    return call(send_rows_kernel, "send_rows", [kept(*part)] * 2, scratch, 4, *operands, in_specs=hbm)


def load_kernel(s_hbm, f_hbm, sent, s_ref, f_ref, sems):
    del sent
    copies = [
        pltpu.make_async_copy(a, b, sems.at[k]) for k, (a, b) in enumerate(((s_hbm, s_ref), (f_hbm, f_ref)))
    ]
    for copy in copies:
        copy.start()
    for copy in copies:
        copy.wait()


def load(source, phase, sent):
    any_space = pl.BlockSpec(memory_space=pl.ANY)
    hbm = [pl.BlockSpec(memory_space=pltpu.HBM)] * 2
    operands = [pltpu.with_memory_space_constraint(x, pltpu.HBM) for x in (source, phase)]
    out = [kept(32, 32, 256), pltpu.VMEM((32, 32, 256), jnp.int32)]
    scratch = [pltpu.SemaphoreType.DMA((2,))]
    return call(load_kernel, "load", out, scratch, 4, *operands, sent, in_specs=[*hbm, any_space])


def halo_rows(lo, hi):
    low_y, high_y = edge("gy")
    above = iota((8, 256), 0) < 4
    outer = (above & high_y) | (~above & low_y)
    source = jnp.where(outer, 0.0, jnp.where(above, hi, lo))
    code = jnp.where(outer, OUT, pltpu.roll(jnp.where(above, lo, hi), 4, lo.ndim - 2))
    return source, code


def send_planes_kernel(s_in, f_in, ylo, yhi, dn_ref, upw_ref):
    for first, out_ref, skip in ((0, dn_ref, 0), (28, upw_ref, 1)):
        block = slice(first, first + 4)
        source, code = halo_rows(ylo[block], yhi[block])
        out_ref[:3, :32] = s_in[first + skip : first + skip + 3]
        out_ref[:3, 32:] = source[skip : skip + 3]
        out_ref[3:, :32] = f_in[block].astype(F32)
        out_ref[3:, 32:] = code


def water_to_mobility(n):
    return 0.25 * ((8.0 - n) * 0.125 + n * (0.125 * WATER))


def lanes_to_128():
    return iota((256, 128), 0) - 2 * iota((256, 128), 1)


def halve0(ks, r_ref, src1, t_ref, u_ref):
    for i, k in enumerate(ks):
        t_ref[i * 40 : i * 40 + 40] = restrict_x(r_ref, 2 * k + 4)
    coarse = dot(t_ref[: len(ks) * 40], restrict_weight(lanes_to_128()))
    for i in range(len(ks)):
        t = coarse[i * 40 : i * 40 + 40]
        above = up_y(t)
        u_ref[i * 40 : i * 40 + 40] = (t + above) * 0.375 + (dn_y(t) + up_y(above)) * 0.125
    for i, k in enumerate(ks):
        src1[k] = every_other(u_ref, i * 40, 16)


def inner0_kernel(
    s_in, f_in, ylo, yhi,
    s_ref, c_ref, wx, wy, wz, q_ref, p1, p2, r_ref, src1, mob1,
    t_ref, u_ref,
):
    def own_planes(j, n):
        here, there = pl.ds(j, n), pl.ds(j + X0, n)
        source, code = halo_rows(ylo[here], yhi[here])
        s_ref[there, :32] = s_in[here]
        s_ref[there, 32:] = source
        c_ref[there, :32] = f_in[here].astype(F32)
        c_ref[there, 32:] = code

    blocks(0, 32, 4, own_planes)
    w = (wx, wy, wz, q_ref)
    weights_pass(6, 36, 10, c_ref, w, s_ref, p1, face_code, OUT, True)
    sweep(7, 35, 14, p1, p2, s_ref, w)
    remainder(8, 34, 13, p2, r_ref, s_ref, w)

    halve0(range(2, 14), r_ref, src1, t_ref, u_ref)
    for k in range(16):
        t_ref[k * 40 : k * 40 + 40] = c_ref[2 * k + X0] + c_ref[2 * k + X0 + 1]
    water = dot(t_ref[...], pair_weight(lanes_to_128()), exact=True)
    for k in range(16):
        t = water[k * 40 : k * 40 + 40]
        u_ref[k * 40 : k * 40 + 40] = t + up_y(t)
    for k in range(16):
        mob1[k] = water_to_mobility(every_other(u_ref, k * 40, 16))


def inner0(source, phase, ylo, yhi):
    return call(
        inner0_kernel, "inner0", [kept(*BIG)] * 9 + [kept(16, 16, 128)] * 2,
        [kept(640, 256), kept(640, 128)], 4, source, phase, ylo, yhi,
    )


def lay_rows(out, first, rows):
    for k in range(4):
        out[first + k] = rows[k // 2 * 16 : k // 2 * 16 + 16, k % 2 * 128 : k % 2 * 128 + 128]


def outer0_kernel(
    xlo, xhi, mob1, s_0, c_0, wx_0, wy_0, wz_0, q_0, p1_0, p2_0, r_0, src1_0,
    s_ref, c_ref, wx, wy, wz, q_ref, p1, p2, r_ref, src1, dn1, upw1, rows_dn, rows_up,
    t_ref, u_ref,
):
    low_x, high_x = edge("gx")
    s_ref[2:5] = blank(low_x, xlo[:3], 0.0)
    c_ref[1:5] = blank(low_x, xlo[3:], OUT)
    s_ref[37:40] = blank(high_x, xhi[:3], 0.0)
    c_ref[37:41] = blank(high_x, xhi[3:], OUT)
    w = (wx, wy, wz, q_ref)
    wx[1] = face_code(c_ref[1], c_ref[2])
    wx[35] = face_code(c_ref[35], c_ref[36])
    planes_at((2, 3, 4, 5, 36, 37, 38, 39), weights_plane(c_ref, s_ref, face_code, OUT, True), (*w, p1))
    planes_at((3, 4, 5, 6, 35, 36, 37, 38), sweep_plane(p1, s_ref, w), (p2,))
    planes_at((4, 5, 6, 7, 34, 35, 36, 37), remainder_plane(p2, s_ref, w), (r_ref,))
    halve0((0, 1, 14, 15), r_ref, src1, t_ref, u_ref)
    dn1[:5] = src1[:5]
    dn1[5:11] = mob1[:6]
    lay_rows(dn1, 11, p2[X0 + 2, :32])
    upw1[:5] = src1[11:]
    upw1[5:11] = mob1[10:]
    lay_rows(upw1, 11, p2[X0 + 29, :32])
    for k in range(32):
        rows_dn[k : k + 1] = p2[X0 + k, 2:3]
        rows_up[k : k + 1] = p2[X0 + k, 29:30]


def outer0(xlo, xhi, mob1, state):
    return call(
        outer0_kernel, "outer0",
        [kept(*BIG)] * 9 + [kept(16, 16, 128)] + [kept(15, 16, 128)] * 2 + [kept(32, 256)] * 2,
        [kept(160, 256), kept(160, 128)], 4, xlo, xhi, mob1, *state, aliases={3 + k: k for k in range(10)},
    )


def pack1_kernel(src, mob, xlo, xhi, rows_dn, rows_up, dn_ref, upw_ref):
    low_x, high_x = edge("gx")
    for rows, out, p_rows in ((slice(0, 8), dn_ref, rows_dn), (slice(8, 16), upw_ref, rows_up)):
        out[0, :8] = jnp.zeros((8, 128), F32)
        out[N1 - 1, :8] = jnp.zeros((8, 128), F32)
        out[1:6, :8] = blank(low_x, xlo[:5, rows], 0.0)
        out[0:6, 8:] = blank(low_x, xlo[5:11, rows], 0.0)
        out[6:22, :8] = src[:, rows]
        out[6:22, 8:] = mob[:, rows]
        out[22:27, :8] = blank(high_x, xhi[:5, rows], 0.0)
        out[22:28, 8:] = blank(high_x, xhi[5:11, rows], 0.0)
        lay_rows(out, N1, p_rows[...])


def pack1(*operands):
    return call(pack1_kernel, "pack1", [kept(N1 + 4, 16, 128)] * 2, [], 4, *operands)


def down1_kernel(
    src, mob, xlo, xhi, ylo, yhi,
    own2, dn2, upw2, s_ref, wx, wy, wz, q_ref, p2,
    m_ref, p1, r_ref, t_ref, u_ref, pk_ref,
):
    low_x, high_x = edge("gx")
    low_y, high_y = edge("gy")
    zero = jnp.zeros((32, 128), F32)
    s_ref[0] = zero
    s_ref[N1 - 1] = zero
    s_ref[1:6, :16] = blank(low_x, xlo[:5], 0.0)
    m_ref[0:6, :16] = blank(low_x, xlo[5:11], 0.0)
    s_ref[6:22, :16] = src[...]
    m_ref[6:22, :16] = mob[...]
    s_ref[22:27, :16] = blank(high_x, xhi[:5], 0.0)
    m_ref[22:28, :16] = blank(high_x, xhi[5:11], 0.0)
    s_ref[:, 16:24] = blank(high_y, yhi[:N1, :8], 0.0)
    m_ref[:, 16:24] = blank(high_y, yhi[:N1, 8:], 0.0)
    s_ref[:, 24:] = blank(low_y, ylo[:N1, :8], 0.0)
    m_ref[:, 24:] = blank(low_y, ylo[:N1, 8:], 0.0)
    w = (wx, wy, wz, q_ref)

    weights_pass(1, N1 - 1, 26, m_ref, w, s_ref, p1, face_mean, 0.0, True)
    sweep(2, N1 - 2, 24, p1, p2, s_ref, w)
    remainder(3, N1 - 3, 22, p2, r_ref, s_ref, w)

    for k, packed in enumerate(halve(12, r_ref, m_ref, t_ref, u_ref, 64, full_dot)):
        pk_ref[k] = packed
    own2[...] = pk_ref[2:10]
    dn2[...] = pk_ref[2:12]
    upw2[...] = pk_ref[0:10]


def down1(*operands):
    return call(
        down1_kernel, "down1", [kept(k, 16, 128) for k in (8, 10, 10)] + [kept(N1, 32, 128)] * 6,
        [kept(N1, 32, 128)] * 3 + [kept(384, 256), kept(384, 128), kept(12, 16, 128)], 6, *operands,
    )


def pack2_kernel(own, xlo, xhi, dn_ref, upw_ref):
    low_x, high_x = edge("gx")
    row = iota((8, 128), 0)
    for a in range(N2 // 4):
        two_dn = two_up = jnp.zeros((8, 128), F32)
        for b in range(4):
            j = 4 * a + b
            if j < 10:
                plane = blank(low_x, xlo[j], 0.0)
            elif j < 18:
                plane = own[j - 10]
            else:
                plane = blank(high_x, xhi[j - 18], 0.0)
            dn_ref[j] = plane[:8]
            upw_ref[j] = plane[:8]
            here = (row == 2 * b) | (row == 2 * b + 1)
            two_dn = jnp.where(here, pltpu.roll(plane[8:], 2 * b, 0) if b else plane[8:], two_dn)
            two_up = jnp.where(here, pltpu.roll(plane[8:], 2 * b + 2, 0) if b < 3 else plane[8:], two_up)
        dn_ref[N2 + a] = two_dn
        upw_ref[N2 + a] = two_up


def pack2(*operands):
    return call(pack2_kernel, "pack2", [kept(N2 + N2 // 4, 8, 128)] * 2, [], 4, *operands)


def up_kernel(
    ext, ylo, yhi, s1, wx1, wy1, wz1, q1, down1_ref,
    wx0, wy0, wz0, q0, s0, down0_ref, plane_lo, plane_hi, rows_lo, rows_hi,
    scaled, residual,
    pa0, pb0,
    pa1, pb1,
    s2, m2, wx2, wy2, wz2, q2, pa2, pb2, r2,
    s3, m3, wx3, wy3, wz3, q3, pa3, pb3,
    t_ref, u_ref, v_ref, rise_lo, rise_hi, out_a, out_b, row_ref, sems,
):
    low_y, high_y = edge("gy")

    lane8, sub8 = iota((8, 128), 1), iota((8, 128), 0)

    def put(j, rows, packed):
        s2[j, rows] = packed
        m2[j, rows] = jnp.where(lane8 < 64, pltpu.roll(packed, 64, 1), 0.0)

    for j in range(N2):
        a, b = divmod(j, 4)
        hi, lo = yhi[N2 + a], ylo[N2 + a]
        hi = pltpu.roll(hi, 8 - 2 * b, 0) if b else hi
        lo = pltpu.roll(lo, 6 - 2 * b, 0) if b < 3 else lo
        put(j, slice(0, 8), ext[j])
        put(j, slice(8, 16), blank(high_y, yhi[j], 0.0))
        put(j, slice(16, 24), jnp.where((sub8 < 4) & ~high_y, hi, jnp.where((sub8 >= 4) & ~low_y, lo, 0.0)))
        put(j, slice(24, 32), blank(low_y, ylo[j], 0.0))

    w2 = (wx2, wy2, wz2, q2)

    weights_pass(1, N2 - 1, 26, m2, w2, s2, pa2, face_mean, 0.0, False)
    sweep(2, N2 - 2, 24, pa2, pb2, s2, w2)
    remainder(3, N2 - 3, 22, pb2, r2, s2, w2)

    lane16 = iota((16, 128), 1)
    for k, packed in enumerate(halve(12, r2, m2, t_ref, u_ref, 32, dot)):
        s3[k] = packed
        m3[k] = jnp.where(lane16 < 64, pltpu.roll(packed, 64, 1), 0.0)
    w3 = (wx3, wy3, wz3, q3)

    weights_pass(1, N3 - 1, 10, m3, w3, s3, pa3, face_mean, 0.0, False)
    sweep(2, N3 - 2, 8, pa3, pb3, s3, w3)

    lane_in, lane_out = iota((128, 128), 0), iota((128, 128), 1)
    double = pair_weight(lane_out - 2 * lane_in)
    for k in range(8):
        v_ref[k * 16 : k * 16 + 16] = pb3[k + 2]
    rise = dot(v_ref[:128], jnp.where(lane_in < 32, double, 0.0))
    for k in range(8):
        twice(u_ref, k * 32, rise[k * 16 : k * 16 + 16])
    for k in range(8):
        for j in (2 * k + 6, 2 * k + 7):
            pb2[j] = pb2[j] + u_ref[k * 32 : k * 32 + 32]
    sweep(7, 21, 14, pb2, pa2, s2, w2)
    sweep(8, 20, 12, pa2, pb2, s2, w2)

    for k in range(12):
        v_ref[k * 16 : k * 16 + 8] = pb2[k + 8, :8]
        v_ref[k * 16 + 8 : k * 16 + 16] = jnp.where(sub8 < 4, pb2[k + 8, 8:16], pb2[k + 8, 24:])
    rise = dot(v_ref[:192], double)
    for k in range(12):
        twice(u_ref, k * 32, rise[k * 16 : k * 16 + 16])
    for k in range(12):
        for j in (2 * k + 2, 2 * k + 3):
            pa1[j] = down1_ref[j] + u_ref[k * 32 : k * 32 + 32]
    w1 = (wx1, wy1, wz1, q1)
    sweep(3, 25, 22, pa1, pb1, s1, w1)
    sweep(4, 24, 20, pb1, pa1, s1, w1)

    for k in range(20):
        v_ref[k * 24 : k * 24 + 16] = pa1[k + 4, :16]
        v_ref[k * 24 + 16 : k * 24 + 24] = jnp.where(
            sub8 < 2, pa1[k + 4, 16:24], pltpu.roll(pa1[k + 4, 24:], 4, 0)
        )
    for z, out in ((0, rise_lo), (128, rise_hi)):
        double = pair_weight(lane_out + z - 2 * lane_in)
        rise = dot(v_ref[...], double)
        for k in range(20):
            twice(out, k * 48, rise[k * 24 : k * 24 + 24])

    def rise_at(k):
        here = pl.ds(k * 48 if isinstance(k, int) else pl.multiple_of(k * 48, 8), 40)
        return jnp.concatenate([rise_lo[here], rise_hi[here]], 1)

    low_x, high_x = edge("gx")
    row8 = iota((8, 256), 0)

    def plane_of(message, first):
        tiles = [message[first + k] for k in range(4)]
        return jnp.concatenate(
            [jnp.concatenate(tiles[:2], 1), jnp.concatenate(tiles[2:], 1), jnp.zeros((8, 256), F32)], 0
        )

    pa0[2] = rise_at(0) + blank(low_x, plane_of(plane_lo, 11), 0.0)
    pa0[N0 - 3] = rise_at(19) + blank(high_x, plane_of(plane_hi, 11), 0.0)
    for k in range(4):
        h, z = k // 2 * 16, k % 2 * 128
        row_ref[0, h : h + 16, z : z + 128] = blank(high_y, rows_hi[N1 + k], 0.0)
        row_ref[1, h : h + 16, z : z + 128] = blank(low_y, rows_lo[N1 + k], 0.0)
    for j in (3, 4, 37, 38):
        pa0[j] = down0_ref[j] + rise_at((j - 1) // 2)

    def rise0(k, n):
        for i in range(n):
            rise = rise_at(k + i)
            for j in (2 * (k + i) + 1, 2 * (k + i) + 2):
                pa0[j, :32] = down0_ref[j, :32] + rise[:32]
                above = row_ref[0, pl.ds(j - X0, 1)]
                below = row_ref[1, pl.ds(j - X0, 1)]
                halo = jnp.where(row8 == 2, above, jnp.where(row8 == 5, below, down0_ref[j, 32:]))
                pa0[j, 32:] = halo + rise[32:]

    blocks(2, 18, 2, rise0)
    w0 = (wx0, wy0, wz0, q0)
    sweep(3, N0 - 3, 12, pa0, pb0, s0, w0)
    sweep(4, N0 - 4, 17, pb0, pa0, s0, w0)

    def out_copies(k, j):
        here = pl.ds(j, 8)
        return (
            pltpu.make_async_copy(out_a.at[here], scaled.at[here], sems.at[0, k]),
            pltpu.make_async_copy(out_b.at[here], residual.at[here], sems.at[1, k]),
        )

    def last(k, carry):
        j = k * 8
        results = []
        for i in range(8):
            p = pa0[j + i + X0]
            dp = (OMEGA / q0[j + i + X0]) * p
            results.append((dp[:32], (s0[j + i + X0] + flow(j + i + X0, p, pa0, w0) - dp)[:32]))
        for i, (a, b) in enumerate(results):
            out_a[j + i] = a
            out_b[j + i] = b
        for copy in out_copies(k, j):
            copy.start()
        return carry

    lax.fori_loop(0, 4, last, 0)
    for k in range(4):
        for copy in out_copies(k, k * 8):
            copy.wait()


def way_up(*operands):
    shape = jax.ShapeDtypeStruct((32, 32, 256), F32)
    buf = lambda count, *shape: [kept(*shape)] * count
    scratch = (
        buf(2, *BIG)
        + buf(2, N1, 32, 128)
        + buf(9, N2, 32, 128)
        + buf(8, N3, 16, 128)
        + buf(1, 384, 256)
        + buf(1, 384, 128)
        + buf(1, 480, 128)
        + buf(2, 960, 128)
        + buf(2, 32, 32, 256)
        + buf(1, 2, 32, 256)
        + [pltpu.SemaphoreType.DMA((2, 4))]
    )
    hbm = pl.BlockSpec(memory_space=pl.ANY)
    return call(up_kernel, "way_up", [shape] * 2, scratch, 20, *operands, out_specs=[hbm] * 2)


def shift(a, axis, step):
    count = lax.axis_size(axis)
    return lax.ppermute(a, axis, [(i, (i + step) % count) for i in range(count)])


def both(to_low, to_high, axis):
    return shift(to_high, axis, 1), shift(to_low, axis, -1)


def shards(source, phase):
    dn0, up0 = send_rows(source, phase)
    ylo, yhi = both(dn0, up0, "gy")
    source, phase = load(source, phase, dn0)
    msg = [kept(7, 40, 256)] * 2
    dn0, up0 = call(send_planes_kernel, "send_planes", msg, [], 4, source, phase, ylo, yhi)
    xlo, xhi = both(dn0, up0, "gx")
    *state, mob1 = inner0(source, phase, ylo, yhi)
    s0, _, wx0, wy0, wz0, q0, _, p0, _, src1, dn1, up1, rows_dn, rows_up = outer0(xlo, xhi, mob1, state)
    xlo1, xhi1 = both(dn1, up1, "gx")
    ylo1, yhi1 = both(*pack1(src1, mob1, xlo1, xhi1, rows_dn, rows_up), "gy")
    own2, dn2, up2, *level1 = down1(src1, mob1, xlo1, xhi1, ylo1, yhi1)
    xlo, xhi = both(dn2, up2, "gx")
    ext, ext_up = pack2(own2, xlo, xhi)
    ylo, yhi = both(ext, ext_up, "gy")
    level0 = (wx0, wy0, wz0, q0, s0, p0, xlo1, xhi1, ylo1, yhi1)
    return tuple(way_up(ext, ylo, yhi, *level1, *level0))


def solution(mesh):
    spec = P("gx", "gy", None)
    return jax.shard_map(shards, mesh=mesh, in_specs=(spec, spec), out_specs=(spec, spec), check_vma=False)
```

```python
import jax
import jax.numpy as jnp
from jax import lax
from jax.experimental import pallas as pl
from jax.experimental.pallas import tpu as pltpu
from jax.sharding import PartitionSpec as P

OMEGA = 0.8
KEEP = 0.2
WATER = 0.001
MIXED = 2.0 * WATER / (1.0 + WATER)
OUT = 0.25
F32 = jnp.float32
MIB = 1024 * 1024


def up_y(a):
    return pltpu.roll(a, a.shape[-2] - 1, a.ndim - 2)


def dn_y(a):
    return pltpu.roll(a, 1, a.ndim - 2)


def up_z(a):
    return pltpu.roll(a, a.shape[-1] - 1, a.ndim - 1)


def dn_z(a):
    return pltpu.roll(a, 1, a.ndim - 1)


def iota(shape, dim):
    return lax.broadcasted_iota(jnp.int32, shape, dim)


def ring(row, cut, rows):
    return jnp.where(row < cut, row, row - rows)


def restrict_weight(offset):
    near = (offset == 0) | (offset == 1)
    far = (offset == -1) | (offset == 2)
    return jnp.where(near, 0.375, jnp.where(far, 0.125, 0.0)).astype(F32)


def pair_weight(offset):
    return jnp.where((offset == 0) | (offset == 1), 1.0, 0.0).astype(F32)


def dot(a, b, exact=False):
    high, b = a.astype(jnp.bfloat16), b.astype(jnp.bfloat16)
    if exact:
        return jnp.dot(high, b, preferred_element_type=F32)
    low = (a - high.astype(F32)).astype(jnp.bfloat16)
    if a.shape[1] == 128:
        both = jnp.concatenate([high, low], 1)
        return jnp.dot(both, jnp.concatenate([b, b], 0), preferred_element_type=F32)
    return jnp.dot(high, b, preferred_element_type=F32) + jnp.dot(low, b, preferred_element_type=F32)


def full_dot(a, b):
    return jnp.dot(a, b, precision=lax.Precision.HIGHEST, preferred_element_type=F32)


def face_code(a, b):
    s = a + b
    return jnp.where(s < 0.75, 1.0, jnp.where(s < 1.1, MIXED, WATER)).astype(F32)


def face_mean(a, b):
    product = a * b
    return jnp.where(product > 0.0, 2.0 * product / (a + b), jnp.maximum(a, b))


def blocks(lo, hi, size, work):
    count, rest = divmod(hi - lo, size)
    if count == 1:
        work(lo, size)
    elif count:

        def body(i, carry):
            work(lo + i * size, size)
            return carry

        lax.fori_loop(0, count, body, 0)
    if rest:
        work(hi - rest, rest)


def planes(lo, hi, size, plane, refs):
    def work(j, n):
        results = [plane(j + i) for i in range(n)]
        for i, values in enumerate(results):
            for ref, value in zip(refs, values):
                ref[j + i] = value

    blocks(lo, hi, size, work)


def planes_at(js, plane, refs):
    results = [plane(j) for j in js]
    for j, values in zip(js, results):
        for ref, value in zip(refs, values):
            ref[j] = value


def weights_at(m_low, m, m_high, face, outside, full):
    lane = iota(m.shape, m.ndim - 1)
    last = m.shape[-1] - 1
    wx, wx_low = face(m, m_high), face(m_low, m)
    wy = face(m, up_y(m))
    m_up = up_z(m)
    if full:
        m_up = jnp.where(lane == last, outside, m_up)
    wz = face(m, m_up)
    wz_low = dn_z(wz)
    if full:
        wz_low = jnp.where(lane == 0, face(m, jnp.full_like(m, outside)), wz_low)
    d = (wx + wx_low) + (wy + dn_y(wy)) + (wz + wz_low)
    q = jnp.where(m != outside, OMEGA / d, 0.0)
    if full:
        wz = jnp.where(lane == last, 0.0, wz)
    return wx, wy, wz, q


def weights_plane(m_ref, s_ref, face, outside, full):
    def plane(j):
        wx, wy, wz, q = weights_at(m_ref[j - 1], m_ref[j], m_ref[j + 1], face, outside, full)
        return wx, wy, wz, q, q * s_ref[j]

    return plane


def weights_pass(lo, hi, size, m_ref, w, s_ref, p_ref, face, outside, full):
    w[0][lo - 1] = face(m_ref[lo - 1], m_ref[lo])
    planes(lo, hi, size, weights_plane(m_ref, s_ref, face, outside, full), (*w, p_ref))


def flow(j, p, p_ref, w):
    wx_ref, wy_ref, wz_ref = w[:3]
    wy, wz = wy_ref[j], wz_ref[j]
    along_x = wx_ref[j] * p_ref[j + 1] + wx_ref[j - 1] * p_ref[j - 1]
    along_y = wy * up_y(p) + dn_y(wy * p)
    along_z = wz * up_z(p) + dn_z(wz * p)
    return along_x + along_y + along_z


def sweep_plane(p_ref, s_ref, w):
    def plane(j):
        p = p_ref[j]
        total = flow(j, p, p_ref, w)
        return (KEEP * p + w[3][j] * (total if s_ref is None else s_ref[j] + total),)

    return plane


def sweep(lo, hi, size, p_ref, out_ref, s_ref, w):
    planes(lo, hi, size, sweep_plane(p_ref, s_ref, w), (out_ref,))


def remainder_plane(p_ref, s_ref, w):
    def plane(j):
        p, q = p_ref[j], w[3][j]
        r = s_ref[j] + flow(j, p, p_ref, w) - (OMEGA / q) * p
        return (jnp.where(q > 0.0, r, 0.0),)

    return plane


def remainder(lo, hi, size, p_ref, out_ref, s_ref, w):
    planes(lo, hi, size, remainder_plane(p_ref, s_ref, w), (out_ref,))


def halving(valid):
    lane_in, lane_out = iota((256, 128), 0), iota((256, 128), 1)
    down = jnp.where((lane_in < 128) & (lane_out < valid), restrict_weight(lane_in - 2 * lane_out), 0.0)
    return down + jnp.where(lane_in >= 128, pair_weight(lane_in - 2 * lane_out), 0.0)


def halve_rows(t):
    above = up_y(t)
    near, far = t + above, dn_y(t) + up_y(above)
    return jnp.where(iota(t.shape, 1) < 64, near * 0.375 + far * 0.125, near)


def every_other(ref, first, count):
    return ref[pl.ds(first, count, stride=2)]


def twice(ref, first, value):
    count = value.shape[0]
    ref[pl.ds(first, count, stride=2)] = value
    ref[pl.ds(first + 1, count, stride=2)] = value


def halve(count, r_ref, m_ref, t_ref, u_ref, valid, product):
    for k in range(count):
        rows = slice(k * 32, k * 32 + 32)
        t_ref[rows, :128] = restrict_x(r_ref, 2 * k + 1) if 1 <= k < count - 1 else jnp.zeros((32, 128), F32)
        t_ref[rows, 128:] = (m_ref[2 * k + 2] + m_ref[2 * k + 3]) * (0.25 * 0.125)
    packed = product(t_ref[...], halving(valid))
    for k in range(count):
        u_ref[k * 32 : k * 32 + 32] = halve_rows(packed[k * 32 : k * 32 + 32])
    return [every_other(u_ref, k * 32, 16) for k in range(count)]


def restrict_x(r_ref, j):
    return (r_ref[j] + r_ref[j + 3]) * 0.125 + (r_ref[j + 1] + r_ref[j + 2]) * 0.375


def edge(axis):
    i = lax.axis_index(axis)
    return i == 0, i == lax.axis_size(axis) - 1


def blank(flag, value, other):
    return jnp.where(flag, other, value)


X0 = 5
N0 = 32 + 2 * X0
N1 = 28
N2 = 28
N3 = 12
BIG = (N0, 40, 256)
VM = pl.BlockSpec(memory_space=pltpu.VMEM)


def call(kernel, name, out_shape, scratch, limit, *operands, aliases=None, in_specs=None, out_specs=None):
    return pl.pallas_call(
        kernel,
        in_specs=[VM] * len(operands) if in_specs is None else in_specs,
        out_specs=[VM] * len(out_shape) if out_specs is None else out_specs,
        out_shape=out_shape,
        scratch_shapes=scratch,
        input_output_aliases=aliases or {},
        compiler_params=pltpu.CompilerParams(vmem_limit_bytes=limit * MIB),
        name=name,
    )(*operands)


def kept(*shape):
    return pltpu.VMEM(shape, F32)


def send_rows_kernel(s_hbm, f_hbm, dn_ref, upw_ref, s_lo, s_hi, f_lo, f_hi, sems):
    parts = ((s_hbm, 0, s_lo), (f_hbm, 0, f_lo), (s_hbm, 24, s_hi), (f_hbm, 24, f_hi))
    copies = [
        pltpu.make_async_copy(ref.at[:, pl.ds(first, 8)], part, sems.at[k])
        for k, (ref, first, part) in enumerate(parts)
    ]
    for copy in copies:
        copy.start()
    for copy in copies:
        copy.wait()
    above = iota((8, 256), 0) < 4

    def work(j, n):
        here = pl.ds(j, n)
        dn_ref[here] = jnp.where(above, s_lo[here], pltpu.roll(f_lo[here].astype(F32), 4, 1))
        upw_ref[here] = jnp.where(above, pltpu.roll(f_hi[here].astype(F32), 4, 1), s_hi[here])

    blocks(0, 32, 8, work)


def send_rows(source, phase):
    part = (32, 8, 256)
    scratch = [kept(*part)] * 2 + [pltpu.VMEM(part, jnp.int32)] * 2 + [pltpu.SemaphoreType.DMA((4,))]
    hbm = [pl.BlockSpec(memory_space=pltpu.HBM)] * 2
    operands = [pltpu.with_memory_space_constraint(x, pltpu.HBM) for x in (source, phase)]
    return call(send_rows_kernel, "send_rows", [kept(*part)] * 2, scratch, 4, *operands, in_specs=hbm)


def load_kernel(s_hbm, f_hbm, sent, s_ref, f_ref, sems):
    del sent
    copies = [
        pltpu.make_async_copy(a, b, sems.at[k]) for k, (a, b) in enumerate(((s_hbm, s_ref), (f_hbm, f_ref)))
    ]
    for copy in copies:
        copy.start()
    for copy in copies:
        copy.wait()


def load(source, phase, sent):
    any_space = pl.BlockSpec(memory_space=pl.ANY)
    hbm = [pl.BlockSpec(memory_space=pltpu.HBM)] * 2
    operands = [pltpu.with_memory_space_constraint(x, pltpu.HBM) for x in (source, phase)]
    out = [kept(32, 32, 256), pltpu.VMEM((32, 32, 256), jnp.int32)]
    scratch = [pltpu.SemaphoreType.DMA((2,))]
    return call(load_kernel, "load", out, scratch, 4, *operands, sent, in_specs=[*hbm, any_space])


def halo_rows(lo, hi):
    low_y, high_y = edge("gy")
    above = iota((8, 256), 0) < 4
    outer = (above & high_y) | (~above & low_y)
    source = jnp.where(outer, 0.0, jnp.where(above, hi, lo))
    code = jnp.where(outer, OUT, pltpu.roll(jnp.where(above, lo, hi), 4, lo.ndim - 2))
    return source, code


def send_planes_kernel(s_in, f_in, ylo, yhi, dn_ref, upw_ref):
    for first, out_ref, last, at in ((0, dn_ref, 2, (0, 1, 2)), (28, upw_ref, 1, (None, 0, 1, 2))):
        block = slice(first, first + 4)
        halo_source, halo_code = halo_rows(ylo[block], yhi[block])
        code = [jnp.concatenate([f_in[first + k].astype(F32), halo_code[k]], 0) for k in range(4)]
        source = [jnp.concatenate([s_in[first + k], halo_source[k]], 0) for k in range(4)]
        q = weights_at(code[last - 1], code[last], code[last + 1], face_code, OUT, True)[3]
        source[last] = q * source[last]
        for k, place in enumerate(at):
            if place is not None:
                out_ref[place] = source[k]
                out_ref[place + 3] = code[k]


def water_to_mobility(n):
    return 0.25 * ((8.0 - n) * 0.125 + n * (0.125 * WATER))


def lanes_to_128():
    return iota((256, 128), 0) - 2 * iota((256, 128), 1)


def halve0(ks, r_ref, src1, t_ref, u_ref):
    for i, k in enumerate(ks):
        t_ref[i * 40 : i * 40 + 40] = restrict_x(r_ref, 2 * k + 4)
    coarse = dot(t_ref[: len(ks) * 40], restrict_weight(lanes_to_128()))
    for i in range(len(ks)):
        t = coarse[i * 40 : i * 40 + 40]
        above = up_y(t)
        u_ref[i * 40 : i * 40 + 40] = (t + above) * 0.375 + (dn_y(t) + up_y(above)) * 0.125
    for i, k in enumerate(ks):
        src1[k] = every_other(u_ref, i * 40, 16)


def inner0_kernel(
    s_in, f_in, ylo, yhi,
    s_ref, c_ref, wx, wy, wz, q_ref, p1, p2, r_ref, src1, mob1,
    t_ref, u_ref,
):
    def own_planes(j, n):
        here, there = pl.ds(j, n), pl.ds(j + X0, n)
        source, code = halo_rows(ylo[here], yhi[here])
        s_ref[there, :32] = s_in[here]
        s_ref[there, 32:] = source
        c_ref[there, :32] = f_in[here].astype(F32)
        c_ref[there, 32:] = code

    blocks(0, 32, 4, own_planes)
    w = (wx, wy, wz, q_ref)
    weights_pass(6, 36, 10, c_ref, w, s_ref, p1, face_code, OUT, True)
    sweep(7, 35, 14, p1, p2, s_ref, w)
    remainder(8, 34, 13, p2, r_ref, s_ref, w)

    halve0(range(2, 14), r_ref, src1, t_ref, u_ref)
    for k in range(16):
        t_ref[k * 40 : k * 40 + 40] = c_ref[2 * k + X0] + c_ref[2 * k + X0 + 1]
    water = dot(t_ref[...], pair_weight(lanes_to_128()), exact=True)
    for k in range(16):
        t = water[k * 40 : k * 40 + 40]
        u_ref[k * 40 : k * 40 + 40] = t + up_y(t)
    for k in range(16):
        mob1[k] = water_to_mobility(every_other(u_ref, k * 40, 16))


def inner0(source, phase, ylo, yhi):
    return call(
        inner0_kernel, "inner0", [kept(*BIG)] * 9 + [kept(16, 16, 128)] * 2,
        [kept(640, 256), kept(640, 128)], 4, source, phase, ylo, yhi,
    )


def lay_rows(out, first, rows):
    for k in range(4):
        out[first + k] = rows[k // 2 * 16 : k // 2 * 16 + 16, k % 2 * 128 : k % 2 * 128 + 128]


def outer0_kernel(
    xlo, xhi, mob1, s_0, c_0, wx_0, wy_0, wz_0, q_0, p1_0, p2_0, r_0, src1_0,
    s_ref, c_ref, wx, wy, wz, q_ref, p1, p2, r_ref, src1, dn1, upw1, rows_dn, rows_up,
    t_ref, u_ref,
):
    low_x, high_x = edge("gx")
    p1[2] = blank(low_x, xlo[0], 0.0)
    s_ref[3:5] = blank(low_x, xlo[1:3], 0.0)
    c_ref[2:5] = blank(low_x, xlo[3:], OUT)
    s_ref[37:39] = blank(high_x, xhi[:2], 0.0)
    p1[39] = blank(high_x, xhi[2], 0.0)
    c_ref[37:40] = blank(high_x, xhi[3:], OUT)
    w = (wx, wy, wz, q_ref)
    wx[2] = face_code(c_ref[2], c_ref[3])
    wx[35] = face_code(c_ref[35], c_ref[36])
    planes_at((3, 4, 5, 36, 37, 38), weights_plane(c_ref, s_ref, face_code, OUT, True), (*w, p1))
    planes_at((3, 4, 5, 6, 35, 36, 37, 38), sweep_plane(p1, s_ref, w), (p2,))
    planes_at((4, 5, 6, 7, 34, 35, 36, 37), remainder_plane(p2, s_ref, w), (r_ref,))
    halve0((0, 1, 14, 15), r_ref, src1, t_ref, u_ref)
    dn1[:5] = src1[:5]
    dn1[5:11] = mob1[:6]
    lay_rows(dn1, 11, p2[X0 + 2, :32])
    upw1[:5] = src1[11:]
    upw1[5:11] = mob1[10:]
    lay_rows(upw1, 11, p2[X0 + 29, :32])
    for k in range(32):
        rows_dn[k : k + 1] = p2[X0 + k, 2:3]
        rows_up[k : k + 1] = p2[X0 + k, 29:30]


def outer0(xlo, xhi, mob1, state):
    return call(
        outer0_kernel, "outer0",
        [kept(*BIG)] * 9 + [kept(16, 16, 128)] + [kept(15, 16, 128)] * 2 + [kept(32, 256)] * 2,
        [kept(160, 256), kept(160, 128)], 4, xlo, xhi, mob1, *state, aliases={3 + k: k for k in range(10)},
    )


def pack1_kernel(src, mob, xlo, xhi, rows_dn, rows_up, dn_ref, upw_ref):
    low_x, high_x = edge("gx")
    for rows, out, p_rows in ((slice(0, 8), dn_ref, rows_dn), (slice(8, 16), upw_ref, rows_up)):
        out[0, :8] = jnp.zeros((8, 128), F32)
        out[N1 - 1, :8] = jnp.zeros((8, 128), F32)
        out[1:6, :8] = blank(low_x, xlo[:5, rows], 0.0)
        out[0:6, 8:] = blank(low_x, xlo[5:11, rows], 0.0)
        out[6:22, :8] = src[:, rows]
        out[6:22, 8:] = mob[:, rows]
        out[22:27, :8] = blank(high_x, xhi[:5, rows], 0.0)
        out[22:28, 8:] = blank(high_x, xhi[5:11, rows], 0.0)
        lay_rows(out, N1, p_rows[...])


def pack1(*operands):
    return call(pack1_kernel, "pack1", [kept(N1 + 4, 16, 128)] * 2, [], 4, *operands)


def down1_kernel(
    src, mob, xlo, xhi, ylo, yhi,
    own2, dn2, upw2, s_ref, wx, wy, wz, q_ref, p2,
    m_ref, p1, r_ref, t_ref, u_ref, pk_ref,
):
    low_x, high_x = edge("gx")
    low_y, high_y = edge("gy")
    zero = jnp.zeros((32, 128), F32)
    s_ref[0] = zero
    s_ref[N1 - 1] = zero
    s_ref[1:6, :16] = blank(low_x, xlo[:5], 0.0)
    m_ref[0:6, :16] = blank(low_x, xlo[5:11], 0.0)
    s_ref[6:22, :16] = src[...]
    m_ref[6:22, :16] = mob[...]
    s_ref[22:27, :16] = blank(high_x, xhi[:5], 0.0)
    m_ref[22:28, :16] = blank(high_x, xhi[5:11], 0.0)
    s_ref[:, 16:24] = blank(high_y, yhi[:N1, :8], 0.0)
    m_ref[:, 16:24] = blank(high_y, yhi[:N1, 8:], 0.0)
    s_ref[:, 24:] = blank(low_y, ylo[:N1, :8], 0.0)
    m_ref[:, 24:] = blank(low_y, ylo[:N1, 8:], 0.0)
    w = (wx, wy, wz, q_ref)

    weights_pass(1, N1 - 1, 26, m_ref, w, s_ref, p1, face_mean, 0.0, True)
    sweep(2, N1 - 2, 24, p1, p2, s_ref, w)
    remainder(3, N1 - 3, 22, p2, r_ref, s_ref, w)

    for k, packed in enumerate(halve(12, r_ref, m_ref, t_ref, u_ref, 64, full_dot)):
        pk_ref[k] = packed
    own2[...] = pk_ref[2:10]
    row = iota((8, 128), 0)
    for out, first in ((dn2, 2), (upw2, 0)):
        for k in range(10):
            out[k] = pk_ref[first + k, :8]
        for k in range(5):
            a, b = pk_ref[first + 2 * k, 8:], pk_ref[first + 2 * k + 1, 8:]
            b = jnp.where(row < 4, pltpu.roll(b, 2, 0), pltpu.roll(b, 6, 0))
            out[10 + k] = jnp.where((row < 2) | (row >= 6), a, b)


def down1(*operands):
    return call(
        down1_kernel, "down1", [kept(8, 16, 128)] + [kept(15, 8, 128)] * 2 + [kept(N1, 32, 128)] * 6,
        [kept(N1, 32, 128)] * 3 + [kept(384, 256), kept(384, 128), kept(12, 16, 128)], 6, *operands,
    )


def pack2_kernel(own, xlo, xhi, dn_ref, upw_ref):
    low_x, high_x = edge("gx")
    row = iota((8, 128), 0)
    for a in range(N2 // 4):
        two_dn = two_up = jnp.zeros((8, 128), F32)
        for b in range(4):
            j = 4 * a + b
            if 10 <= j < 18:
                tile, more = own[j - 10, :8], own[j - 10, 8:]
            else:
                flag, halo, k = (low_x, xlo, j) if j < 10 else (high_x, xhi, j - 18)
                tile, more = blank(flag, halo[k], 0.0), blank(flag, halo[10 + k // 2], 0.0)
                if k % 2:
                    more = jnp.where(row < 4, pltpu.roll(more, 6, 0), pltpu.roll(more, 2, 0))
            dn_ref[j] = tile
            upw_ref[j] = tile
            here = (row == 2 * b) | (row == 2 * b + 1)
            two_dn = jnp.where(here, pltpu.roll(more, 2 * b, 0) if b else more, two_dn)
            two_up = jnp.where(here, pltpu.roll(more, 2 * b + 2, 0) if b < 3 else more, two_up)
        dn_ref[N2 + a] = two_dn
        upw_ref[N2 + a] = two_up


def pack2(*operands):
    return call(pack2_kernel, "pack2", [kept(N2 + N2 // 4, 8, 128)] * 2, [], 4, *operands)


def before_kernel(wx0, wy0, wz0, q0, s0, down0_ref, plane_lo, plane_hi, rows_lo, rows_hi, out_ref, pa0, pb0, row_ref):
    low_x, high_x = edge("gx")
    low_y, high_y = edge("gy")
    row8 = iota((8, 256), 0)

    def plane_of(message, first):
        tiles = [message[first + k] for k in range(4)]
        return jnp.concatenate(
            [jnp.concatenate(tiles[:2], 1), jnp.concatenate(tiles[2:], 1), jnp.zeros((8, 256), F32)], 0
        )

    pa0[2] = blank(low_x, plane_of(plane_lo, 11), 0.0)
    pa0[N0 - 3] = blank(high_x, plane_of(plane_hi, 11), 0.0)
    for k in range(4):
        h, z = k // 2 * 16, k % 2 * 128
        row_ref[0, h : h + 16, z : z + 128] = blank(high_y, rows_hi[N1 + k], 0.0)
        row_ref[1, h : h + 16, z : z + 128] = blank(low_y, rows_lo[N1 + k], 0.0)
    for j in (3, 4, 37, 38):
        pa0[j] = down0_ref[j]

    def own_planes(j, n):
        for i in range(n):
            above = row_ref[0, pl.ds(j + i, 1)]
            below = row_ref[1, pl.ds(j + i, 1)]
            p = down0_ref[j + i + X0]
            halo = jnp.where(row8 == 2, above, jnp.where(row8 == 5, below, p[32:]))
            pa0[j + i + X0, :32] = p[:32]
            pa0[j + i + X0, 32:] = halo

    blocks(0, 32, 8, own_planes)
    w0 = (wx0, wy0, wz0, q0)
    sweep(3, N0 - 3, 12, pa0, pb0, s0, w0)
    sweep(4, N0 - 4, 17, pb0, out_ref, s0, w0)


def before(*operands):
    scratch = [kept(*BIG)] * 2 + [kept(2, 32, 256)]
    return call(before_kernel, "before", [kept(*BIG)], scratch, 5, *operands)[0]


def base_kernel(wx0, wy0, wz0, q0, s0, p_ref, sent, base_s, base_r):
    del sent
    w0 = (wx0, wy0, wz0, q0)

    def plane(j):
        p = p_ref[j + X0]
        dp = (OMEGA / q0[j + X0]) * p
        return dp[:32], (s0[j + X0] + flow(j + X0, p, p_ref, w0) - dp)[:32]

    planes(0, 32, 8, plane, (base_s, base_r))


def base(*operands):
    return call(base_kernel, "base", [kept(32, 32, 256)] * 2, [], 4, *operands)


def up_kernel(
    ext, ylo, yhi, s1, wx1, wy1, wz1, q1, down1_ref,
    wx0, wy0, wz0, q0, base_s, base_r,
    scaled, residual,
    pa0, pb0,
    pa1, pb1,
    s2, m2, wx2, wy2, wz2, q2, pa2, pb2, r2,
    s3, m3, wx3, wy3, wz3, q3, pa3, pb3,
    t_ref, u_ref, v_ref, rise_lo, rise_hi, out_a, out_b, sems,
):
    low_y, high_y = edge("gy")

    lane8, sub8 = iota((8, 128), 1), iota((8, 128), 0)

    def put(j, rows, packed):
        s2[j, rows] = packed
        m2[j, rows] = jnp.where(lane8 < 64, pltpu.roll(packed, 64, 1), 0.0)

    for j in range(N2):
        a, b = divmod(j, 4)
        hi, lo = yhi[N2 + a], ylo[N2 + a]
        hi = pltpu.roll(hi, 8 - 2 * b, 0) if b else hi
        lo = pltpu.roll(lo, 6 - 2 * b, 0) if b < 3 else lo
        put(j, slice(0, 8), ext[j])
        put(j, slice(8, 16), blank(high_y, yhi[j], 0.0))
        put(j, slice(16, 24), jnp.where((sub8 < 4) & ~high_y, hi, jnp.where((sub8 >= 4) & ~low_y, lo, 0.0)))
        put(j, slice(24, 32), blank(low_y, ylo[j], 0.0))

    w2 = (wx2, wy2, wz2, q2)

    weights_pass(1, N2 - 1, 26, m2, w2, s2, pa2, face_mean, 0.0, False)
    sweep(2, N2 - 2, 24, pa2, pb2, s2, w2)
    remainder(3, N2 - 3, 22, pb2, r2, s2, w2)

    lane16 = iota((16, 128), 1)
    for k, packed in enumerate(halve(12, r2, m2, t_ref, u_ref, 32, dot)):
        s3[k] = packed
        m3[k] = jnp.where(lane16 < 64, pltpu.roll(packed, 64, 1), 0.0)
    w3 = (wx3, wy3, wz3, q3)

    weights_pass(1, N3 - 1, 10, m3, w3, s3, pa3, face_mean, 0.0, False)
    sweep(2, N3 - 2, 8, pa3, pb3, s3, w3)

    lane_in, lane_out = iota((128, 128), 0), iota((128, 128), 1)
    double = pair_weight(lane_out - 2 * lane_in)
    for k in range(8):
        v_ref[k * 16 : k * 16 + 16] = pb3[k + 2]
    rise = dot(v_ref[:128], jnp.where(lane_in < 32, double, 0.0))
    for k in range(8):
        twice(u_ref, k * 32, rise[k * 16 : k * 16 + 16])
    for k in range(8):
        for j in (2 * k + 6, 2 * k + 7):
            pb2[j] = pb2[j] + u_ref[k * 32 : k * 32 + 32]
    sweep(7, 21, 14, pb2, pa2, s2, w2)
    sweep(8, 20, 12, pa2, pb2, s2, w2)

    for k in range(12):
        v_ref[k * 16 : k * 16 + 8] = pb2[k + 8, :8]
        v_ref[k * 16 + 8 : k * 16 + 16] = jnp.where(sub8 < 4, pb2[k + 8, 8:16], pb2[k + 8, 24:])
    rise = dot(v_ref[:192], double)
    for k in range(12):
        twice(u_ref, k * 32, rise[k * 16 : k * 16 + 16])
    for k in range(12):
        for j in (2 * k + 2, 2 * k + 3):
            pa1[j] = down1_ref[j] + u_ref[k * 32 : k * 32 + 32]
    w1 = (wx1, wy1, wz1, q1)
    sweep(3, 25, 22, pa1, pb1, s1, w1)
    sweep(4, 24, 20, pb1, pa1, s1, w1)

    for k in range(20):
        v_ref[k * 24 : k * 24 + 16] = pa1[k + 4, :16]
        v_ref[k * 24 + 16 : k * 24 + 24] = jnp.where(
            sub8 < 2, pa1[k + 4, 16:24], pltpu.roll(pa1[k + 4, 24:], 4, 0)
        )
    for z, out in ((0, rise_lo), (128, rise_hi)):
        double = pair_weight(lane_out + z - 2 * lane_in)
        rise = dot(v_ref[...], double)
        for k in range(20):
            twice(out, k * 48, rise[k * 24 : k * 24 + 24])

    def rise_at(k):
        here = pl.ds(k * 48 if isinstance(k, int) else pl.multiple_of(k * 48, 8), 40)
        return jnp.concatenate([rise_lo[here], rise_hi[here]], 1)

    w0 = (wx0, wy0, wz0, q0)

    def first_pairs(k0, n):
        results = []
        for i in range(n):
            k = k0 + i
            low, e, high = rise_at(k - 1), rise_at(k), rise_at(k + 1)
            e_up_y, e_up_z = up_y(e), up_z(e)
            for j, x_low, x_high in ((2 * k + 1, low, e), (2 * k + 2, e, high)):
                wy, wz = wy0[j], wz0[j]
                along_x = wx0[j] * x_high + wx0[j - 1] * x_low
                along_y = wy * e_up_y + dn_y(wy * e)
                along_z = wz * e_up_z + dn_z(wz * e)
                results.append((j, KEEP * e + q0[j] * (along_x + along_y + along_z)))
        for j, value in results:
            pb0[j] = value

    blocks(1, 19, 6, first_pairs)
    sweep(4, N0 - 4, 17, pb0, pa0, None, w0)

    def out_copies(k, j):
        here = pl.ds(j, 8)
        return (
            pltpu.make_async_copy(out_a.at[here], scaled.at[here], sems.at[0, k]),
            pltpu.make_async_copy(out_b.at[here], residual.at[here], sems.at[1, k]),
        )

    def last(k, carry):
        j = k * 8
        results = []
        for i in range(8):
            p = pa0[j + i + X0]
            dp = (OMEGA / q0[j + i + X0]) * p
            a = base_s[j + i] + dp[:32]
            results.append((a, base_r[j + i] + (flow(j + i + X0, p, pa0, w0) - dp)[:32]))
        for i, (a, b) in enumerate(results):
            out_a[j + i] = a
            out_b[j + i] = b
        for copy in out_copies(k, j):
            copy.start()
        return carry

    lax.fori_loop(0, 4, last, 0)
    for k in range(4):
        for copy in out_copies(k, k * 8):
            copy.wait()


def way_up(*operands):
    shape = jax.ShapeDtypeStruct((32, 32, 256), F32)
    buf = lambda count, *shape: [kept(*shape)] * count
    scratch = (
        buf(2, *BIG)
        + buf(2, N1, 32, 128)
        + buf(9, N2, 32, 128)
        + buf(8, N3, 16, 128)
        + buf(1, 384, 256)
        + buf(1, 384, 128)
        + buf(1, 480, 128)
        + buf(2, 960, 128)
        + buf(2, 32, 32, 256)
        + [pltpu.SemaphoreType.DMA((2, 4))]
    )
    hbm = pl.BlockSpec(memory_space=pl.ANY)
    return call(up_kernel, "way_up", [shape] * 2, scratch, 20, *operands, out_specs=[hbm] * 2)


def shift(a, axis, step):
    count = lax.axis_size(axis)
    return lax.ppermute(a, axis, [(i, (i + step) % count) for i in range(count)])


def both(to_low, to_high, axis):
    return shift(to_high, axis, 1), shift(to_low, axis, -1)


def shards(source, phase):
    dn0, up0 = send_rows(source, phase)
    ylo, yhi = both(dn0, up0, "gy")
    source, phase = load(source, phase, dn0)
    msg = [kept(6, 40, 256)] * 2
    dn0, up0 = call(send_planes_kernel, "send_planes", msg, [], 4, source, phase, ylo, yhi)
    xlo, xhi = both(dn0, up0, "gx")
    *state, mob1 = inner0(source, phase, ylo, yhi)
    s0, _, wx0, wy0, wz0, q0, _, p0, _, src1, dn1, up1, rows_dn, rows_up = outer0(xlo, xhi, mob1, state)
    xlo1, xhi1 = both(dn1, up1, "gx")
    ylo1, yhi1 = both(*pack1(src1, mob1, xlo1, xhi1, rows_dn, rows_up), "gy")
    own2, dn2, up2, *level1 = down1(src1, mob1, xlo1, xhi1, ylo1, yhi1)
    xlo, xhi = both(dn2, up2, "gx")
    ext, ext_up = pack2(own2, xlo, xhi)
    ylo, yhi = both(ext, ext_up, "gy")
    weights = (wx0, wy0, wz0, q0)
    p0 = before(*weights, s0, p0, xlo1, xhi1, ylo1, yhi1)
    return tuple(way_up(ext, ylo, yhi, *level1, *weights, *base(*weights, s0, p0, ext)))


def solution(mesh):
    spec = P("gx", "gy", None)
    return jax.shard_map(shards, mesh=mesh, in_specs=(spec, spec), out_specs=(spec, spec), check_vma=False)
```

```python
import jax
import jax.numpy as jnp
from jax import lax
from jax.experimental import pallas as pl
from jax.experimental.pallas import tpu as pltpu
from jax.sharding import PartitionSpec as P

OMEGA = 0.8
KEEP = 0.2
WATER = 0.001
MIXED = 2.0 * WATER / (1.0 + WATER)
OUT = 0.25
F32 = jnp.float32
MIB = 1024 * 1024


def up_y(a):
    return pltpu.roll(a, a.shape[-2] - 1, a.ndim - 2)


def dn_y(a):
    return pltpu.roll(a, 1, a.ndim - 2)


def up_z(a):
    return pltpu.roll(a, a.shape[-1] - 1, a.ndim - 1)


def dn_z(a):
    return pltpu.roll(a, 1, a.ndim - 1)


def iota(shape, dim):
    return lax.broadcasted_iota(jnp.int32, shape, dim)


def ring(row, cut, rows):
    return jnp.where(row < cut, row, row - rows)


def restrict_weight(offset):
    near = (offset == 0) | (offset == 1)
    far = (offset == -1) | (offset == 2)
    return jnp.where(near, 0.375, jnp.where(far, 0.125, 0.0)).astype(F32)


def pair_weight(offset):
    return jnp.where((offset == 0) | (offset == 1), 1.0, 0.0).astype(F32)


def dot(a, b, exact=False):
    high, b = a.astype(jnp.bfloat16), b.astype(jnp.bfloat16)
    if exact:
        return jnp.dot(high, b, preferred_element_type=F32)
    low = (a - high.astype(F32)).astype(jnp.bfloat16)
    if a.shape[1] == 128:
        both = jnp.concatenate([high, low], 1)
        return jnp.dot(both, jnp.concatenate([b, b], 0), preferred_element_type=F32)
    return jnp.dot(high, b, preferred_element_type=F32) + jnp.dot(low, b, preferred_element_type=F32)


def full_dot(a, b):
    return jnp.dot(a, b, precision=lax.Precision.HIGHEST, preferred_element_type=F32)


def face_code(a, b):
    s = a + b
    return jnp.where(s < 0.75, 1.0, jnp.where(s < 1.1, MIXED, WATER)).astype(F32)


def face_mean(a, b):
    product = a * b
    return jnp.where(product > 0.0, 2.0 * product / (a + b), jnp.maximum(a, b))


def blocks(lo, hi, size, work):
    count, rest = divmod(hi - lo, size)
    if count == 1:
        work(lo, size)
    elif count:

        def body(i, carry):
            work(lo + i * size, size)
            return carry

        lax.fori_loop(0, count, body, 0)
    if rest:
        work(hi - rest, rest)


def planes(lo, hi, size, plane, refs):
    def work(j, n):
        results = [plane(j + i) for i in range(n)]
        for i, values in enumerate(results):
            for ref, value in zip(refs, values):
                ref[j + i] = value

    blocks(lo, hi, size, work)


def planes_at(js, plane, refs):
    results = [plane(j) for j in js]
    for j, values in zip(js, results):
        for ref, value in zip(refs, values):
            ref[j] = value


def weights_at(m_low, m, m_high, face, outside, full):
    lane = iota(m.shape, m.ndim - 1)
    last = m.shape[-1] - 1
    wx, wx_low = face(m, m_high), face(m_low, m)
    wy = face(m, up_y(m))
    m_up = up_z(m)
    if full:
        m_up = jnp.where(lane == last, outside, m_up)
    wz = face(m, m_up)
    wz_low = dn_z(wz)
    if full:
        wz_low = jnp.where(lane == 0, face(m, jnp.full_like(m, outside)), wz_low)
    d = (wx + wx_low) + (wy + dn_y(wy)) + (wz + wz_low)
    q = jnp.where(m != outside, OMEGA / d, 0.0)
    if full:
        wz = jnp.where(lane == last, 0.0, wz)
    return wx, wy, wz, q


def weights_plane(m_ref, s_ref, face, outside, full):
    def plane(j):
        wx, wy, wz, q = weights_at(m_ref[j - 1], m_ref[j], m_ref[j + 1], face, outside, full)
        return wx, wy, wz, q, q * s_ref[j]

    return plane


def weights_pass(lo, hi, size, m_ref, w, s_ref, p_ref, face, outside, full):
    w[0][lo - 1] = face(m_ref[lo - 1], m_ref[lo])
    planes(lo, hi, size, weights_plane(m_ref, s_ref, face, outside, full), (*w, p_ref))


def flow(j, p, p_ref, w):
    wx_ref, wy_ref, wz_ref = w[:3]
    wy, wz = wy_ref[j], wz_ref[j]
    along_x = wx_ref[j] * p_ref[j + 1] + wx_ref[j - 1] * p_ref[j - 1]
    along_y = wy * up_y(p) + dn_y(wy * p)
    along_z = wz * up_z(p) + dn_z(wz * p)
    return along_x + along_y + along_z


def sweep_plane(p_ref, s_ref, w):
    def plane(j):
        p = p_ref[j]
        total = flow(j, p, p_ref, w)
        return (KEEP * p + w[3][j] * (total if s_ref is None else s_ref[j] + total),)

    return plane


def sweep(lo, hi, size, p_ref, out_ref, s_ref, w):
    planes(lo, hi, size, sweep_plane(p_ref, s_ref, w), (out_ref,))


def remainder_plane(p_ref, s_ref, w):
    def plane(j):
        p, q = p_ref[j], w[3][j]
        r = s_ref[j] + flow(j, p, p_ref, w) - (OMEGA / q) * p
        return (jnp.where(q > 0.0, r, 0.0),)

    return plane


def remainder(lo, hi, size, p_ref, out_ref, s_ref, w):
    planes(lo, hi, size, remainder_plane(p_ref, s_ref, w), (out_ref,))


def halving(valid):
    lane_in, lane_out = iota((256, 128), 0), iota((256, 128), 1)
    down = jnp.where((lane_in < 128) & (lane_out < valid), restrict_weight(lane_in - 2 * lane_out), 0.0)
    return down + jnp.where(lane_in >= 128, pair_weight(lane_in - 2 * lane_out), 0.0)


def halve_rows(t):
    above = up_y(t)
    near, far = t + above, dn_y(t) + up_y(above)
    return jnp.where(iota(t.shape, 1) < 64, near * 0.375 + far * 0.125, near)


def every_other(ref, first, count):
    return ref[pl.ds(first, count, stride=2)]


def twice(ref, first, value):
    count = value.shape[0]
    ref[pl.ds(first, count, stride=2)] = value
    ref[pl.ds(first + 1, count, stride=2)] = value


def halve(count, r_ref, m_ref, t_ref, u_ref, valid, product):
    for k in range(count):
        rows = slice(k * 32, k * 32 + 32)
        t_ref[rows, :128] = restrict_x(r_ref, 2 * k + 1) if 1 <= k < count - 1 else jnp.zeros((32, 128), F32)
        t_ref[rows, 128:] = (m_ref[2 * k + 2] + m_ref[2 * k + 3]) * (0.25 * 0.125)
    packed = product(t_ref[...], halving(valid))
    for k in range(count):
        u_ref[k * 32 : k * 32 + 32] = halve_rows(packed[k * 32 : k * 32 + 32])
    return [every_other(u_ref, k * 32, 16) for k in range(count)]


def restrict_x(r_ref, j):
    return (r_ref[j] + r_ref[j + 3]) * 0.125 + (r_ref[j + 1] + r_ref[j + 2]) * 0.375


def edge(axis):
    i = lax.axis_index(axis)
    return i == 0, i == lax.axis_size(axis) - 1


def blank(flag, value, other):
    return jnp.where(flag, other, value)


X0 = 5
N0 = 32 + 2 * X0
N1 = 28
N2 = 28
N3 = 12
BIG = (N0, 40, 256)
VM = pl.BlockSpec(memory_space=pltpu.VMEM)


def call(kernel, name, out_shape, scratch, limit, *operands, aliases=None, in_specs=None, out_specs=None):
    return pl.pallas_call(
        kernel,
        in_specs=[VM] * len(operands) if in_specs is None else in_specs,
        out_specs=[VM] * len(out_shape) if out_specs is None else out_specs,
        out_shape=out_shape,
        scratch_shapes=scratch,
        input_output_aliases=aliases or {},
        compiler_params=pltpu.CompilerParams(vmem_limit_bytes=limit * MIB),
        name=name,
    )(*operands)


def kept(*shape):
    return pltpu.VMEM(shape, F32)


def send_rows_kernel(s_hbm, f_hbm, dn_ref, upw_ref, s_lo, s_hi, f_lo, f_hi, sems):
    parts = ((s_hbm, 0, s_lo), (f_hbm, 0, f_lo), (s_hbm, 24, s_hi), (f_hbm, 24, f_hi))
    copies = [
        pltpu.make_async_copy(ref.at[:, pl.ds(first, 8)], part, sems.at[k])
        for k, (ref, first, part) in enumerate(parts)
    ]
    for copy in copies:
        copy.start()
    for copy in copies:
        copy.wait()
    above = iota((8, 256), 0) < 4

    def work(j, n):
        here = pl.ds(j, n)
        dn_ref[here] = jnp.where(above, s_lo[here], pltpu.roll(f_lo[here].astype(F32), 4, 1))
        upw_ref[here] = jnp.where(above, pltpu.roll(f_hi[here].astype(F32), 4, 1), s_hi[here])

    blocks(0, 32, 8, work)


def send_rows(source, phase):
    part = (32, 8, 256)
    scratch = [kept(*part)] * 2 + [pltpu.VMEM(part, jnp.int32)] * 2 + [pltpu.SemaphoreType.DMA((4,))]
    hbm = [pl.BlockSpec(memory_space=pltpu.HBM)] * 2
    operands = [pltpu.with_memory_space_constraint(x, pltpu.HBM) for x in (source, phase)]
    return call(send_rows_kernel, "send_rows", [kept(*part)] * 2, scratch, 4, *operands, in_specs=hbm)


def load_kernel(s_hbm, f_hbm, sent, s_ref, f_ref, sems):
    del sent
    copies = [
        pltpu.make_async_copy(a, b, sems.at[k]) for k, (a, b) in enumerate(((s_hbm, s_ref), (f_hbm, f_ref)))
    ]
    for copy in copies:
        copy.start()
    for copy in copies:
        copy.wait()


def load(source, phase, sent):
    any_space = pl.BlockSpec(memory_space=pl.ANY)
    hbm = [pl.BlockSpec(memory_space=pltpu.HBM)] * 2
    operands = [pltpu.with_memory_space_constraint(x, pltpu.HBM) for x in (source, phase)]
    out = [kept(32, 32, 256), pltpu.VMEM((32, 32, 256), jnp.int32)]
    scratch = [pltpu.SemaphoreType.DMA((2,))]
    return call(load_kernel, "load", out, scratch, 4, *operands, sent, in_specs=[*hbm, any_space])


def halo_rows(lo, hi):
    low_y, high_y = edge("gy")
    above = iota((8, 256), 0) < 4
    outer = (above & high_y) | (~above & low_y)
    source = jnp.where(outer, 0.0, jnp.where(above, hi, lo))
    code = jnp.where(outer, OUT, pltpu.roll(jnp.where(above, lo, hi), 4, lo.ndim - 2))
    return source, code


def send_planes_kernel(s_in, f_in, ylo, yhi, dn_ref, upw_ref):
    for first, out_ref, last, at in ((0, dn_ref, 2, (0, 1, 2)), (28, upw_ref, 1, (None, 0, 1, 2))):
        block = slice(first, first + 4)
        halo_source, halo_code = halo_rows(ylo[block], yhi[block])
        code = [jnp.concatenate([f_in[first + k].astype(F32), halo_code[k]], 0) for k in range(4)]
        source = [jnp.concatenate([s_in[first + k], halo_source[k]], 0) for k in range(4)]
        q = weights_at(code[last - 1], code[last], code[last + 1], face_code, OUT, True)[3]
        source[last] = q * source[last]
        for k, place in enumerate(at):
            if place is not None:
                out_ref[place] = source[k]
                out_ref[place + 3] = code[k]


def water_to_mobility(n):
    return 0.25 * ((8.0 - n) * 0.125 + n * (0.125 * WATER))


def lanes_to_128():
    return iota((256, 128), 0) - 2 * iota((256, 128), 1)


def halve0(ks, r_ref, src1, t_ref, u_ref):
    for i, k in enumerate(ks):
        t_ref[i * 40 : i * 40 + 40] = restrict_x(r_ref, 2 * k + 4)
    coarse = dot(t_ref[: len(ks) * 40], restrict_weight(lanes_to_128()))
    for i in range(len(ks)):
        t = coarse[i * 40 : i * 40 + 40]
        above = up_y(t)
        u_ref[i * 40 : i * 40 + 40] = (t + above) * 0.375 + (dn_y(t) + up_y(above)) * 0.125
    for i, k in enumerate(ks):
        src1[k] = every_other(u_ref, i * 40, 16)


def inner0_kernel(
    s_in, f_in, ylo, yhi,
    s_ref, c_ref, wx, wy, wz, q_ref, p1, p2, r_ref, src1, mob1,
    t_ref, u_ref,
):
    def own_planes(j, n):
        here, there = pl.ds(j, n), pl.ds(j + X0, n)
        source, code = halo_rows(ylo[here], yhi[here])
        s_ref[there, :32] = s_in[here]
        s_ref[there, 32:] = source
        c_ref[there, :32] = f_in[here].astype(F32)
        c_ref[there, 32:] = code

    blocks(0, 32, 4, own_planes)
    w = (wx, wy, wz, q_ref)
    weights_pass(6, 36, 10, c_ref, w, s_ref, p1, face_code, OUT, True)
    sweep(7, 35, 14, p1, p2, s_ref, w)
    remainder(8, 34, 13, p2, r_ref, s_ref, w)

    halve0(range(2, 14), r_ref, src1, t_ref, u_ref)
    for k in range(16):
        t_ref[k * 40 : k * 40 + 40] = c_ref[2 * k + X0] + c_ref[2 * k + X0 + 1]
    water = dot(t_ref[...], pair_weight(lanes_to_128()), exact=True)
    for k in range(16):
        t = water[k * 40 : k * 40 + 40]
        u_ref[k * 40 : k * 40 + 40] = t + up_y(t)
    for k in range(16):
        mob1[k] = water_to_mobility(every_other(u_ref, k * 40, 16))


def inner0(source, phase, ylo, yhi):
    return call(
        inner0_kernel, "inner0", [kept(*BIG)] * 9 + [kept(16, 16, 128)] * 2,
        [kept(640, 256), kept(640, 128)], 4, source, phase, ylo, yhi,
    )


def lay_rows(out, first, rows):
    for k in range(4):
        out[first + k] = rows[k // 2 * 16 : k // 2 * 16 + 16, k % 2 * 128 : k % 2 * 128 + 128]


def outer0_kernel(
    xlo, xhi, mob1, s_0, c_0, wx_0, wy_0, wz_0, q_0, p1_0, p2_0, r_0, src1_0,
    s_ref, c_ref, wx, wy, wz, q_ref, p1, p2, r_ref, src1, dn1, upw1,
    t_ref, u_ref,
):
    low_x, high_x = edge("gx")
    p1[2] = blank(low_x, xlo[0], 0.0)
    s_ref[3:5] = blank(low_x, xlo[1:3], 0.0)
    c_ref[2:5] = blank(low_x, xlo[3:], OUT)
    s_ref[37:39] = blank(high_x, xhi[:2], 0.0)
    p1[39] = blank(high_x, xhi[2], 0.0)
    c_ref[37:40] = blank(high_x, xhi[3:], OUT)
    w = (wx, wy, wz, q_ref)
    wx[2] = face_code(c_ref[2], c_ref[3])
    wx[35] = face_code(c_ref[35], c_ref[36])
    planes_at((3, 4, 5, 36, 37, 38), weights_plane(c_ref, s_ref, face_code, OUT, True), (*w, p1))
    planes_at((3, 4, 5, 6, 35, 36, 37, 38), sweep_plane(p1, s_ref, w), (p2,))
    planes_at((4, 5, 6, 7, 34, 35, 36, 37), remainder_plane(p2, s_ref, w), (r_ref,))
    halve0((0, 1, 14, 15), r_ref, src1, t_ref, u_ref)
    dn1[:5] = src1[:5]
    dn1[5:11] = mob1[:6]
    upw1[:5] = src1[11:]
    upw1[5:11] = mob1[10:]


def outer0(xlo, xhi, mob1, state):
    return call(
        outer0_kernel, "outer0",
        [kept(*BIG)] * 9 + [kept(16, 16, 128)] + [kept(11, 16, 128)] * 2,
        [kept(160, 256), kept(160, 128)], 4, xlo, xhi, mob1, *state, aliases={3 + k: k for k in range(10)},
    )


def edge_rows_kernel(p, rows_dn, rows_up):
    for k in range(32):
        rows_dn[k : k + 1] = p[X0 + k, 0:1]
        rows_up[k : k + 1] = p[X0 + k, 31:32]


def edge_rows(p2):
    return call(edge_rows_kernel, "edge_rows", [kept(32, 256)] * 2, [], 4, p2)


def pack1_kernel(src, mob, xlo, xhi, rows_dn, rows_up, dn_ref, upw_ref):
    low_x, high_x = edge("gx")
    for rows, out, p_rows in ((slice(0, 8), dn_ref, rows_dn), (slice(8, 16), upw_ref, rows_up)):
        out[0, :8] = jnp.zeros((8, 128), F32)
        out[N1 - 1, :8] = jnp.zeros((8, 128), F32)
        out[1:6, :8] = blank(low_x, xlo[:5, rows], 0.0)
        out[0:6, 8:] = blank(low_x, xlo[5:11, rows], 0.0)
        out[6:22, :8] = src[:, rows]
        out[6:22, 8:] = mob[:, rows]
        out[22:27, :8] = blank(high_x, xhi[:5, rows], 0.0)
        out[22:28, 8:] = blank(high_x, xhi[5:11, rows], 0.0)
        lay_rows(out, N1, p_rows[...])


def pack1(*operands):
    return call(pack1_kernel, "pack1", [kept(N1 + 4, 16, 128)] * 2, [], 4, *operands)


def down1_kernel(
    src, mob, xlo, xhi, ylo, yhi, p0,
    own2, dn2, upw2, s_ref, wx, wy, wz, q_ref, p2,
    m_ref, p1, r_ref, t_ref, u_ref, pk_ref,
):
    low_x, high_x = edge("gx")
    low_y, high_y = edge("gy")
    zero = jnp.zeros((32, 128), F32)
    s_ref[0] = zero
    s_ref[N1 - 1] = zero
    s_ref[1:6, :16] = blank(low_x, xlo[:5], 0.0)
    m_ref[0:6, :16] = blank(low_x, xlo[5:11], 0.0)
    s_ref[6:22, :16] = src[...]
    m_ref[6:22, :16] = mob[...]
    s_ref[22:27, :16] = blank(high_x, xhi[:5], 0.0)
    m_ref[22:28, :16] = blank(high_x, xhi[5:11], 0.0)
    s_ref[:, 16:24] = blank(high_y, yhi[:N1, :8], 0.0)
    m_ref[:, 16:24] = blank(high_y, yhi[:N1, 8:], 0.0)
    s_ref[:, 24:] = blank(low_y, ylo[:N1, :8], 0.0)
    m_ref[:, 24:] = blank(low_y, ylo[:N1, 8:], 0.0)
    w = (wx, wy, wz, q_ref)

    weights_pass(1, N1 - 1, 26, m_ref, w, s_ref, p1, face_mean, 0.0, True)
    sweep(2, N1 - 2, 24, p1, p2, s_ref, w)
    remainder(3, N1 - 3, 22, p2, r_ref, s_ref, w)

    for k, packed in enumerate(halve(12, r_ref, m_ref, t_ref, u_ref, 64, full_dot)):
        pk_ref[k] = packed
    own2[...] = pk_ref[2:10]
    row = iota((8, 128), 0)
    for out, first, plane in ((dn2, 2, X0), (upw2, 0, X0 + 31)):
        for k in range(8):
            h, z = k // 2 * 8, k % 2 * 128
            out[15 + k] = p0[plane, h : h + 8, z : z + 128]
        for k in range(10):
            out[k] = pk_ref[first + k, :8]
        for k in range(5):
            a, b = pk_ref[first + 2 * k, 8:], pk_ref[first + 2 * k + 1, 8:]
            b = jnp.where(row < 4, pltpu.roll(b, 2, 0), pltpu.roll(b, 6, 0))
            out[10 + k] = jnp.where((row < 2) | (row >= 6), a, b)


def down1(*operands):
    return call(
        down1_kernel, "down1", [kept(8, 16, 128)] + [kept(23, 8, 128)] * 2 + [kept(N1, 32, 128)] * 6,
        [kept(N1, 32, 128)] * 3 + [kept(384, 256), kept(384, 128), kept(12, 16, 128)], 6, *operands,
    )


def pack2_kernel(own, xlo, xhi, dn_ref, upw_ref):
    low_x, high_x = edge("gx")
    row = iota((8, 128), 0)
    for a in range(N2 // 4):
        two_dn = two_up = jnp.zeros((8, 128), F32)
        for b in range(4):
            j = 4 * a + b
            if 10 <= j < 18:
                tile, more = own[j - 10, :8], own[j - 10, 8:]
            else:
                flag, halo, k = (low_x, xlo, j) if j < 10 else (high_x, xhi, j - 18)
                tile, more = blank(flag, halo[k], 0.0), blank(flag, halo[10 + k // 2], 0.0)
                if k % 2:
                    more = jnp.where(row < 4, pltpu.roll(more, 6, 0), pltpu.roll(more, 2, 0))
            dn_ref[j] = tile
            upw_ref[j] = tile
            here = (row == 2 * b) | (row == 2 * b + 1)
            two_dn = jnp.where(here, pltpu.roll(more, 2 * b, 0) if b else more, two_dn)
            two_up = jnp.where(here, pltpu.roll(more, 2 * b + 2, 0) if b < 3 else more, two_up)
        dn_ref[N2 + a] = two_dn
        upw_ref[N2 + a] = two_up


def pack2(*operands):
    return call(pack2_kernel, "pack2", [kept(N2 + N2 // 4, 8, 128)] * 2, [], 4, *operands)


def before_kernel(wx0, wy0, wz0, q0, s0, down0_ref, out_ref, pb0):
    w0 = (wx0, wy0, wz0, q0)
    sweep(X0 - 1, X0 + 33, 17, down0_ref, pb0, s0, w0)
    sweep(X0, X0 + 32, 16, pb0, out_ref, s0, w0)


def before(*operands):
    return call(before_kernel, "before", [kept(*BIG)], [kept(*BIG)], 4, *operands)[0]


def base_kernel(
    wx0, wy0, wz0, q0, s0, p_0, plane_lo, plane_hi, rows_lo, rows_hi, sent, base_s, base_r, p_ref, row_ref
):
    del p_0, sent
    low_x, high_x = edge("gx")
    low_y, high_y = edge("gy")
    row8 = iota((8, 256), 0)
    for k in range(8):
        h, z = k // 2 * 8, k % 2 * 128
        p_ref[X0 - 1, h : h + 8, z : z + 128] = blank(low_x, plane_lo[15 + k], 0.0)
        p_ref[X0 + 32, h : h + 8, z : z + 128] = blank(high_x, plane_hi[15 + k], 0.0)
    for k in range(4):
        h, z = k // 2 * 16, k % 2 * 128
        row_ref[0, h : h + 16, z : z + 128] = blank(high_y, rows_hi[N1 + k], 0.0)
        row_ref[1, h : h + 16, z : z + 128] = blank(low_y, rows_lo[N1 + k], 0.0)

    def halo(j, n):
        for i in range(n):
            above = row_ref[0, pl.ds(j + i, 1)]
            below = row_ref[1, pl.ds(j + i, 1)]
            p_ref[j + i + X0, 32:] = jnp.where(row8 == 0, above, jnp.where(row8 == 7, below, 0.0))

    blocks(0, 32, 8, halo)
    p_ref[X0 - 1, 32:] = jnp.zeros((8, 256), F32)
    p_ref[X0 + 32, 32:] = jnp.zeros((8, 256), F32)
    w0 = (wx0, wy0, wz0, q0)

    def plane(j):
        p = p_ref[j + X0]
        dp = (OMEGA / q0[j + X0]) * p
        return dp[:32], (s0[j + X0] + flow(j + X0, p, p_ref, w0) - dp)[:32]

    planes(0, 32, 8, plane, (base_s, base_r))


def base(*operands):
    out = [kept(32, 32, 256)] * 2 + [kept(*BIG)]
    return call(base_kernel, "base", out, [kept(2, 32, 256)], 4, *operands, aliases={5: 2})[:2]


def up_kernel(
    ext, ylo, yhi, s1, wx1, wy1, wz1, q1, down1_ref,
    wx0, wy0, wz0, q0, base_s, base_r,
    scaled, residual,
    pa0, pb0,
    pa1, pb1,
    s2, m2, wx2, wy2, wz2, q2, pa2, pb2, r2,
    s3, m3, wx3, wy3, wz3, q3, pa3, pb3,
    t_ref, u_ref, v_ref, rise_lo, rise_hi, out_a, out_b, sems,
):
    low_y, high_y = edge("gy")

    lane8, sub8 = iota((8, 128), 1), iota((8, 128), 0)

    def put(j, rows, packed):
        s2[j, rows] = packed
        m2[j, rows] = jnp.where(lane8 < 64, pltpu.roll(packed, 64, 1), 0.0)

    for j in range(N2):
        a, b = divmod(j, 4)
        hi, lo = yhi[N2 + a], ylo[N2 + a]
        hi = pltpu.roll(hi, 8 - 2 * b, 0) if b else hi
        lo = pltpu.roll(lo, 6 - 2 * b, 0) if b < 3 else lo
        put(j, slice(0, 8), ext[j])
        put(j, slice(8, 16), blank(high_y, yhi[j], 0.0))
        put(j, slice(16, 24), jnp.where((sub8 < 4) & ~high_y, hi, jnp.where((sub8 >= 4) & ~low_y, lo, 0.0)))
        put(j, slice(24, 32), blank(low_y, ylo[j], 0.0))

    w2 = (wx2, wy2, wz2, q2)

    weights_pass(1, N2 - 1, 26, m2, w2, s2, pa2, face_mean, 0.0, False)
    sweep(2, N2 - 2, 24, pa2, pb2, s2, w2)
    remainder(3, N2 - 3, 22, pb2, r2, s2, w2)

    lane16 = iota((16, 128), 1)
    for k, packed in enumerate(halve(12, r2, m2, t_ref, u_ref, 32, dot)):
        s3[k] = packed
        m3[k] = jnp.where(lane16 < 64, pltpu.roll(packed, 64, 1), 0.0)
    w3 = (wx3, wy3, wz3, q3)

    weights_pass(1, N3 - 1, 10, m3, w3, s3, pa3, face_mean, 0.0, False)
    sweep(2, N3 - 2, 8, pa3, pb3, s3, w3)

    lane_in, lane_out = iota((128, 128), 0), iota((128, 128), 1)
    double = pair_weight(lane_out - 2 * lane_in)
    for k in range(8):
        v_ref[k * 16 : k * 16 + 16] = pb3[k + 2]
    rise = dot(v_ref[:128], jnp.where(lane_in < 32, double, 0.0))
    for k in range(8):
        twice(u_ref, k * 32, rise[k * 16 : k * 16 + 16])
    for k in range(8):
        for j in (2 * k + 6, 2 * k + 7):
            pb2[j] = pb2[j] + u_ref[k * 32 : k * 32 + 32]
    sweep(7, 21, 14, pb2, pa2, s2, w2)
    sweep(8, 20, 12, pa2, pb2, s2, w2)

    for k in range(12):
        v_ref[k * 16 : k * 16 + 8] = pb2[k + 8, :8]
        v_ref[k * 16 + 8 : k * 16 + 16] = jnp.where(sub8 < 4, pb2[k + 8, 8:16], pb2[k + 8, 24:])
    rise = dot(v_ref[:192], double)
    for k in range(12):
        twice(u_ref, k * 32, rise[k * 16 : k * 16 + 16])
    for k in range(12):
        for j in (2 * k + 2, 2 * k + 3):
            pa1[j] = down1_ref[j] + u_ref[k * 32 : k * 32 + 32]
    w1 = (wx1, wy1, wz1, q1)
    sweep(3, 25, 22, pa1, pb1, s1, w1)
    sweep(4, 24, 20, pb1, pa1, s1, w1)

    for k in range(20):
        v_ref[k * 24 : k * 24 + 16] = pa1[k + 4, :16]
        v_ref[k * 24 + 16 : k * 24 + 24] = jnp.where(
            sub8 < 2, pa1[k + 4, 16:24], pltpu.roll(pa1[k + 4, 24:], 4, 0)
        )
    for z, out in ((0, rise_lo), (128, rise_hi)):
        double = pair_weight(lane_out + z - 2 * lane_in)
        rise = dot(v_ref[...], double)
        for k in range(20):
            twice(out, k * 48, rise[k * 24 : k * 24 + 24])

    def rise_at(k):
        here = pl.ds(k * 48 if isinstance(k, int) else pl.multiple_of(k * 48, 8), 40)
        return jnp.concatenate([rise_lo[here], rise_hi[here]], 1)

    w0 = (wx0, wy0, wz0, q0)

    def first_pairs(k0, n):
        results = []
        for i in range(n):
            k = k0 + i
            low, e, high = rise_at(k - 1), rise_at(k), rise_at(k + 1)
            e_up_y, e_up_z = up_y(e), up_z(e)
            for j, x_low, x_high in ((2 * k + 1, low, e), (2 * k + 2, e, high)):
                wy, wz = wy0[j], wz0[j]
                along_x = wx0[j] * x_high + wx0[j - 1] * x_low
                along_y = wy * e_up_y + dn_y(wy * e)
                along_z = wz * e_up_z + dn_z(wz * e)
                results.append((j, KEEP * e + q0[j] * (along_x + along_y + along_z)))
        for j, value in results:
            pb0[j] = value

    blocks(1, 19, 6, first_pairs)
    sweep(4, N0 - 4, 17, pb0, pa0, None, w0)

    def out_copies(k, j):
        here = pl.ds(j, 8)
        return (
            pltpu.make_async_copy(out_a.at[here], scaled.at[here], sems.at[0, k]),
            pltpu.make_async_copy(out_b.at[here], residual.at[here], sems.at[1, k]),
        )

    def last(k, carry):
        j = k * 8
        results = []
        for i in range(8):
            p = pa0[j + i + X0]
            dp = (OMEGA / q0[j + i + X0]) * p
            a = base_s[j + i] + dp[:32]
            results.append((a, base_r[j + i] + (flow(j + i + X0, p, pa0, w0) - dp)[:32]))
        for i, (a, b) in enumerate(results):
            out_a[j + i] = a
            out_b[j + i] = b
        for copy in out_copies(k, j):
            copy.start()
        return carry

    lax.fori_loop(0, 4, last, 0)
    for k in range(4):
        for copy in out_copies(k, k * 8):
            copy.wait()


def way_up(*operands):
    shape = jax.ShapeDtypeStruct((32, 32, 256), F32)
    buf = lambda count, *shape: [kept(*shape)] * count
    scratch = (
        buf(2, *BIG)
        + buf(2, N1, 32, 128)
        + buf(9, N2, 32, 128)
        + buf(8, N3, 16, 128)
        + buf(1, 384, 256)
        + buf(1, 384, 128)
        + buf(1, 480, 128)
        + buf(2, 960, 128)
        + buf(2, 32, 32, 256)
        + [pltpu.SemaphoreType.DMA((2, 4))]
    )
    hbm = pl.BlockSpec(memory_space=pl.ANY)
    return call(up_kernel, "way_up", [shape] * 2, scratch, 20, *operands, out_specs=[hbm] * 2)


def shift(a, axis, step):
    count = lax.axis_size(axis)
    return lax.ppermute(a, axis, [(i, (i + step) % count) for i in range(count)])


def both(to_low, to_high, axis):
    return shift(to_high, axis, 1), shift(to_low, axis, -1)


def shards(source, phase):
    dn0, up0 = send_rows(source, phase)
    ylo, yhi = both(dn0, up0, "gy")
    source, phase = load(source, phase, dn0)
    msg = [kept(6, 40, 256)] * 2
    dn0, up0 = call(send_planes_kernel, "send_planes", msg, [], 4, source, phase, ylo, yhi)
    xlo, xhi = both(dn0, up0, "gx")
    *state, mob1 = inner0(source, phase, ylo, yhi)
    s0, _, wx0, wy0, wz0, q0, _, p0, _, src1, dn1, up1 = outer0(xlo, xhi, mob1, state)
    weights = (wx0, wy0, wz0, q0)
    xlo1, xhi1 = both(dn1, up1, "gx")
    p0 = before(*weights, s0, p0)
    ylo1, yhi1 = both(*pack1(src1, mob1, xlo1, xhi1, *edge_rows(p0)), "gy")
    own2, dn2, up2, *level1 = down1(src1, mob1, xlo1, xhi1, ylo1, yhi1, p0)
    xlo, xhi = both(dn2, up2, "gx")
    ext, ext_up = pack2(own2, xlo, xhi)
    ylo, yhi = both(ext, ext_up, "gy")
    based = base(*weights, s0, p0, xlo, xhi, ylo1, yhi1, ext)
    return tuple(way_up(ext, ylo, yhi, *level1, *weights, *based))


def solution(mesh):
    spec = P("gx", "gy", None)
    return jax.shard_map(shards, mesh=mesh, in_specs=(spec, spec), out_specs=(spec, spec), check_vma=False)
```

```python
import jax
import jax.numpy as jnp
from jax import lax
from jax.experimental import pallas as pl
from jax.experimental.pallas import tpu as pltpu
from jax.sharding import PartitionSpec as P

OMEGA = 0.8
KEEP = 0.2
WATER = 0.001
MIXED = 2.0 * WATER / (1.0 + WATER)
OUT = 0.25
F32 = jnp.float32
MIB = 1024 * 1024


def up_y(a):
    return pltpu.roll(a, a.shape[-2] - 1, a.ndim - 2)


def dn_y(a):
    return pltpu.roll(a, 1, a.ndim - 2)


def up_z(a):
    return pltpu.roll(a, a.shape[-1] - 1, a.ndim - 1)


def dn_z(a):
    return pltpu.roll(a, 1, a.ndim - 1)


def iota(shape, dim):
    return lax.broadcasted_iota(jnp.int32, shape, dim)


def ring(row, cut, rows):
    return jnp.where(row < cut, row, row - rows)


def restrict_weight(offset):
    near = (offset == 0) | (offset == 1)
    far = (offset == -1) | (offset == 2)
    return jnp.where(near, 0.375, jnp.where(far, 0.125, 0.0)).astype(F32)


def pair_weight(offset):
    return jnp.where((offset == 0) | (offset == 1), 1.0, 0.0).astype(F32)


def dot(a, b, exact=False):
    high, b = a.astype(jnp.bfloat16), b.astype(jnp.bfloat16)
    if exact:
        return jnp.dot(high, b, preferred_element_type=F32)
    low = (a - high.astype(F32)).astype(jnp.bfloat16)
    if a.shape[1] == 128:
        both = jnp.concatenate([high, low], 1)
        return jnp.dot(both, jnp.concatenate([b, b], 0), preferred_element_type=F32)
    return jnp.dot(high, b, preferred_element_type=F32) + jnp.dot(low, b, preferred_element_type=F32)


def full_dot(a, b):
    return jnp.dot(a, b, precision=lax.Precision.HIGHEST, preferred_element_type=F32)


def face_code(a, b):
    s = a + b
    return jnp.where(s < 0.75, 1.0, jnp.where(s < 1.1, MIXED, WATER)).astype(F32)


def face_mean(a, b):
    product = a * b
    return jnp.where(product > 0.0, 2.0 * product / (a + b), jnp.maximum(a, b))


def blocks(lo, hi, size, work):
    count, rest = divmod(hi - lo, size)
    if count == 1:
        work(lo, size)
    elif count:

        def body(i, carry):
            work(lo + i * size, size)
            return carry

        lax.fori_loop(0, count, body, 0)
    if rest:
        work(hi - rest, rest)


def planes(lo, hi, size, plane, refs):
    def work(j, n):
        results = [plane(j + i) for i in range(n)]
        for i, values in enumerate(results):
            for ref, value in zip(refs, values):
                ref[j + i] = value

    blocks(lo, hi, size, work)


def planes_at(js, plane, refs):
    results = [plane(j) for j in js]
    for j, values in zip(js, results):
        for ref, value in zip(refs, values):
            ref[j] = value


def weights_at(m_low, m, m_high, face, outside, full):
    lane = iota(m.shape, m.ndim - 1)
    last = m.shape[-1] - 1
    wx, wx_low = face(m, m_high), face(m_low, m)
    wy = face(m, up_y(m))
    m_up = up_z(m)
    if full:
        m_up = jnp.where(lane == last, outside, m_up)
    wz = face(m, m_up)
    wz_low = dn_z(wz)
    if full:
        wz_low = jnp.where(lane == 0, face(m, jnp.full_like(m, outside)), wz_low)
    d = (wx + wx_low) + (wy + dn_y(wy)) + (wz + wz_low)
    q = jnp.where(m != outside, OMEGA / d, 0.0)
    if full:
        wz = jnp.where(lane == last, 0.0, wz)
    return wx, wy, wz, q


def weights_plane(m_ref, s_ref, face, outside, full):
    def plane(j):
        wx, wy, wz, q = weights_at(m_ref[j - 1], m_ref[j], m_ref[j + 1], face, outside, full)
        return wx, wy, wz, q, q * s_ref[j]

    return plane


def weights_pass(lo, hi, size, m_ref, w, s_ref, p_ref, face, outside, full):
    w[0][lo - 1] = face(m_ref[lo - 1], m_ref[lo])
    planes(lo, hi, size, weights_plane(m_ref, s_ref, face, outside, full), (*w, p_ref))


def flow(j, p, p_ref, w):
    wx_ref, wy_ref, wz_ref = w[:3]
    wy, wz = wy_ref[j], wz_ref[j]
    along_x = wx_ref[j] * p_ref[j + 1] + wx_ref[j - 1] * p_ref[j - 1]
    along_y = wy * up_y(p) + dn_y(wy * p)
    along_z = wz * up_z(p) + dn_z(wz * p)
    return along_x + along_y + along_z


def sweep_plane(p_ref, s_ref, w):
    def plane(j):
        p = p_ref[j]
        total = flow(j, p, p_ref, w)
        return (KEEP * p + w[3][j] * (total if s_ref is None else s_ref[j] + total),)

    return plane


def sweep(lo, hi, size, p_ref, out_ref, s_ref, w):
    planes(lo, hi, size, sweep_plane(p_ref, s_ref, w), (out_ref,))


def remainder_plane(p_ref, s_ref, w):
    def plane(j):
        p, q = p_ref[j], w[3][j]
        r = s_ref[j] + flow(j, p, p_ref, w) - (OMEGA / q) * p
        return (jnp.where(q > 0.0, r, 0.0),)

    return plane


def remainder(lo, hi, size, p_ref, out_ref, s_ref, w):
    planes(lo, hi, size, remainder_plane(p_ref, s_ref, w), (out_ref,))


def halving(valid):
    lane_in, lane_out = iota((256, 128), 0), iota((256, 128), 1)
    down = jnp.where((lane_in < 128) & (lane_out < valid), restrict_weight(lane_in - 2 * lane_out), 0.0)
    return down + jnp.where(lane_in >= 128, pair_weight(lane_in - 2 * lane_out), 0.0)


def halve_rows(t):
    above = up_y(t)
    near, far = t + above, dn_y(t) + up_y(above)
    return jnp.where(iota(t.shape, 1) < 64, near * 0.375 + far * 0.125, near)


def every_other(ref, first, count):
    return ref[pl.ds(first, count, stride=2)]


def twice(ref, first, value):
    count = value.shape[0]
    ref[pl.ds(first, count, stride=2)] = value
    ref[pl.ds(first + 1, count, stride=2)] = value


def halve(count, r_ref, m_ref, t_ref, u_ref, valid, product):
    for k in range(count):
        rows = slice(k * 32, k * 32 + 32)
        t_ref[rows, :128] = restrict_x(r_ref, 2 * k + 1) if 1 <= k < count - 1 else jnp.zeros((32, 128), F32)
        t_ref[rows, 128:] = (m_ref[2 * k + 2] + m_ref[2 * k + 3]) * (0.25 * 0.125)
    packed = product(t_ref[...], halving(valid))
    for k in range(count):
        u_ref[k * 32 : k * 32 + 32] = halve_rows(packed[k * 32 : k * 32 + 32])
    return [every_other(u_ref, k * 32, 16) for k in range(count)]


def restrict_x(r_ref, j):
    return (r_ref[j] + r_ref[j + 3]) * 0.125 + (r_ref[j + 1] + r_ref[j + 2]) * 0.375


def edge(axis):
    i = lax.axis_index(axis)
    return i == 0, i == lax.axis_size(axis) - 1


def blank(flag, value, other):
    return jnp.where(flag, other, value)


X0 = 5
N0 = 32 + 2 * X0
N1 = 28
N2 = 28
N3 = 12
BIG = (N0, 40, 256)
VM = pl.BlockSpec(memory_space=pltpu.VMEM)


def call(kernel, name, out_shape, scratch, limit, *operands, aliases=None, in_specs=None, out_specs=None):
    return pl.pallas_call(
        kernel,
        in_specs=[VM] * len(operands) if in_specs is None else in_specs,
        out_specs=[VM] * len(out_shape) if out_specs is None else out_specs,
        out_shape=out_shape,
        scratch_shapes=scratch,
        input_output_aliases=aliases or {},
        compiler_params=pltpu.CompilerParams(vmem_limit_bytes=limit * MIB),
        name=name,
    )(*operands)


def kept(*shape):
    return pltpu.VMEM(shape, F32)


def send_rows_kernel(s_hbm, f_hbm, dn_ref, upw_ref, s_lo, s_hi, f_lo, f_hi, sems):
    parts = ((s_hbm, 0, s_lo), (f_hbm, 0, f_lo), (s_hbm, 24, s_hi), (f_hbm, 24, f_hi))
    copies = [
        pltpu.make_async_copy(ref.at[:, pl.ds(first, 8)], part, sems.at[k])
        for k, (ref, first, part) in enumerate(parts)
    ]
    for copy in copies:
        copy.start()
    for copy in copies:
        copy.wait()
    above = iota((8, 256), 0) < 4

    def work(j, n):
        here = pl.ds(j, n)
        dn_ref[here] = jnp.where(above, s_lo[here], pltpu.roll(f_lo[here].astype(F32), 4, 1))
        upw_ref[here] = jnp.where(above, pltpu.roll(f_hi[here].astype(F32), 4, 1), s_hi[here])

    blocks(0, 32, 8, work)


def send_rows(source, phase):
    part = (32, 8, 256)
    scratch = [kept(*part)] * 2 + [pltpu.VMEM(part, jnp.int32)] * 2 + [pltpu.SemaphoreType.DMA((4,))]
    hbm = [pl.BlockSpec(memory_space=pltpu.HBM)] * 2
    operands = [pltpu.with_memory_space_constraint(x, pltpu.HBM) for x in (source, phase)]
    return call(send_rows_kernel, "send_rows", [kept(*part)] * 2, scratch, 4, *operands, in_specs=hbm)


def load_kernel(s_hbm, f_hbm, sent, s_ref, f_ref, sems):
    del sent
    copies = [
        pltpu.make_async_copy(a, b, sems.at[k]) for k, (a, b) in enumerate(((s_hbm, s_ref), (f_hbm, f_ref)))
    ]
    for copy in copies:
        copy.start()
    for copy in copies:
        copy.wait()


def load(source, phase, sent):
    any_space = pl.BlockSpec(memory_space=pl.ANY)
    hbm = [pl.BlockSpec(memory_space=pltpu.HBM)] * 2
    operands = [pltpu.with_memory_space_constraint(x, pltpu.HBM) for x in (source, phase)]
    out = [kept(32, 32, 256), pltpu.VMEM((32, 32, 256), jnp.int32)]
    scratch = [pltpu.SemaphoreType.DMA((2,))]
    return call(load_kernel, "load", out, scratch, 4, *operands, sent, in_specs=[*hbm, any_space])


def halo_rows(lo, hi):
    low_y, high_y = edge("gy")
    above = iota((8, 256), 0) < 4
    outer = (above & high_y) | (~above & low_y)
    source = jnp.where(outer, 0.0, jnp.where(above, hi, lo))
    code = jnp.where(outer, OUT, pltpu.roll(jnp.where(above, lo, hi), 4, lo.ndim - 2))
    return source, code


def send_planes_kernel(s_in, f_in, ylo, yhi, ahead, dn_ref, upw_ref):
    del ahead
    for first, out_ref, last, at in ((0, dn_ref, 2, (0, 1, 2)), (28, upw_ref, 1, (None, 0, 1, 2))):
        block = slice(first, first + 4)
        halo_source, halo_code = halo_rows(ylo[block], yhi[block])
        code = [jnp.concatenate([f_in[first + k].astype(F32), halo_code[k]], 0) for k in range(4)]
        source = [jnp.concatenate([s_in[first + k], halo_source[k]], 0) for k in range(4)]
        q = weights_at(code[last - 1], code[last], code[last + 1], face_code, OUT, True)[3]
        source[last] = q * source[last]
        for k, place in enumerate(at):
            if place is not None:
                out_ref[place] = source[k]
                out_ref[place + 3] = code[k]


def water_to_mobility(n):
    return 0.25 * ((8.0 - n) * 0.125 + n * (0.125 * WATER))


def lanes_to_128():
    return iota((256, 128), 0) - 2 * iota((256, 128), 1)


def mobility1_kernel(f_in, mob1, t_ref, u_ref):
    for k in range(16):
        t_ref[k * 32 : k * 32 + 32] = (f_in[2 * k] + f_in[2 * k + 1]).astype(F32)
    water = dot(t_ref[...], pair_weight(lanes_to_128()), exact=True)
    for k in range(16):
        t = water[k * 32 : k * 32 + 32]
        u_ref[k * 32 : k * 32 + 32] = t + up_y(t)
    for k in range(16):
        mob1[k] = water_to_mobility(every_other(u_ref, k * 32, 16))


def mobility1(phase):
    return call(
        mobility1_kernel, "mobility1", [kept(16, 16, 128)], [kept(512, 256), kept(512, 128)], 4, phase
    )[0]


def halve0(ks, r_ref, src1, t_ref, u_ref):
    for i, k in enumerate(ks):
        t_ref[i * 40 : i * 40 + 40] = restrict_x(r_ref, 2 * k + 4)
    coarse = dot(t_ref[: len(ks) * 40], restrict_weight(lanes_to_128()))
    for i in range(len(ks)):
        t = coarse[i * 40 : i * 40 + 40]
        above = up_y(t)
        u_ref[i * 40 : i * 40 + 40] = (t + above) * 0.375 + (dn_y(t) + up_y(above)) * 0.125
    for i, k in enumerate(ks):
        src1[k] = every_other(u_ref, i * 40, 16)


def inner0_kernel(
    s_in, f_in, ylo, yhi,
    s_ref, c_ref, wx, wy, wz, q_ref, p1, p2, r_ref, src1,
    t_ref, u_ref,
):
    def own_planes(j, n):
        here, there = pl.ds(j, n), pl.ds(j + X0, n)
        source, code = halo_rows(ylo[here], yhi[here])
        s_ref[there, :32] = s_in[here]
        s_ref[there, 32:] = source
        c_ref[there, :32] = f_in[here].astype(F32)
        c_ref[there, 32:] = code

    blocks(0, 32, 4, own_planes)
    w = (wx, wy, wz, q_ref)
    weights_pass(6, 36, 10, c_ref, w, s_ref, p1, face_code, OUT, True)
    sweep(7, 35, 14, p1, p2, s_ref, w)
    remainder(8, 34, 13, p2, r_ref, s_ref, w)

    halve0(range(2, 14), r_ref, src1, t_ref, u_ref)


def inner0(source, phase, ylo, yhi):
    return call(
        inner0_kernel, "inner0", [kept(*BIG)] * 9 + [kept(16, 16, 128)],
        [kept(480, 256), kept(480, 128)], 4, source, phase, ylo, yhi,
    )


def lay_rows(out, first, rows):
    for k in range(4):
        out[first + k] = rows[k // 2 * 16 : k // 2 * 16 + 16, k % 2 * 128 : k % 2 * 128 + 128]


def outer0_kernel(
    xlo, xhi, mob1, s_0, c_0, wx_0, wy_0, wz_0, q_0, p1_0, p2_0, r_0, src1_0,
    s_ref, c_ref, wx, wy, wz, q_ref, p1, p2, r_ref, src1, dn1, upw1,
    t_ref, u_ref,
):
    low_x, high_x = edge("gx")
    p1[2] = blank(low_x, xlo[0], 0.0)
    s_ref[3:5] = blank(low_x, xlo[1:3], 0.0)
    c_ref[2:5] = blank(low_x, xlo[3:], OUT)
    s_ref[37:39] = blank(high_x, xhi[:2], 0.0)
    p1[39] = blank(high_x, xhi[2], 0.0)
    c_ref[37:40] = blank(high_x, xhi[3:], OUT)
    w = (wx, wy, wz, q_ref)
    wx[2] = face_code(c_ref[2], c_ref[3])
    wx[35] = face_code(c_ref[35], c_ref[36])
    planes_at((3, 4, 5, 36, 37, 38), weights_plane(c_ref, s_ref, face_code, OUT, True), (*w, p1))
    planes_at((3, 4, 5, 6, 35, 36, 37, 38), sweep_plane(p1, s_ref, w), (p2,))
    planes_at((4, 5, 6, 7, 34, 35, 36, 37), remainder_plane(p2, s_ref, w), (r_ref,))
    halve0((0, 1, 14, 15), r_ref, src1, t_ref, u_ref)
    dn1[:5] = src1[:5]
    dn1[5:11] = mob1[:6]
    upw1[:5] = src1[11:]
    upw1[5:11] = mob1[10:]


def outer0(xlo, xhi, mob1, state):
    return call(
        outer0_kernel, "outer0",
        [kept(*BIG)] * 9 + [kept(16, 16, 128)] + [kept(11, 16, 128)] * 2,
        [kept(160, 256), kept(160, 128)], 4, xlo, xhi, mob1, *state, aliases={3 + k: k for k in range(10)},
    )


def edge_rows_kernel(p, rows_dn, rows_up):
    for k in range(32):
        rows_dn[k : k + 1] = p[X0 + k, 0:1]
        rows_up[k : k + 1] = p[X0 + k, 31:32]


def edge_rows(p2):
    return call(edge_rows_kernel, "edge_rows", [kept(32, 256)] * 2, [], 4, p2)


def pack1_kernel(src, mob, xlo, xhi, rows_dn, rows_up, dn_ref, upw_ref):
    low_x, high_x = edge("gx")
    for rows, out, p_rows in ((slice(0, 8), dn_ref, rows_dn), (slice(8, 16), upw_ref, rows_up)):
        out[0, :8] = jnp.zeros((8, 128), F32)
        out[N1 - 1, :8] = jnp.zeros((8, 128), F32)
        out[1:6, :8] = blank(low_x, xlo[:5, rows], 0.0)
        out[0:6, 8:] = blank(low_x, xlo[5:11, rows], 0.0)
        out[6:22, :8] = src[:, rows]
        out[6:22, 8:] = mob[:, rows]
        out[22:27, :8] = blank(high_x, xhi[:5, rows], 0.0)
        out[22:28, 8:] = blank(high_x, xhi[5:11, rows], 0.0)
        lay_rows(out, N1, p_rows[...])


def pack1(*operands):
    return call(pack1_kernel, "pack1", [kept(N1 + 4, 16, 128)] * 2, [], 4, *operands)


def down1_kernel(
    src, mob, xlo, xhi, ylo, yhi, p0,
    own2, dn2, upw2, s_ref, wx, wy, wz, q_ref, p2,
    m_ref, p1, r_ref, t_ref, u_ref, pk_ref,
):
    low_x, high_x = edge("gx")
    low_y, high_y = edge("gy")
    zero = jnp.zeros((32, 128), F32)
    s_ref[0] = zero
    s_ref[N1 - 1] = zero
    s_ref[1:6, :16] = blank(low_x, xlo[:5], 0.0)
    m_ref[0:6, :16] = blank(low_x, xlo[5:11], 0.0)
    s_ref[6:22, :16] = src[...]
    m_ref[6:22, :16] = mob[...]
    s_ref[22:27, :16] = blank(high_x, xhi[:5], 0.0)
    m_ref[22:28, :16] = blank(high_x, xhi[5:11], 0.0)
    s_ref[:, 16:24] = blank(high_y, yhi[:N1, :8], 0.0)
    m_ref[:, 16:24] = blank(high_y, yhi[:N1, 8:], 0.0)
    s_ref[:, 24:] = blank(low_y, ylo[:N1, :8], 0.0)
    m_ref[:, 24:] = blank(low_y, ylo[:N1, 8:], 0.0)
    w = (wx, wy, wz, q_ref)

    weights_pass(1, N1 - 1, 26, m_ref, w, s_ref, p1, face_mean, 0.0, True)
    sweep(2, N1 - 2, 24, p1, p2, s_ref, w)
    remainder(3, N1 - 3, 22, p2, r_ref, s_ref, w)

    for k, packed in enumerate(halve(12, r_ref, m_ref, t_ref, u_ref, 64, full_dot)):
        pk_ref[k] = packed
    own2[...] = pk_ref[2:10]
    row = iota((8, 128), 0)
    for out, first, plane in ((dn2, 2, X0), (upw2, 0, X0 + 31)):
        for k in range(8):
            h, z = k // 2 * 8, k % 2 * 128
            out[15 + k] = p0[plane, h : h + 8, z : z + 128]
        for k in range(10):
            out[k] = pk_ref[first + k, :8]
        for k in range(5):
            a, b = pk_ref[first + 2 * k, 8:], pk_ref[first + 2 * k + 1, 8:]
            b = jnp.where(row < 4, pltpu.roll(b, 2, 0), pltpu.roll(b, 6, 0))
            out[10 + k] = jnp.where((row < 2) | (row >= 6), a, b)


def down1(*operands):
    return call(
        down1_kernel, "down1", [kept(8, 16, 128)] + [kept(23, 8, 128)] * 2 + [kept(N1, 32, 128)] * 6,
        [kept(N1, 32, 128)] * 3 + [kept(384, 256), kept(384, 128), kept(12, 16, 128)], 6, *operands,
    )


def pack2_kernel(own, xlo, xhi, dn_ref, upw_ref):
    low_x, high_x = edge("gx")
    row = iota((8, 128), 0)
    for a in range(N2 // 4):
        two_dn = two_up = jnp.zeros((8, 128), F32)
        for b in range(4):
            j = 4 * a + b
            if 10 <= j < 18:
                tile, more = own[j - 10, :8], own[j - 10, 8:]
            else:
                flag, halo, k = (low_x, xlo, j) if j < 10 else (high_x, xhi, j - 18)
                tile, more = blank(flag, halo[k], 0.0), blank(flag, halo[10 + k // 2], 0.0)
                if k % 2:
                    more = jnp.where(row < 4, pltpu.roll(more, 6, 0), pltpu.roll(more, 2, 0))
            dn_ref[j] = tile
            upw_ref[j] = tile
            here = (row == 2 * b) | (row == 2 * b + 1)
            two_dn = jnp.where(here, pltpu.roll(more, 2 * b, 0) if b else more, two_dn)
            two_up = jnp.where(here, pltpu.roll(more, 2 * b + 2, 0) if b < 3 else more, two_up)
        dn_ref[N2 + a] = two_dn
        upw_ref[N2 + a] = two_up


def pack2(*operands):
    return call(pack2_kernel, "pack2", [kept(N2 + N2 // 4, 8, 128)] * 2, [], 4, *operands)


def before_kernel(wx0, wy0, wz0, q0, s0, down0_ref, out_ref, pb0):
    w0 = (wx0, wy0, wz0, q0)
    sweep(X0 - 1, X0 + 33, 17, down0_ref, pb0, s0, w0)
    sweep(X0, X0 + 32, 16, pb0, out_ref, s0, w0)


def before(*operands):
    return call(before_kernel, "before", [kept(*BIG)], [kept(*BIG)], 4, *operands)[0]


def base_kernel(
    wx0, wy0, wz0, q0, s0, p_0, plane_lo, plane_hi, rows_lo, rows_hi, sent, base_s, base_r, p_ref, row_ref
):
    del p_0, sent
    low_x, high_x = edge("gx")
    low_y, high_y = edge("gy")
    row8 = iota((8, 256), 0)
    for k in range(8):
        h, z = k // 2 * 8, k % 2 * 128
        p_ref[X0 - 1, h : h + 8, z : z + 128] = blank(low_x, plane_lo[15 + k], 0.0)
        p_ref[X0 + 32, h : h + 8, z : z + 128] = blank(high_x, plane_hi[15 + k], 0.0)
    for k in range(4):
        h, z = k // 2 * 16, k % 2 * 128
        row_ref[0, h : h + 16, z : z + 128] = blank(high_y, rows_hi[N1 + k], 0.0)
        row_ref[1, h : h + 16, z : z + 128] = blank(low_y, rows_lo[N1 + k], 0.0)

    def halo(j, n):
        for i in range(n):
            above = row_ref[0, pl.ds(j + i, 1)]
            below = row_ref[1, pl.ds(j + i, 1)]
            p_ref[j + i + X0, 32:] = jnp.where(row8 == 0, above, jnp.where(row8 == 7, below, 0.0))

    blocks(0, 32, 8, halo)
    p_ref[X0 - 1, 32:] = jnp.zeros((8, 256), F32)
    p_ref[X0 + 32, 32:] = jnp.zeros((8, 256), F32)
    w0 = (wx0, wy0, wz0, q0)

    def plane(j):
        p = p_ref[j + X0]
        dp = (OMEGA / q0[j + X0]) * p
        return dp[:32], (s0[j + X0] + flow(j + X0, p, p_ref, w0) - dp)[:32]

    planes(0, 32, 8, plane, (base_s, base_r))


def base(*operands):
    out = [kept(32, 32, 256)] * 2 + [kept(*BIG)]
    return call(base_kernel, "base", out, [kept(2, 32, 256)], 4, *operands, aliases={5: 2})[:2]


def up_kernel(
    ext, ylo, yhi, s1, wx1, wy1, wz1, q1, down1_ref,
    wx0, wy0, wz0, q0, base_s, base_r,
    scaled, residual,
    pa0, pb0,
    pa1, pb1,
    s2, m2, wx2, wy2, wz2, q2, pa2, pb2, r2,
    s3, m3, wx3, wy3, wz3, q3, pa3, pb3,
    t_ref, u_ref, v_ref, rise_lo, rise_hi, out_a, out_b, sems,
):
    low_y, high_y = edge("gy")

    lane8, sub8 = iota((8, 128), 1), iota((8, 128), 0)

    def put(j, rows, packed):
        s2[j, rows] = packed
        m2[j, rows] = jnp.where(lane8 < 64, pltpu.roll(packed, 64, 1), 0.0)

    for j in range(N2):
        a, b = divmod(j, 4)
        hi, lo = yhi[N2 + a], ylo[N2 + a]
        hi = pltpu.roll(hi, 8 - 2 * b, 0) if b else hi
        lo = pltpu.roll(lo, 6 - 2 * b, 0) if b < 3 else lo
        put(j, slice(0, 8), ext[j])
        put(j, slice(8, 16), blank(high_y, yhi[j], 0.0))
        put(j, slice(16, 24), jnp.where((sub8 < 4) & ~high_y, hi, jnp.where((sub8 >= 4) & ~low_y, lo, 0.0)))
        put(j, slice(24, 32), blank(low_y, ylo[j], 0.0))

    w2 = (wx2, wy2, wz2, q2)

    weights_pass(1, N2 - 1, 26, m2, w2, s2, pa2, face_mean, 0.0, False)
    sweep(2, N2 - 2, 24, pa2, pb2, s2, w2)
    remainder(3, N2 - 3, 22, pb2, r2, s2, w2)

    lane16 = iota((16, 128), 1)
    for k, packed in enumerate(halve(12, r2, m2, t_ref, u_ref, 32, dot)):
        s3[k] = packed
        m3[k] = jnp.where(lane16 < 64, pltpu.roll(packed, 64, 1), 0.0)
    w3 = (wx3, wy3, wz3, q3)

    weights_pass(1, N3 - 1, 10, m3, w3, s3, pa3, face_mean, 0.0, False)
    sweep(2, N3 - 2, 8, pa3, pb3, s3, w3)

    lane_in, lane_out = iota((128, 128), 0), iota((128, 128), 1)
    double = pair_weight(lane_out - 2 * lane_in)
    for k in range(8):
        v_ref[k * 16 : k * 16 + 16] = pb3[k + 2]
    rise = dot(v_ref[:128], jnp.where(lane_in < 32, double, 0.0))
    for k in range(8):
        twice(u_ref, k * 32, rise[k * 16 : k * 16 + 16])
    for k in range(8):
        for j in (2 * k + 6, 2 * k + 7):
            pb2[j] = pb2[j] + u_ref[k * 32 : k * 32 + 32]
    sweep(7, 21, 14, pb2, pa2, s2, w2)
    sweep(8, 20, 12, pa2, pb2, s2, w2)

    for k in range(12):
        v_ref[k * 16 : k * 16 + 8] = pb2[k + 8, :8]
        v_ref[k * 16 + 8 : k * 16 + 16] = jnp.where(sub8 < 4, pb2[k + 8, 8:16], pb2[k + 8, 24:])
    rise = dot(v_ref[:192], double)
    for k in range(12):
        twice(u_ref, k * 32, rise[k * 16 : k * 16 + 16])
    for k in range(12):
        for j in (2 * k + 2, 2 * k + 3):
            pa1[j] = down1_ref[j] + u_ref[k * 32 : k * 32 + 32]
    w1 = (wx1, wy1, wz1, q1)
    sweep(3, 25, 22, pa1, pb1, s1, w1)
    sweep(4, 24, 20, pb1, pa1, s1, w1)

    for k in range(20):
        v_ref[k * 24 : k * 24 + 16] = pa1[k + 4, :16]
        v_ref[k * 24 + 16 : k * 24 + 24] = jnp.where(
            sub8 < 2, pa1[k + 4, 16:24], pltpu.roll(pa1[k + 4, 24:], 4, 0)
        )
    for z, out in ((0, rise_lo), (128, rise_hi)):
        double = pair_weight(lane_out + z - 2 * lane_in)
        rise = dot(v_ref[...], double)
        for k in range(20):
            twice(out, k * 48, rise[k * 24 : k * 24 + 24])

    def rise_at(k):
        here = pl.ds(k * 48 if isinstance(k, int) else pl.multiple_of(k * 48, 8), 40)
        return jnp.concatenate([rise_lo[here], rise_hi[here]], 1)

    w0 = (wx0, wy0, wz0, q0)

    def first_pairs(k0, n):
        results = []
        for i in range(n):
            k = k0 + i
            low, e, high = rise_at(k - 1), rise_at(k), rise_at(k + 1)
            e_up_y, e_up_z = up_y(e), up_z(e)
            for j, x_low, x_high in ((2 * k + 1, low, e), (2 * k + 2, e, high)):
                wy, wz = wy0[j], wz0[j]
                along_x = wx0[j] * x_high + wx0[j - 1] * x_low
                along_y = wy * e_up_y + dn_y(wy * e)
                along_z = wz * e_up_z + dn_z(wz * e)
                results.append((j, KEEP * e + q0[j] * (along_x + along_y + along_z)))
        for j, value in results:
            pb0[j] = value

    blocks(1, 19, 6, first_pairs)
    sweep(4, N0 - 4, 17, pb0, pa0, None, w0)

    def out_copies(k, j):
        here = pl.ds(j, 8)
        return (
            pltpu.make_async_copy(out_a.at[here], scaled.at[here], sems.at[0, k]),
            pltpu.make_async_copy(out_b.at[here], residual.at[here], sems.at[1, k]),
        )

    def last(k, carry):
        j = k * 8
        results = []
        for i in range(8):
            p = pa0[j + i + X0]
            dp = (OMEGA / q0[j + i + X0]) * p
            a = base_s[j + i] + dp[:32]
            results.append((a, base_r[j + i] + (flow(j + i + X0, p, pa0, w0) - dp)[:32]))
        for i, (a, b) in enumerate(results):
            out_a[j + i] = a
            out_b[j + i] = b
        for copy in out_copies(k, j):
            copy.start()
        return carry

    lax.fori_loop(0, 4, last, 0)
    for k in range(4):
        for copy in out_copies(k, k * 8):
            copy.wait()


def way_up(*operands):
    shape = jax.ShapeDtypeStruct((32, 32, 256), F32)
    buf = lambda count, *shape: [kept(*shape)] * count
    scratch = (
        buf(2, *BIG)
        + buf(2, N1, 32, 128)
        + buf(9, N2, 32, 128)
        + buf(8, N3, 16, 128)
        + buf(1, 384, 256)
        + buf(1, 384, 128)
        + buf(1, 480, 128)
        + buf(2, 960, 128)
        + buf(2, 32, 32, 256)
        + [pltpu.SemaphoreType.DMA((2, 4))]
    )
    hbm = pl.BlockSpec(memory_space=pl.ANY)
    return call(up_kernel, "way_up", [shape] * 2, scratch, 20, *operands, out_specs=[hbm] * 2)


def shift(a, axis, step):
    count = lax.axis_size(axis)
    return lax.ppermute(a, axis, [(i, (i + step) % count) for i in range(count)])


def both(to_low, to_high, axis):
    return shift(to_high, axis, 1), shift(to_low, axis, -1)


def shards(source, phase):
    dn0, up0 = send_rows(source, phase)
    ylo, yhi = both(dn0, up0, "gy")
    source, phase = load(source, phase, dn0)
    mob1 = mobility1(phase)
    msg = [kept(6, 40, 256)] * 2
    dn0, up0 = call(send_planes_kernel, "send_planes", msg, [], 4, source, phase, ylo, yhi, mob1)
    xlo, xhi = both(dn0, up0, "gx")
    state = inner0(source, phase, ylo, yhi)
    s0, _, wx0, wy0, wz0, q0, _, p0, _, src1, dn1, up1 = outer0(xlo, xhi, mob1, state)
    weights = (wx0, wy0, wz0, q0)
    xlo1, xhi1 = both(dn1, up1, "gx")
    p0 = before(*weights, s0, p0)
    ylo1, yhi1 = both(*pack1(src1, mob1, xlo1, xhi1, *edge_rows(p0)), "gy")
    own2, dn2, up2, *level1 = down1(src1, mob1, xlo1, xhi1, ylo1, yhi1, p0)
    xlo, xhi = both(dn2, up2, "gx")
    ext, ext_up = pack2(own2, xlo, xhi)
    ylo, yhi = both(ext, ext_up, "gy")
    based = base(*weights, s0, p0, xlo, xhi, ylo1, yhi1, ext)
    return tuple(way_up(ext, ylo, yhi, *level1, *weights, *based))


def solution(mesh):
    spec = P("gx", "gy", None)
    return jax.shard_map(shards, mesh=mesh, in_specs=(spec, spec), out_specs=(spec, spec), check_vma=False)
```
